32 devices in a mesh: dp: 8 (over y, x, core), fsdp: 4 (over z).
Axes of the slice: x: 2, y: 2, z: 4, core: 2. Of those that a mesh axis runs over, the one named last changes fastest.
Arguments:
- small_images: bfloat16 [128, 20, 20, 192], P(('dp', 'fsdp')), may hold values from -6 to 6
- medium_images: bfloat16 [128, 28, 28, 192], P(('dp', 'fsdp')), may hold values from -6 to 6
- large_images: bfloat16 [128, 36, 36, 192], P(('dp', 'fsdp')), may hold values from -6 to 6
- counts: int32 [32, 3], P(('dp', 'fsdp')), may hold values from 1 to 4, as said below
- first_params: float32 [811008], P(('dp', 'fsdp')), may hold values from -2 to 2, as said below
- second_params: float32 [954368], P(('dp', 'fsdp')), may hold values from -2 to 2, as said below
- small_cotangent: bfloat16 [128, 10, 10, 512], P(('dp', 'fsdp')), may hold values from -6 to 6
- medium_cotangent: bfloat16 [128, 14, 14, 512], P(('dp', 'fsdp')), may hold values from -6 to 6
- large_cotangent: bfloat16 [128, 18, 18, 512], P(('dp', 'fsdp')), may hold values from -6 to 6
Outputs:
- small_output: bfloat16 [128, 10, 10, 512], P(('dp', 'fsdp'))
- medium_output: bfloat16 [128, 14, 14, 512], P(('dp', 'fsdp'))
- large_output: bfloat16 [128, 18, 18, 512], P(('dp', 'fsdp'))
- small_image_grad: float32 [128, 20, 20, 192], P(('dp', 'fsdp'))
- medium_image_grad: float32 [128, 28, 28, 192], P(('dp', 'fsdp'))
- large_image_grad: float32 [128, 36, 36, 192], P(('dp', 'fsdp'))
- first_param_grads: float32 [811008], P(('dp', 'fsdp'))
- second_param_grads: float32 [954368], P(('dp', 'fsdp'))
The draws below stay inside these ranges and needn't reach their ends.
Inputs may be any that keep to these rules, and one draw needn't show every extreme that they name: counts[d, b] live images of device d in bucket b occupy its first slots; in every bucket one device has 4 live images and another has 1. `first_params`: block one's parameters in the layout of the first step, zeros past them. `second_params`: block two's parameters in the layout of the first step, zeros past them.
All inputs are finite; a program needn't handle non-finite values.
Results may differ from the reference program's by a relative error of at most 0.014.
The reference program's roundings to bfloat16 on the way count: a program that leaves them out, or rounds other values in their place, can miss the bound.
Values may be sent and summed in bfloat16 or wider, within the bound.
A program may use at most 320 MiB of HBM per device.

```python
import math
from functools import partial
import jax
import jax.numpy as jnp
from jax import lax

WIDTH_IN = 192
GROUPS = 8
GROUP_WIDTH = 64
SQUEEZE_A = 48
SQUEEZE_B = 128
GRID_S = 20
GRID_M = 28
GRID_L = 36
IMG_DEV = 4
WIDTH = 512
IMAGES = 128
P1 = 811008
P2 = 954368
DEVICES = 32


def segments(is_first):
    if is_first:
        width_in, squeeze = (WIDTH_IN, SQUEEZE_A)
    else:
        width_in, squeeze = (WIDTH, SQUEEZE_B)
    entries = [(width_in * WIDTH, width_in ** (-0.5), 0.0), (9 * GROUP_WIDTH * WIDTH, (9 * GROUP_WIDTH) ** (-0.5), 0.0), (WIDTH * squeeze, WIDTH ** (-0.5), 0.0), (squeeze, 0.5, 0.0), (squeeze * WIDTH, squeeze ** (-0.5), 0.0), (WIDTH, 0.5, 0.0), (WIDTH * WIDTH, WIDTH ** (-0.5), 0.0)]
    if is_first:
        entries.append((WIDTH_IN * WIDTH, WIDTH_IN ** (-0.5), 0.0))
    norm_pairs = 4 if is_first else 3
    for pair_index in range(norm_pairs):
        entries.append((WIDTH, 0.2, 1.0))
        entries.append((WIDTH, 0.3, 0.0))
    return entries


def shape_noise(noise, is_first, total_length):
    entries = segments(is_first)
    scales = jnp.concatenate([jnp.full((length,), spread, jnp.float32) for length, spread, center in entries])
    centers = jnp.concatenate([jnp.full((length,), center, jnp.float32) for length, spread, center in entries])
    used = scales.shape[0]
    values = noise[:used] * scales + centers
    return jnp.pad(values, (0, total_length - used))


def draw_counts(key, part):
    key = jax.random.fold_in(key, 1)
    key_values, key_top, key_bottom = jax.random.split(key, 3)
    values = jax.random.randint(key_values, (DEVICES, 3), 1, IMG_DEV + 1)
    top_device = jax.random.randint(key_top, (3,), 0, DEVICES)
    bottom_device = (top_device + 1 + jax.random.randint(key_bottom, (3,), 0, DEVICES - 1)) % DEVICES
    devices_col = jnp.arange(DEVICES, dtype=jnp.int32)[:, None]
    values = jnp.where(devices_col == top_device[None, :], IMG_DEV, values)
    values = jnp.where(devices_col == bottom_device[None, :], 1, values)
    return values.astype(jnp.int32)


def draw_first_params(key, part):
    key = jax.random.fold_in(key, 2)
    noise = jnp.clip(jax.random.normal(key, (P1,), jnp.float32), -4.0, 4.0)
    return shape_noise(noise, True, P1)


def draw_second_params(key, part):
    key = jax.random.fold_in(key, 3)
    noise = jnp.clip(jax.random.normal(key, (P2,), jnp.float32), -4.0, 4.0)
    return shape_noise(noise, False, P2)


def block_levels(own_key, extent, cuts, smallest, largest):
    def one(position, shards_of):
        heights = jax.random.uniform(jax.random.fold_in(jax.random.fold_in(own_key, 6), position), (shards_of,), jnp.float32, smallest / len(cuts), largest / len(cuts))
        return jnp.repeat(jnp.exp(heights), extent[position] // shards_of).reshape((-1,) + (1,) * (len(extent) - position - 1))

    level = one(*cuts[0])
    for cut in cuts[1:]:
        level = level * one(*cut)
    return level


def centred(stream_key, dims, scale, bound, shards=(), kind=jnp.bfloat16):
    factor_of = block_levels(stream_key, dims, shards, -0.22, 0.18) if shards else 1.0
    array = jax.random.normal(stream_key, dims, jnp.float32) * scale * factor_of
    return jnp.minimum(jnp.maximum(array, -bound), bound).astype(kind)


def setup_inputs(seed: int = 0) -> dict:
    seeds = jax.random.split(jax.random.key(seed), 10)
    return {
        "small_images": centred(seeds[0], (IMAGES, GRID_S, GRID_S, WIDTH_IN), 1.0, 6.0, ((0, 32),)),
        "medium_images": centred(seeds[1], (IMAGES, GRID_M, GRID_M, WIDTH_IN), 1.0, 6.0, ((0, 32),)),
        "large_images": centred(seeds[2], (IMAGES, GRID_L, GRID_L, WIDTH_IN), 1.0, 6.0, ((0, 32),)),
        "counts": draw_counts(jax.random.fold_in(seeds[9], 71), 0),
        "first_params": draw_first_params(jax.random.fold_in(seeds[9], 71), 0),
        "second_params": draw_second_params(jax.random.fold_in(seeds[9], 71), 0),
        "small_cotangent": centred(seeds[6], (IMAGES, GRID_S // 2, GRID_S // 2, WIDTH), 1.0, 6.0, ((0, 32),)),
        "medium_cotangent": centred(seeds[7], (IMAGES, GRID_M // 2, GRID_M // 2, WIDTH), 1.0, 6.0, ((0, 32),)),
        "large_cotangent": centred(seeds[8], (IMAGES, GRID_L // 2, GRID_L // 2, WIDTH), 1.0, 6.0, ((0, 32),)),
    }


@jax.custom_vjp
def low(v):
    return lax.optimization_barrier(v.astype(jnp.bfloat16)).astype(jnp.float32)

@jax.custom_vjp
def low_back(v):
    return v

def low_keep(v):
    return (low(v), None)

def low_pass(kept, grad):
    return (grad,)

def back_keep(v):
    return (v, None)

def back_low(kept, grad):
    return (low(grad),)
low.defvjp(low_keep, low_pass)
low_back.defvjp(back_keep, back_low)
EPSILON = 1e-05
HIGHEST = lax.Precision.HIGHEST

def layout(is_first):
    if is_first:
        width_in, squeeze = (WIDTH_IN, SQUEEZE_A)
    else:
        width_in, squeeze = (WIDTH, SQUEEZE_B)
    entries = [('w_in', (width_in, WIDTH)), ('w_group', (9, GROUPS, GROUP_WIDTH, GROUP_WIDTH)), ('se_down', (WIDTH, squeeze)), ('se_down_bias', (squeeze,)), ('se_up', (squeeze, WIDTH)), ('se_up_bias', (WIDTH,)), ('w_out', (WIDTH, WIDTH))]
    if is_first:
        entries.append(('w_short', (WIDTH_IN, WIDTH)))
    norm_names = ['gain_one', 'shift_one', 'gain_two', 'shift_two', 'gain_three', 'shift_three']
    if is_first:
        norm_names = norm_names + ['gain_short', 'shift_short']
    return entries + [(entry_name, (WIDTH,)) for entry_name in norm_names]

def unflatten(flat, is_first):
    params = {}
    offset = 0
    for entry_name, entry_shape in layout(is_first):
        length = math.prod(entry_shape)
        params[entry_name] = flat[offset:offset + length].reshape(entry_shape)
        offset = offset + length
    return params

def point_conv(values, weight):
    return jnp.einsum('nhwc,cd->nhwd', values, weight, precision=HIGHEST)

def group_conv(values, weight, stride):
    batch_size, height, width_px, channels = values.shape
    out_h, out_w = (height // stride, width_px // stride)
    padded = jnp.pad(values, ((0, 0), (1, 1), (1, 1), (0, 0)))
    total = jnp.zeros((batch_size, out_h, out_w, GROUPS, GROUP_WIDTH), values.dtype)
    for tap_index in range(9):
        row_off, col_off = (tap_index // 3, tap_index % 3)
        window = padded[:, row_off:row_off + stride * out_h:stride, col_off:col_off + stride * out_w:stride, :]
        window = window.reshape(batch_size, out_h, out_w, GROUPS, GROUP_WIDTH)
        total = total + jnp.einsum('nhwgi,gio->nhwgo', window, weight[tap_index], precision=HIGHEST)
    return total.reshape(batch_size, out_h, out_w, channels)

def batch_norm(values, masks, gain, shift):
    total_count = sum((jnp.sum(mask) * value.shape[1] * value.shape[2] for value, mask in zip(values, masks)))
    total_sum = sum((lax.optimization_barrier(jnp.sum(value * mask[:, None, None, None], axis=(0, 1, 2))) for value, mask in zip(values, masks)))
    total_square = sum((lax.optimization_barrier(jnp.sum(value * value * mask[:, None, None, None], axis=(0, 1, 2))) for value, mask in zip(values, masks)))
    mean_value = total_sum / total_count
    variance = total_square / total_count - mean_value * mean_value
    inv_std = lax.rsqrt(variance + EPSILON)
    return [(value - mean_value) * inv_std * gain + shift for value in values]

def block(acts, masks, params, is_first):
    stride = 2 if is_first else 1
    first_out = [low_back(point_conv(value, params['w_in'])) for value in acts]
    hidden_one = [low(jax.nn.silu(value)) for value in batch_norm(first_out, masks, params['gain_one'], params['shift_one'])]
    second_out = [low_back(group_conv(value, params['w_group'], stride)) for value in hidden_one]
    activated = [jax.nn.silu(value) for value in batch_norm(second_out, masks, params['gain_two'], params['shift_two'])]
    gated = []
    for value in activated:
        pooled = lax.optimization_barrier(jnp.mean(value, axis=(1, 2)))
        squeezed = jax.nn.silu(jnp.dot(pooled, params['se_down'], precision=HIGHEST) + params['se_down_bias'])
        excite = jax.nn.sigmoid(jnp.dot(squeezed, params['se_up'], precision=HIGHEST) + params['se_up_bias'])
        gated.append(low(value * excite[:, None, None, :]))
    third_out = [low_back(point_conv(value, params['w_out'])) for value in gated]
    branch = batch_norm(third_out, masks, params['gain_three'], params['shift_three'])
    if is_first:
        short_out = [low_back(point_conv(value[:, ::2, ::2, :], params['w_short'])) for value in acts]
        skip = batch_norm(short_out, masks, params['gain_short'], params['shift_short'])
    else:
        skip = acts
    return [jax.nn.silu(left + right) for left, right in zip(branch, skip)]

def forward(images, first_flat, second_flat, masks):
    first_weights = unflatten(low(first_flat), True)
    second_weights = unflatten(low(second_flat), False)
    middle = [low(value) for value in jax.checkpoint(partial(block, is_first=True))(images, masks, first_weights)]
    final = jax.checkpoint(partial(block, is_first=False))(middle, masks, second_weights)
    return [value * mask[:, None, None, None] for value, mask in zip(final, masks)]

def reference(small_images, medium_images, large_images, counts, first_params, second_params, small_cotangent, medium_cotangent, large_cotangent):
    images = [value.astype(jnp.float32) for value in (small_images, medium_images, large_images)]
    masks = []
    for bucket, value in enumerate(images):
        slots = jnp.arange(value.shape[0], dtype=jnp.int32)
        owners = slots // IMG_DEV
        masks.append((slots % IMG_DEV < counts[owners, bucket]).astype(jnp.float32))

    def loss_inputs(image_list, first_flat, second_flat):
        return forward(image_list, first_flat, second_flat, masks)
    outputs, pullback = jax.vjp(loss_inputs, images, first_params, second_params)
    cotangents = [value.astype(jnp.float32) for value in (small_cotangent, medium_cotangent, large_cotangent)]
    image_grads, first_grads, second_grads = pullback(cotangents)
    return (outputs[0].astype(jnp.bfloat16), outputs[1].astype(jnp.bfloat16), outputs[2].astype(jnp.bfloat16), image_grads[0], image_grads[1], image_grads[2], first_grads, second_grads)
```

```python
import functools
import math
import types
import typing

import jax
import jax.numpy as jnp
from jax import lax
from jax.experimental import pallas as pl
from jax.experimental.pallas import tpu as pltpu
from jax.sharding import PartitionSpec as P

WIDTH_IN = 192
GROUPS = 8
GROUP_WIDTH = 64
SQUEEZE_A = 48
SQUEEZE_B = 128
WIDTH = 512


MESH = pl.DeviceIdType.MESH
UNROLL = 1
EPSILON = 1e-05
HIGHEST = lax.Precision.HIGHEST
PLAIN_DIMS = ("NHWC", "HWIO", "NHWC")
WEIGHT_DIMS = ("CHWN", "IHWO", "NHWC")


class Table(types.SimpleNamespace):
    pass


class FirstParams(typing.NamedTuple):
    w_in: typing.Any
    w_group: typing.Any
    se_down: typing.Any
    se_down_bias: typing.Any
    se_up: typing.Any
    se_up_bias: typing.Any
    w_out: typing.Any
    w_short: typing.Any
    gain_one: typing.Any
    shift_one: typing.Any
    gain_two: typing.Any
    shift_two: typing.Any
    gain_three: typing.Any
    shift_three: typing.Any
    gain_short: typing.Any
    shift_short: typing.Any


class SecondParams(typing.NamedTuple):
    w_in: typing.Any
    w_group: typing.Any
    se_down: typing.Any
    se_down_bias: typing.Any
    se_up: typing.Any
    se_up_bias: typing.Any
    w_out: typing.Any
    gain_one: typing.Any
    shift_one: typing.Any
    gain_two: typing.Any
    shift_two: typing.Any
    gain_three: typing.Any
    shift_three: typing.Any


def layout(is_first):
    if is_first:
        width_in, squeeze = (WIDTH_IN, SQUEEZE_A)
    else:
        width_in, squeeze = (WIDTH, SQUEEZE_B)
    shapes = [
        (width_in, WIDTH),
        (9, GROUPS, GROUP_WIDTH, GROUP_WIDTH),
        (WIDTH, squeeze),
        (squeeze,),
        (squeeze, WIDTH),
        (WIDTH,),
        (WIDTH, WIDTH),
    ]
    if is_first:
        return FirstParams(*shapes, (WIDTH_IN, WIDTH), *([(WIDTH,)] * 8))
    return SecondParams(*shapes, *([(WIDTH,)] * 6))


def unflatten(flat, is_first):
    parts = []
    offset = 0
    for entry_shape in layout(is_first):
        length = math.prod(entry_shape)
        parts.append(flat[offset : offset + length].reshape(entry_shape))
        offset = offset + length
    return type(layout(is_first))(*parts)


def flatten(grads, is_first, full_length):
    entries = type(layout(is_first))(**vars(grads))
    joined = jnp.concatenate([entry.reshape(-1) for entry in entries])
    return jnp.pad(joined, (0, full_length - joined.shape[0]))


def sum_kernel(groups, inner, values_ref, total_ref, slots, send_sem, recv_sem):
    outer_index, inner_index = lax.axis_index("dp"), lax.axis_index("fsdp")
    me = outer_index * inner + inner_index
    devices = groups * inner

    def partner(step):
        other = lax.rem(me + step, devices)
        return (other // inner, lax.rem(other, inner))

    def greet(step, carry):
        pl.semaphore_signal(barrier, inc=1, device_id=partner(step), device_id_type=MESH)
        return carry

    def send(step, carry):
        pltpu.make_async_remote_copy(
            src_ref=values_ref,
            dst_ref=slots.at[step - 1],
            send_sem=send_sem,
            recv_sem=recv_sem,
            device_id=partner(step),
            device_id_type=MESH,
        ).start()
        return carry

    barrier = pltpu.get_barrier_semaphore()
    lax.fori_loop(1, devices, greet, 0, unroll=UNROLL)
    pl.semaphore_wait(barrier, devices - 1)
    lax.fori_loop(1, devices, send, 0, unroll=UNROLL)
    pltpu.make_async_copy(slots, slots, recv_sem).wait()
    total_ref[...] = values_ref[...] + jnp.sum(slots[...], axis=0)
    pltpu.make_async_copy(slots, slots, send_sem).wait()


def sum_devices(values):
    groups, inner = lax.axis_size("dp"), lax.axis_size("fsdp")
    rows = values.reshape(-1, 128)
    return pl.pallas_call(
        functools.partial(sum_kernel, groups, inner),
        out_shape=jax.ShapeDtypeStruct(rows.shape, jnp.float32),
        in_specs=[pl.BlockSpec(memory_space=pltpu.VMEM)],
        out_specs=pl.BlockSpec(memory_space=pltpu.VMEM),
        scratch_shapes=[
            pltpu.VMEM((groups * inner - 1,) + rows.shape, jnp.float32),
            pltpu.SemaphoreType.DMA(()),
            pltpu.SemaphoreType.DMA(()),
        ],
        compiler_params=pltpu.CompilerParams(collective_id=0, has_side_effects=True),
    )(rows).reshape(values.shape)


def gather_forward(shard):
    return lax.all_gather(shard.astype(jnp.bfloat16), ("dp", "fsdp"), axis=0, tiled=True)


def gather_backward(shard):
    return lax.all_gather(shard.astype(jnp.bfloat16), ("dp", "fsdp"), axis=0, tiled=True)


def scatter_grads(flat):
    return lax.psum_scatter(flat, ("dp", "fsdp"), scatter_dimension=0, tiled=True)


def silu_grad(values):
    sig = jax.nn.sigmoid(values)
    return sig * (1.0 + values * (1.0 - sig))


def point_conv(values, weight):
    return jnp.einsum("nhwc,cd->nhwd", values, weight, preferred_element_type=jnp.float32)


def point_back(grads, weight):
    return jnp.einsum("nhwd,cd->nhwc", grads, weight, preferred_element_type=jnp.float32)


def point_weight(values, grads):
    return jnp.einsum("nhwc,nhwd->cd", values, grads, preferred_element_type=jnp.float32)


def even_pixels(values):
    batch_size, height, width_px, channels = values.shape
    return values.reshape(batch_size, height // 2, 2, width_px // 2, 2, channels)[:, :, 0, :, 0, :]


def group_kernel(weight):
    split = weight.reshape(3, 3, GROUPS, GROUP_WIDTH, GROUP_WIDTH)
    return split.transpose(0, 1, 3, 2, 4).reshape(3, 3, GROUP_WIDTH, GROUPS * GROUP_WIDTH)


def group_conv(values, weight, stride):
    return lax.conv_general_dilated(
        values,
        group_kernel(weight),
        (stride, stride),
        ((1, 1), (1, 1)),
        dimension_numbers=PLAIN_DIMS,
        feature_group_count=GROUPS,
        preferred_element_type=jnp.float32,
    )


def group_back(values, grads, weight, stride):
    split = weight.reshape(3, 3, GROUPS, GROUP_WIDTH, GROUP_WIDTH)[::-1, ::-1]
    flipped = split.transpose(0, 1, 4, 2, 3).reshape(3, 3, GROUP_WIDTH, GROUPS * GROUP_WIDTH)
    grad_values = lax.conv_general_dilated(
        grads,
        flipped,
        (1, 1),
        ((1, stride), (1, stride)),
        lhs_dilation=(stride, stride),
        dimension_numbers=PLAIN_DIMS,
        feature_group_count=GROUPS,
        preferred_element_type=jnp.float32,
    )
    tail = 2 - stride
    raw = lax.conv_general_dilated(
        values,
        grads,
        (1, 1),
        ((1, tail), (1, tail)),
        rhs_dilation=(stride, stride),
        dimension_numbers=WEIGHT_DIMS,
        batch_group_count=GROUPS,
        preferred_element_type=jnp.float32,
    )
    tap_grads = raw.reshape(GROUP_WIDTH, 3, 3, GROUPS, GROUP_WIDTH).transpose(1, 2, 3, 0, 4)
    return (grad_values, tap_grads.reshape(9, GROUPS, GROUP_WIDTH, GROUP_WIDTH))


def short_back(grads, weight):
    kernel = weight.T[None, None, :, :]
    return lax.conv_general_dilated(
        grads,
        kernel,
        (1, 1),
        ((0, 1), (0, 1)),
        lhs_dilation=(2, 2),
        dimension_numbers=PLAIN_DIMS,
        preferred_element_type=jnp.float32,
    )


def norm_forward(values, masks, live_counts):
    local_sum = jnp.zeros((values[0].shape[-1],), jnp.float32)
    local_square = jnp.zeros((values[0].shape[-1],), jnp.float32)
    for value, mask in zip(values, masks):
        weighted = value * mask[:, None, None, None]
        local_sum = local_sum + jnp.sum(weighted, axis=(0, 1, 2))
        local_square = local_square + jnp.sum(weighted * value, axis=(0, 1, 2))
    total_sum, total_square = sum_devices(jnp.stack([local_sum, local_square]))
    total_count = sum(
        live * (value.shape[1] * value.shape[2]) for live, value in zip(live_counts, values)
    )
    mean_value = total_sum / total_count
    variance = total_square / total_count - mean_value * mean_value
    inv_std = lax.rsqrt(variance + EPSILON)
    return ([(value - mean_value) * inv_std for value in values], inv_std, total_count)


def norm_backward(grads, normed, inv_std, total_count, gain, masks):
    local_gain = jnp.zeros((grads[0].shape[-1],), jnp.float32)
    local_shift = jnp.zeros((grads[0].shape[-1],), jnp.float32)
    for grad, value, mask in zip(grads, normed, masks):
        weighted = grad * mask[:, None, None, None]
        local_gain = local_gain + jnp.sum(weighted * value, axis=(0, 1, 2))
        local_shift = local_shift + jnp.sum(weighted, axis=(0, 1, 2))
    total_gain, total_shift = sum_devices(jnp.stack([local_gain, local_shift]))
    factor = gain.astype(jnp.float32) * inv_std
    result = []
    for grad, value, mask in zip(grads, normed, masks):
        inner = factor * (grad - (total_shift + value * total_gain) / total_count)
        result.append((inner * mask[:, None, None, None]).astype(jnp.bfloat16))
    return (result, local_gain, local_shift)


def block_forward(acts, params, masks, live_counts, is_first):
    stride = 2 if is_first else 1
    kept = Table(acts=acts)
    first_out = [point_conv(value, params.w_in) for value in acts]
    kept.normed_one, kept.inv_one, kept.count_one = norm_forward(first_out, masks, live_counts)
    hidden_one = [
        jax.nn.silu(value * params.gain_one + params.shift_one).astype(jnp.bfloat16)
        for value in kept.normed_one
    ]
    kept.hidden_one = hidden_one
    second_out = [group_conv(value, params.w_group, stride) for value in hidden_one]
    kept.normed_two, kept.inv_two, kept.count_two = norm_forward(second_out, masks, live_counts)
    se_down = params.se_down.astype(jnp.float32)
    se_up = params.se_up.astype(jnp.float32)
    activated, pooled_list, squeeze_list, squeezed_list, excite_list, gated = (
        [],
        [],
        [],
        [],
        [],
        [],
    )
    for value in kept.normed_two:
        act_value = jax.nn.silu(value * params.gain_two + params.shift_two)
        pooled = jnp.mean(act_value, axis=(1, 2))
        squeeze_pre = jnp.dot(pooled, se_down, precision=HIGHEST) + params.se_down_bias
        squeezed = jax.nn.silu(squeeze_pre)
        excite = jax.nn.sigmoid(jnp.dot(squeezed, se_up, precision=HIGHEST) + params.se_up_bias)
        activated.append(act_value)
        pooled_list.append(pooled)
        squeeze_list.append(squeeze_pre)
        squeezed_list.append(squeezed)
        excite_list.append(excite)
        gated.append((act_value * excite[:, None, None, :]).astype(jnp.bfloat16))
    kept.activated, kept.pooled, kept.squeeze_pre = (activated, pooled_list, squeeze_list)
    kept.squeezed, kept.excite, kept.gated = (squeezed_list, excite_list, gated)
    third_out = [point_conv(value, params.w_out) for value in gated]
    kept.normed_three, kept.inv_three, kept.count_three = norm_forward(third_out, masks, live_counts)
    branch = [
        value * params.gain_three + params.shift_three for value in kept.normed_three
    ]
    if is_first:
        kept.short_in = [even_pixels(value) for value in acts]
        short_out = [point_conv(value, params.w_short) for value in kept.short_in]
        kept.normed_short, kept.inv_short, kept.count_short = norm_forward(
            short_out, masks, live_counts
        )
        skip = [
            value * params.gain_short + params.shift_short for value in kept.normed_short
        ]
    else:
        skip = [value.astype(jnp.float32) for value in acts]
    total_pre = [left + right for left, right in zip(branch, skip)]
    kept.total_pre = total_pre
    return (kept, [jax.nn.silu(value) for value in total_pre])


def block_backward(kept, params, grad_result, masks, is_first):
    stride = 2 if is_first else 1
    grads = Table()
    grad_pre = [grad * silu_grad(value) for grad, value in zip(grad_result, kept.total_pre)]
    grad_third, grads.gain_three, grads.shift_three = norm_backward(
        grad_pre,
        kept.normed_three,
        kept.inv_three,
        kept.count_three,
        params.gain_three,
        masks,
    )
    grads.w_out = sum(
        (point_weight(value, grad) for value, grad in zip(kept.gated, grad_third))
    )
    se_down = params.se_down.astype(jnp.float32)
    se_up = params.se_up.astype(jnp.float32)
    grad_norm_two = []
    up_grad, up_bias_grad, down_grad, down_bias_grad = (0.0, 0.0, 0.0, 0.0)
    for bucket in range(len(grad_third)):
        grad_gated = point_back(grad_third[bucket], params.w_out)
        act_value = kept.activated[bucket]
        excite = kept.excite[bucket]
        grad_excite = jnp.sum(grad_gated * act_value, axis=(1, 2))
        grad_up_pre = grad_excite * excite * (1.0 - excite)
        up_grad = up_grad + jnp.dot(kept.squeezed[bucket].T, grad_up_pre, precision=HIGHEST)
        up_bias_grad = up_bias_grad + jnp.sum(grad_up_pre, axis=0)
        grad_squeezed = jnp.dot(grad_up_pre, se_up.T, precision=HIGHEST)
        grad_down_pre = grad_squeezed * silu_grad(kept.squeeze_pre[bucket])
        down_grad = down_grad + jnp.dot(kept.pooled[bucket].T, grad_down_pre, precision=HIGHEST)
        down_bias_grad = down_bias_grad + jnp.sum(grad_down_pre, axis=0)
        grad_pooled = jnp.dot(grad_down_pre, se_down.T, precision=HIGHEST)
        pixels = act_value.shape[1] * act_value.shape[2]
        grad_act = grad_gated * excite[:, None, None, :] + grad_pooled[:, None, None, :] / pixels
        pre_two = kept.normed_two[bucket] * params.gain_two + params.shift_two
        grad_norm_two.append(grad_act * silu_grad(pre_two))
    grads.se_up, grads.se_up_bias = (up_grad, up_bias_grad)
    grads.se_down, grads.se_down_bias = (down_grad, down_bias_grad)
    grad_second, grads.gain_two, grads.shift_two = norm_backward(
        grad_norm_two,
        kept.normed_two,
        kept.inv_two,
        kept.count_two,
        params.gain_two,
        masks,
    )
    grad_norm_one = []
    group_grad = 0.0
    for bucket in range(len(grad_second)):
        grad_hidden, tap_grads = group_back(
            kept.hidden_one[bucket], grad_second[bucket], params.w_group, stride
        )
        group_grad = group_grad + tap_grads
        pre_one = kept.normed_one[bucket] * params.gain_one + params.shift_one
        grad_norm_one.append(grad_hidden * silu_grad(pre_one))
    grads.w_group = group_grad
    grad_first, grads.gain_one, grads.shift_one = norm_backward(
        grad_norm_one,
        kept.normed_one,
        kept.inv_one,
        kept.count_one,
        params.gain_one,
        masks,
    )
    acts = kept.acts
    grads.w_in = sum((point_weight(value, grad) for value, grad in zip(acts, grad_first)))
    grad_acts = [point_back(grad, params.w_in) for grad in grad_first]
    if is_first:
        grad_short, grads.gain_short, grads.shift_short = norm_backward(
            grad_pre,
            kept.normed_short,
            kept.inv_short,
            kept.count_short,
            params.gain_short,
            masks,
        )
        grads.w_short = sum(
            (point_weight(value, grad) for value, grad in zip(kept.short_in, grad_short))
        )
        grad_acts = [
            total + short_back(grad, params.w_short)
            for total, grad in zip(grad_acts, grad_short)
        ]
    else:
        grad_acts = [total + grad for total, grad in zip(grad_acts, grad_pre)]
    return (grads, grad_acts)


def per_device(
    small_images,
    medium_images,
    large_images,
    counts,
    first_params,
    second_params,
    small_cotangent,
    medium_cotangent,
    large_cotangent,
):
    images = [small_images, medium_images, large_images]
    masks = [
        (jnp.arange(value.shape[0], dtype=jnp.int32) < counts[0, bucket]).astype(jnp.float32)
        for bucket, value in enumerate(images)
    ]
    live_counts = sum_devices(
        jnp.broadcast_to(jnp.pad(counts.astype(jnp.float32), ((0, 0), (0, 125))), (8, 128))
    )[0]
    live_counts = [live_counts[0], live_counts[1], live_counts[2]]
    first_full = gather_forward(first_params)
    first_weights = unflatten(first_full, True)
    kept_first, middle_values = block_forward(images, first_weights, masks, live_counts, True)
    middle = [value.astype(jnp.bfloat16) for value in middle_values]
    second_full = gather_forward(second_params)
    second_weights = unflatten(second_full, False)
    kept_second, final = block_forward(middle, second_weights, masks, live_counts, False)
    outputs = [
        (value * mask[:, None, None, None]).astype(jnp.bfloat16)
        for value, mask in zip(final, masks)
    ]
    cotangents = [small_cotangent, medium_cotangent, large_cotangent]
    grad_final = [
        value.astype(jnp.float32) * mask[:, None, None, None]
        for value, mask in zip(cotangents, masks)
    ]
    second_back = unflatten(gather_backward(second_params), False)
    second_grads, grad_middle = block_backward(kept_second, second_back, grad_final, masks, False)
    second_flat = flatten(second_grads, False, second_full.shape[0])
    second_out = scatter_grads(second_flat)
    first_back = unflatten(gather_backward(first_params), True)
    first_grads, grad_images = block_backward(kept_first, first_back, grad_middle, masks, True)
    first_flat = flatten(first_grads, True, first_full.shape[0])
    first_out = scatter_grads(first_flat)
    return (
        outputs[0],
        outputs[1],
        outputs[2],
        grad_images[0],
        grad_images[1],
        grad_images[2],
        first_out,
        second_out,
    )


def solution(mesh):
    in_specs = (
        P(("dp", "fsdp"), None, None, None),
        P(("dp", "fsdp"), None, None, None),
        P(("dp", "fsdp"), None, None, None),
        P(("dp", "fsdp"), None),
        P(("dp", "fsdp")),
        P(("dp", "fsdp")),
        P(("dp", "fsdp"), None, None, None),
        P(("dp", "fsdp"), None, None, None),
        P(("dp", "fsdp"), None, None, None),
    )
    out_specs = (
        P(("dp", "fsdp"), None, None, None),
        P(("dp", "fsdp"), None, None, None),
        P(("dp", "fsdp"), None, None, None),
        P(("dp", "fsdp"), None, None, None),
        P(("dp", "fsdp"), None, None, None),
        P(("dp", "fsdp"), None, None, None),
        P(("dp", "fsdp")),
        P(("dp", "fsdp")),
    )
    return jax.shard_map(
        per_device, mesh=mesh, in_specs=in_specs, out_specs=out_specs, check_vma=False
    )
```

```python
import functools
import math

import jax
import jax.numpy as jnp
import numpy as np
from jax import lax
from jax.experimental import pallas as pl
from jax.experimental.pallas import tpu as pltpu
from jax.sharding import PartitionSpec as P

WIDTH_IN = 192
GROUPS = 8
GROUP_WIDTH = 64
SQUEEZE_A = 48
SQUEEZE_B = 128
WIDTH = 512
HALF = 256
TAPS = 9
EPSILON = 1e-05
HIGHEST = lax.Precision.HIGHEST
MESH = pl.DeviceIdType.MESH
F32 = jnp.float32
BF16 = jnp.bfloat16
LIMIT = 63 * 2**20


def shapes_of(is_first):
    width_in, squeeze = (WIDTH_IN, SQUEEZE_A) if is_first else (WIDTH, SQUEEZE_B)
    shapes = [
        (width_in, WIDTH),
        (TAPS, GROUPS, GROUP_WIDTH, GROUP_WIDTH),
        (WIDTH, squeeze),
        (1, squeeze),
        (squeeze, WIDTH),
        (1, WIDTH),
        (WIDTH, WIDTH),
    ]
    if is_first:
        shapes.append((WIDTH_IN, WIDTH))
    shapes.append((8 if is_first else 6, WIDTH))
    return shapes


def unflatten(flat, is_first):
    parts = []
    offset = 0
    for shape in shapes_of(is_first):
        length = math.prod(shape)
        parts.append(flat[offset : offset + length].reshape(shape))
        offset = offset + length
    return parts


def flatten(parts, full_length):
    joined = jnp.concatenate([part.reshape(-1) for part in parts])
    return jnp.pad(joined, (0, full_length - joined.shape[0]))


def block_diagonal(w_group):
    split = w_group.reshape(TAPS, 2, 4, GROUP_WIDTH, 1, GROUP_WIDTH)
    eye = jnp.eye(4, dtype=w_group.dtype).reshape(1, 1, 4, 1, 4, 1)
    return (split * eye).reshape(TAPS, 2, HALF, HALF).transpose(1, 0, 2, 3)


def diagonal(product):
    parts = [slice(g * GROUP_WIDTH, (g + 1) * GROUP_WIDTH) for g in range(4)]
    return jnp.concatenate([product[part, part] for part in parts], axis=0)


def dot(left, right):
    return jnp.dot(left, right, preferred_element_type=F32)


def dot_nt(left, right):
    return lax.dot_general(left, right, (((1,), (1,)), ((), ())), preferred_element_type=F32)


def dot_tn(left, right):
    return lax.dot_general(left, right, (((0,), (0,)), ((), ())), preferred_element_type=F32)


def exact(left, right, dims):
    return lax.dot_general(
        left, right, (dims, ((), ())), precision=HIGHEST, preferred_element_type=F32
    )


def half_silu(half):
    return half + half * jnp.tanh(half)


def half_silu_grad(half, tan):
    return (0.5 + 0.5 * tan) * (1.0 + half * (1.0 - tan))


def fold(values):
    return jnp.sum(values.reshape(-1, 8, WIDTH), axis=0)


def down_to_row(values):
    return jnp.sum(values, axis=0, keepdims=True)


class Geometry:
    def __init__(self, sides):
        self.sides = sides
        self.rows = [side * side * 16 for side in sides]
        self.bases = [sum(self.rows[:b]) for b in range(len(sides))]
        self.total = sum(self.rows)

    def grid(self, extra_rows, extra_cols, start):
        bases = []
        for side in self.sides:
            bases.append(start)
            start = start + (side + extra_rows) * (side + extra_cols) * 16
        return bases, start


def exchange_stages(groups, inner):
    return [groups * inner] if groups * inner <= 64 else [inner, groups]


def aligned(start, size):
    return pl.ds(pl.multiple_of(start, 16), size)


def body(geo, groups, inner, *refs):
    (
        acts, mask, count,
        w_in1, bd1, down1, downb1, up1, upb1, w_out1, w_short, norms1,
        w_in2, bd2, down2, downb2, up2, upb2, w_out2, norms2,
        cot_hbm,
        out_hbm, g1_hbm, gs_hbm, dwg1_hbm, dwg2_hbm,
        dw_in1, ddown1, ddownb1, dup1, dupb1, dw_out1, dw_short, dnorms1,
        dw_in2, ddown2, ddownb2, dup2, dupb2, dw_out2, dnorms2,
        pool, x0, x1, x2, x3, h2, mid, acc, vec, se1, sq1, se2, sq2,
        pay, slots, send_sem, recv_sem, sems,
    ) = refs
    sides, bases, rows_of, total = geo.sides, geo.bases, geo.rows, geo.total
    buckets = range(len(sides))
    devices = groups * inner

    outer_index, inner_index = lax.axis_index("dp"), lax.axis_index("fsdp")

    def any_partner(step):
        other = lax.rem(outer_index * inner + inner_index + step, devices)
        return (other // inner, lax.rem(other, inner))

    def inner_partner(step):
        return (outer_index, lax.rem(inner_index + step, inner))

    def outer_partner(step):
        return (lax.rem(outer_index + step, groups), inner_index)

    barrier = pltpu.get_barrier_semaphore()
    stages = exchange_stages(groups, inner)
    if len(stages) == 1:
        partners = [any_partner]
    else:
        partners = [inner_partner, outer_partner]
    for count_in_stage, partner in zip(stages, partners):

        def greet(step, carry, partner=partner):
            pl.semaphore_signal(barrier, inc=1, device_id=partner(step), device_id_type=MESH)
            return carry

        lax.fori_loop(1, count_in_stage, greet, 0)

    calls = []

    def all_sum(rows):
        parity = len(calls) % 2
        size = -(-len(rows) * 4 // 8) * 8
        if not calls:
            pl.semaphore_wait(barrier, sum(stages) - len(stages))
        calls.append(size)
        sums = None
        for stage, partner in enumerate(partners):
            at = 2 * stage + parity
            if sums is None:
                for r, row in enumerate(rows):
                    for c in range(4):
                        pay[at, 4 * r + c : 4 * r + c + 1, :] = row[:, c * 128 : (c + 1) * 128]
            else:
                pay[at, 0:size, :] = sums

            def send(step, carry, at=at, partner=partner):
                pltpu.make_async_remote_copy(
                    src_ref=pay.at[at, pl.ds(0, size)],
                    dst_ref=slots.at[at, step - 1, pl.ds(0, size)],
                    send_sem=send_sem.at[at],
                    recv_sem=recv_sem.at[at],
                    device_id=partner(step),
                    device_id_type=MESH,
                ).start()
                return carry

            others = stages[stage] - 1
            lax.fori_loop(1, others + 1, send, 0)
            landed = slots.at[at, pl.ds(0, others), pl.ds(0, size)]
            pltpu.make_async_copy(landed, landed, recv_sem.at[at]).wait()
            sums = pay[at, 0:size, :] + jnp.sum(slots[at, 0:others, 0:size, :], axis=0)
            pltpu.make_async_copy(landed, landed, send_sem.at[at]).wait()
        return [
            jnp.concatenate([sums[4 * r + c : 4 * r + c + 1, :] for c in range(4)], axis=1)
            for r in range(len(rows))
        ]

    def each(step, carry):
        for b in buckets:
            def line(i, kept, b=b):
                size = sides[b] * 16
                return step(b, aligned(bases[b] + i * size, size), i, kept)
            carry = lax.fori_loop(0, sides[b], line, carry)
        return carry

    zero8 = jnp.zeros((8, WIDTH), F32)

    def masked(values, b):
        return (values.reshape(-1, 16, WIDTH) * mask[b][None]).reshape(values.shape)

    def set_norm(k, sums, squares, norms, index, live):
        mean = sums / live
        inv_std = lax.rsqrt(squares / live - mean * mean + EPSILON)
        scale = inv_std * norms[2 * index : 2 * index + 1, :]
        offset = norms[2 * index + 1 : 2 * index + 2, :] - mean * scale
        for r, row in enumerate((mean, inv_std, scale, offset, 0.5 * scale, 0.5 * offset)):
            vec[6 * k + r : 6 * k + r + 1, :] = row

    def row(k, r):
        return vec[6 * k + r : 6 * k + r + 1, :]

    def half(k, u):
        return u * row(k, 4) + row(k, 5)

    def set_grad(k, sum_g, sum_d, live, at=48):
        scale, inv_std = row(k, 2), row(k, 1)
        on_u = -scale * inv_std * inv_std * sum_d / live
        vec[at : at + 1, :] = scale
        vec[at + 1 : at + 2, :] = on_u
        vec[at + 2 : at + 3, :] = -scale * sum_g / live - row(k, 0) * on_u

    def grad_u(g, u, b, at=48):
        inner_grad = g * vec[at : at + 1, :] + (u * vec[at + 1 : at + 2, :] + vec[at + 2 : at + 3, :])
        return masked(inner_grad, b).astype(BF16)

    def stats(x):
        def step(b, rows, i, carry):
            u = x[rows, :]
            return carry[0] + fold(u), carry[1] + fold(u * u)
        sums, squares = each(step, (zero8, zero8))
        return down_to_row(sums), down_to_row(squares)

    def window(base, width, b, r0, c0, lanes):
        side = sides[b]
        return jnp.concatenate(
            [
                pool[base + ((r0 + i) * width + c0) * 16 : base + ((r0 + i) * width + c0 + side) * 16, lanes]
                for i in range(side)
            ],
            axis=0,
        )

    lane_halves = [slice(0, HALF), slice(HALF, WIDTH)]

    def pattern(size, bit, value):
        index = lax.broadcasted_iota(jnp.int32, (size, WIDTH), 0)
        return ((index // bit) % 2 == value).astype(F32)

    def fill_halo(base, b, low_r, high_r, low_c, high_c):
        side = sides[b]
        width = side + low_c + high_c
        def cell(r, c, n=1):
            return slice(base + (r * width + c) * 16, base + (r * width + c + n) * 16)
        for i in range(side):
            r = i + low_r
            if low_c:
                value = pool[cell(r, side), :].astype(F32)
                pool[cell(r, 0), :] = (pltpu.roll(value, 1, 0) * pattern(16, 1, 1)).astype(BF16)
            if high_c:
                value = pool[cell(r, low_c), :].astype(F32)
                pool[cell(r, width - 1), :] = (pltpu.roll(value, 15, 0) * pattern(16, 1, 0)).astype(BF16)
        size = width * 16
        if low_r:
            value = pool[cell(side, 0, width), :].astype(F32)
            pool[cell(0, 0, width), :] = (pltpu.roll(value, 2, 0) * pattern(size, 2, 1)).astype(BF16)
        if high_r:
            value = pool[cell(low_r, 0, width), :].astype(F32)
            pool[cell(low_r + side, 0, width), :] = (
                pltpu.roll(value, size - 2, 0) * pattern(size, 2, 0)
            ).astype(BF16)

    index48 = lax.broadcasted_iota(jnp.int32, (48, 48), 0) // 4
    same_image = (index48 == lax.broadcasted_iota(jnp.int32, (48, 48), 1) // 4).astype(F32)
    first_of_image = (lax.broadcasted_iota(jnp.int32, (48, WIDTH), 0) % 4 == 0).astype(F32)

    def squeeze_excite(x, k, down, downb, up, upb, se, sq):
        def step(b, rows, i, carry):
            v = half_silu(half(k, x[rows, :])).reshape(-1, 16, WIDTH)
            return tuple(c + jnp.sum(v, axis=0) if d == b else c for d, c in enumerate(carry))
        zero16 = jnp.zeros((16, WIDTH), F32)
        sums = each(step, tuple(zero16 for _ in buckets))
        scaled = jnp.concatenate([s * (1.0 / (4 * side * side)) for s, side in zip(sums, sides)], axis=0)
        pooled = exact(same_image, scaled, ((1,), (0,)))
        squeeze_pre = exact(pooled, down[...], ((1,), (0,))) + downb[...]
        squeezed = squeeze_pre * jax.nn.sigmoid(squeeze_pre)
        excite = jax.nn.sigmoid(exact(squeezed, up[...], ((1,), (0,))) + upb[...])
        se[0] = pooled
        sq[...] = squeeze_pre
        for b in buckets:
            se[1, 16 * b : 16 * b + 16, :] = excite[16 * b : 16 * b + 16, :] * mask[b]

    def gate(x, k, se, store):
        def step(b, rows, i, carry):
            v = half_silu(half(k, x[rows, :])).reshape(-1, 16, WIDTH)
            v = v * se[1, 16 * b : 16 * b + 16, :][None]
            store(rows, v.reshape(-1, WIDTH).astype(BF16))
            return carry
        each(step, 0)

    def squeeze_excite_back(g, u, k, down, up, se, sq, ddown, ddownb, dup, dupb):
        def step(b, rows, i, carry):
            v = half_silu(half(k, u[rows, :])) * g[rows, :]
            return tuple(
                c + jnp.sum(v.reshape(-1, 16, WIDTH), axis=0) if d == b else c
                for d, c in enumerate(carry)
            )
        zero16 = jnp.zeros((16, WIDTH), F32)
        sums = each(step, tuple(zero16 for _ in buckets))
        grad_excite = exact(same_image, jnp.concatenate(sums, axis=0), ((1,), (0,)))
        excite = se[1]
        grad_up = grad_excite * excite * (1.0 - excite)
        squeeze_pre = sq[...]
        sig = jax.nn.sigmoid(squeeze_pre)
        once = first_of_image
        dup[...] = exact(squeeze_pre * sig, grad_up * once, ((0,), (0,)))
        dupb[...] = down_to_row(grad_up * once)
        grad_pre = exact(grad_up, up[...], ((1,), (1,))) * (sig * (1.0 + squeeze_pre * (1.0 - sig)))
        ddown[...] = exact(se[0] * once, grad_pre, ((0,), (0,)))
        ddownb[...] = down_to_row(grad_pre * once[:, : grad_pre.shape[1]])
        pooled_grad = exact(grad_pre, down[...], ((1,), (1,)))
        for b in buckets:
            pixels = 4 * sides[b] * sides[b]
            vec[56 + 16 * b : 72 + 16 * b, :] = pooled_grad[16 * b : 16 * b + 16, :] * (1.0 / pixels)

        def apply(b, rows, i, carry):
            u_now = u[rows, :]
            y = half(k, u_now)
            slope = half_silu_grad(y, jnp.tanh(y))
            gv = g[rows, :].reshape(-1, 16, WIDTH) * se[1, 16 * b : 16 * b + 16, :][None]
            gv = (gv + vec[56 + 16 * b : 72 + 16 * b, :][None]).reshape(-1, WIDTH) * slope
            g[rows, :] = gv
            return carry[0] + fold(gv), carry[1] + fold(gv * (u_now - row(k, 0)))

        sum_g, sum_d = each(apply, (zero8, zero8))
        return down_to_row(sum_g), down_to_row(sum_d)

    def put_norm_grads(out, index, k, sum_g, sum_d):
        out[2 * index : 2 * index + 1, :] = row(k, 1) * sum_d
        out[2 * index + 1 : 2 * index + 2, :] = sum_g

    planes = [(0, 0), (0, 1), (1, 0), (1, 1)]

    chunk = total // 5
    def stat_dot(plane, weight, carry):
        def step(i, kept):
            u = dot(acts[plane, aligned(i * chunk, chunk), :], weight[...])
            return kept[0] + fold(u), kept[1] + fold(u * u)
        return lax.fori_loop(0, 5, step, carry)
    carry = (zero8, zero8)
    for plane in range(4):
        carry = stat_dot(plane, w_in1, carry)
    short = stat_dot(0, w_short, (zero8, zero8))
    local_count = jnp.concatenate([count[0:1, :]] * 4, axis=1)
    sums = all_sum([down_to_row(v) for v in carry] + [down_to_row(v) for v in short] + [local_count])
    live = sums[4]
    set_norm(0, sums[0], sums[1], norms1, 0, 4.0 * live)
    set_norm(3, sums[2], sums[3], norms1, 3, live)
    vec[54:55, :] = live

    end = 0
    h1_bases = []
    for pr, pc in planes:
        grid_bases, end = geo.grid(pr, pc, end)
        h1_bases.append(grid_bases)
    for plane, (pr, pc) in enumerate(planes):
        x1[...] = dot(acts[plane], w_in1[...])
        def step(b, rows, i, carry, plane=plane, pr=pr, pc=pc):
            width = sides[b] + pc
            start = h1_bases[plane][b] + ((i + pr) * width + pc) * 16
            pool[aligned(start, sides[b] * 16), :] = masked(half_silu(half(0, x1[rows, :])), b).astype(BF16)
            return carry
        each(step, 0)
        for b in buckets:
            fill_halo(h1_bases[plane][b], b, pr, 0, pc, 0)
    for b in buckets:
        for h, lanes in enumerate(lane_halves):
            parts = []
            for tap in range(TAPS):
                dy, dx = tap // 3, tap % 3
                pr, pc = int(dy != 1), int(dx != 1)
                parts.append(
                    window(h1_bases[2 * pr + pc][b], sides[b] + pc, b, int(dy == 2), int(dx == 2), lanes)
                )
            x0[bases[b] : bases[b] + rows_of[b], lanes] = dot(
                jnp.concatenate(parts, axis=1), bd1[h].reshape(TAPS * HALF, HALF)
            )
    h1b_bases, end = geo.grid(2, 2, 0)
    g2b_bases, end = geo.grid(2, 2, end)
    h2b, cot_at = end, end + total
    g3b = cot_at
    fetch = pltpu.make_async_copy(cot_hbm, pool.at[pl.ds(cot_at, total)], sems.at[0])
    fetch.start()
    live = vec[54:55, :]
    sums = all_sum(list(stats(x0)))
    set_norm(1, sums[0], sums[1], norms1, 1, live)
    squeeze_excite(x0, 1, down1, downb1, up1, upb1, se1, sq1)
    def keep_h2(rows, value):
        h2[rows, :] = value
    gate(x0, 1, se1, keep_h2)
    x1[...] = dot(h2[...], w_out1[...])
    sums = all_sum(list(stats(x1)))
    set_norm(2, sums[0], sums[1], norms1, 2, live)
    x2[...] = dot(acts[0], w_short[...])
    def middle(b, rows, i, carry):
        y = half(2, x1[rows, :]) + half(3, x2[rows, :])
        mid[rows, :] = masked(half_silu(y), b).astype(BF16)
        return carry
    each(middle, 0)

    x2[...] = dot(mid[...], w_in2[...])
    sums = all_sum(list(stats(x2)))
    set_norm(4, sums[0], sums[1], norms2, 0, live)
    def hidden(b, rows, i, carry):
        start = h1b_bases[b] + ((i + 1) * (sides[b] + 2) + 1) * 16
        pool[aligned(start, sides[b] * 16), :] = masked(half_silu(half(4, x2[rows, :])), b).astype(BF16)
        return carry
    each(hidden, 0)
    for b in buckets:
        fill_halo(h1b_bases[b], b, 1, 1, 1, 1)
        for h, lanes in enumerate(lane_halves):
            parts = [
                window(h1b_bases[b], sides[b] + 2, b, tap // 3, tap % 3, lanes) for tap in range(TAPS)
            ]
            x3[bases[b] : bases[b] + rows_of[b], lanes] = dot(
                jnp.concatenate(parts, axis=1), bd2[h].reshape(TAPS * HALF, HALF)
            )
    sums = all_sum(list(stats(x3)))
    set_norm(5, sums[0], sums[1], norms2, 1, live)
    squeeze_excite(x3, 5, down2, downb2, up2, upb2, se2, sq2)
    def keep_h2b(rows, value):
        pool[aligned(rows.start + h2b, rows.size), :] = value
    gate(x3, 5, se2, keep_h2b)
    x1[...] = dot(pool[h2b : h2b + total, :], w_out2[...])
    sums = all_sum(list(stats(x1)))
    set_norm(6, sums[0], sums[1], norms2, 2, live)
    fetch.wait()
    out_at = g2b_bases[0]
    def finish(b, rows, i, carry):
        u = x1[rows, :]
        y = half(6, u) + 0.5 * mid[rows, :].astype(F32)
        tan = jnp.tanh(y)
        pool[aligned(rows.start + out_at, rows.size), :] = masked(y + y * tan, b).astype(BF16)
        g = pool[aligned(rows.start + cot_at, rows.size), :].astype(F32) * half_silu_grad(y, tan)
        x2[rows, :] = g
        return carry[0] + fold(g), carry[1] + fold(g * (u - row(6, 0)))
    local = [down_to_row(v) for v in each(finish, (zero8, zero8))]
    put_out = pltpu.make_async_copy(pool.at[pl.ds(out_at, total)], out_hbm, sems.at[1])
    put_out.start()

    put_norm_grads(dnorms2, 2, 6, *local)
    set_grad(6, *all_sum(local), live)
    def third(b, rows, i, carry):
        pool[aligned(rows.start + g3b, rows.size), :] = grad_u(x2[rows, :], x1[rows, :], b)
        return carry
    each(third, 0)
    dw_out2[...] = dot_tn(pool[h2b : h2b + total, :], pool[g3b : g3b + total, :])
    x1[...] = dot_nt(pool[g3b : g3b + total, :], w_out2[...])
    local = squeeze_excite_back(x1, x3, 5, down2, up2, se2, sq2, ddown2, ddownb2, dup2, dupb2)
    put_norm_grads(dnorms2, 1, 5, *local)
    set_grad(5, *all_sum(list(local)), live)
    put_out.wait()
    def second(b, rows, i, carry):
        start = g2b_bases[b] + ((i + 1) * (sides[b] + 2) + 1) * 16
        pool[aligned(start, sides[b] * 16), :] = grad_u(x1[rows, :], x3[rows, :], b)
        return carry
    each(second, 0)
    for b in buckets:
        fill_halo(g2b_bases[b], b, 1, 1, 1, 1)
        for h, lanes in enumerate(lane_halves):
            parts = [
                window(g2b_bases[b], sides[b] + 2, b, 2 - tap // 3, 2 - tap % 3, lanes) for tap in range(TAPS)
            ]
            x1[bases[b] : bases[b] + rows_of[b], lanes] = dot_nt(
                jnp.concatenate(parts, axis=1),
                jnp.concatenate([bd2[h, tap] for tap in range(TAPS)], axis=1),
            )
    for h, lanes in enumerate(lane_halves):
        source = jnp.concatenate(
            [window(h1b_bases[b], sides[b] + 2, b, 1, 1, lanes) for b in buckets], axis=0
        )
        for tap in range(TAPS):
            target = jnp.concatenate(
                [window(g2b_bases[b], sides[b] + 2, b, 2 - tap // 3, 2 - tap % 3, lanes) for b in buckets],
                axis=0,
            )
            acc[tap, h] = diagonal(dot_tn(source, target))
    put_group2 = pltpu.make_async_copy(acc, dwg2_hbm, sems.at[2])
    put_group2.start()
    x3[...] = dot(mid[...], w_in2[...])
    def first(b, rows, i, carry):
        u = x3[rows, :]
        y = half(4, u)
        g = x1[rows, :] * half_silu_grad(y, jnp.tanh(y))
        x1[rows, :] = g
        return carry[0] + fold(g), carry[1] + fold(g * (u - row(4, 0)))
    local = [down_to_row(v) for v in each(first, (zero8, zero8))]
    put_norm_grads(dnorms2, 0, 4, *local)
    set_grad(4, *all_sum(local), live)
    def first_u(b, rows, i, carry):
        pool[aligned(rows.start + g3b, rows.size), :] = grad_u(x1[rows, :], x3[rows, :], b)
        return carry
    each(first_u, 0)
    dw_in2[...] = dot_tn(mid[...], pool[g3b : g3b + total, :])
    x2[...] = x2[...] + dot_nt(pool[g3b : g3b + total, :], w_in2[...])

    x3[...] = dot(h2[...], w_out1[...])
    x1[...] = dot(acts[0], w_short[...])
    def joined(b, rows, i, carry):
        u, s = x3[rows, :], x1[rows, :]
        y = half(2, u) + half(3, s)
        g = x2[rows, :] * half_silu_grad(y, jnp.tanh(y))
        x2[rows, :] = g
        return (
            carry[0] + fold(g),
            carry[1] + fold(g * (u - row(2, 0))),
            carry[2] + fold(g * (s - row(3, 0))),
        )
    local = [down_to_row(v) for v in each(joined, (zero8, zero8, zero8))]
    put_norm_grads(dnorms1, 2, 2, local[0], local[1])
    put_norm_grads(dnorms1, 3, 3, local[0], local[2])
    sums = all_sum(local)
    set_grad(2, sums[0], sums[1], live)
    set_grad(3, sums[0], sums[2], live, 51)
    def both(b, rows, i, carry):
        g = x2[rows, :]
        pool[rows, :] = grad_u(g, x3[rows, :], b)
        mid[rows, :] = grad_u(g, x1[rows, :], b, 51)
        return carry
    each(both, 0)
    put_short = pltpu.make_async_copy(mid, gs_hbm, sems.at[3])
    put_short.start()
    dw_short[...] = dot_tn(acts[0], mid[...])
    dw_out1[...] = dot_tn(h2[...], pool[0:total, :])
    x1[...] = dot_nt(pool[0:total, :], w_out1[...])
    local = squeeze_excite_back(x1, x0, 1, down1, up1, se1, sq1, ddown1, ddownb1, dup1, dupb1)
    put_norm_grads(dnorms1, 1, 1, *local)
    set_grad(1, *all_sum(list(local)), live)
    g2_bases, end = geo.grid(1, 1, 0)
    g1_at = end
    def second_one(b, rows, i, carry):
        start = g2_bases[b] + (i * (sides[b] + 1)) * 16
        pool[aligned(start, sides[b] * 16), :] = grad_u(x1[rows, :], x0[rows, :], b)
        return carry
    each(second_one, 0)
    for b in buckets:
        fill_halo(g2_bases[b], b, 0, 1, 0, 1)
    put_group2.wait()
    carry = (zero8, zero8)
    for plane, (pr, pc) in enumerate(planes):
        taps = [
            tap for tap in range(TAPS) if int(tap // 3 != 1) == pr and int(tap % 3 != 1) == pc
        ]
        for b in buckets:
            size = rows_of[b]
            x0[0:size, :] = dot(acts[plane, bases[b] : bases[b] + size, :], w_in1[...])
            for h, lanes in enumerate(lane_halves):
                parts = [
                    window(g2_bases[b], sides[b] + 1, b, int(tap // 3 == 0), int(tap % 3 == 0), lanes)
                    for tap in taps
                ]
                x1[0:size, lanes] = dot_nt(
                    jnp.concatenate(parts, axis=1), jnp.concatenate([bd1[h, tap] for tap in taps], axis=1)
                )
            def line(i, kept, b=b, plane=plane):
                rows = aligned(i * sides[b] * 16, sides[b] * 16)
                u = x0[rows, :]
                y = half(0, u)
                tan = jnp.tanh(y)
                h2[rows, :] = masked(y + y * tan, b).astype(BF16)
                g = x1[rows, :] * half_silu_grad(y, tan)
                start = g1_at + plane * total + bases[b] + i * sides[b] * 16
                pool[aligned(start, sides[b] * 16), :] = g.astype(BF16)
                return kept[0] + fold(g), kept[1] + fold(g * (u - row(0, 0)))
            carry = lax.fori_loop(0, sides[b], line, carry)
            for h, lanes in enumerate(lane_halves):
                source = h2[0:size, lanes]
                for tap in taps:
                    target = window(
                        g2_bases[b], sides[b] + 1, b, int(tap // 3 == 0), int(tap % 3 == 0), lanes
                    )
                    if b == 0:
                        acc[tap, h] = diagonal(dot_tn(source, target))
                    else:
                        acc[tap, h] += diagonal(dot_tn(source, target))
    put_group1 = pltpu.make_async_copy(acc, dwg1_hbm, sems.at[2])
    put_group1.start()
    local = [down_to_row(v) for v in carry]
    put_norm_grads(dnorms1, 0, 0, *local)
    set_grad(0, *all_sum(local), 4.0 * live)
    puts = []
    for plane in range(4):
        x0[...] = dot(acts[plane], w_in1[...])
        at = g1_at + plane * total
        def first_one(b, rows, i, carry, at=at):
            here = aligned(rows.start + at, rows.size)
            pool[here, :] = grad_u(pool[here, :].astype(F32), x0[rows, :], b)
            return carry
        each(first_one, 0)
        part = dot_tn(acts[plane], pool[at : at + total, :])
        if plane == 0:
            dw_in1[...] = part
        else:
            dw_in1[...] += part
        put = pltpu.make_async_copy(pool.at[pl.ds(at, total)], g1_hbm.at[plane], sems.at[4 + plane])
        put.start()
        puts.append(put)
    for put in puts:
        put.wait()
    put_short.wait()
    put_group1.wait()


def whole():
    return pl.BlockSpec(memory_space=pltpu.VMEM)


def anywhere():
    return pl.BlockSpec(memory_space=pl.ANY)


def shape(dims, dtype=F32):
    return jax.ShapeDtypeStruct(dims, dtype)


def blocks(geo, acts, mask, count, first, second, cot):
    groups, inner = lax.axis_size("dp"), lax.axis_size("fsdp")
    total = geo.total
    (w_in1, wg1, down1, downb1, up1, upb1, w_out1, w_short, norms1) = first
    (w_in2, wg2, down2, downb2, up2, upb2, w_out2, norms2) = second
    ins = [
        acts, mask, count,
        w_in1, block_diagonal(wg1), down1.astype(F32), downb1.astype(F32), up1.astype(F32), upb1.astype(F32),
        w_out1, w_short, norms1.astype(F32),
        w_in2, block_diagonal(wg2), down2.astype(F32), downb2.astype(F32), up2.astype(F32), upb2.astype(F32),
        w_out2, norms2.astype(F32),
        cot,
    ]
    hbm_outs = [
        shape((total, WIDTH), BF16), shape((4, total, WIDTH), BF16), shape((total, WIDTH), BF16),
        shape((TAPS, 2, HALF, GROUP_WIDTH)), shape((TAPS, 2, HALF, GROUP_WIDTH)),
    ]
    vmem_outs = []
    for is_first in (True, False):
        dims = shapes_of(is_first)
        vmem_outs.extend(shape(d) for j, d in enumerate(dims) if j != 1)
    pool_rows = 0
    for pr, pc in ((0, 0), (0, 1), (1, 0), (1, 1)):
        pool_rows = geo.grid(pr, pc, pool_rows)[1]
    pool_rows = max(
        pool_rows, geo.grid(2, 2, geo.grid(2, 2, 0)[1])[1] + 2 * total, geo.grid(1, 1, 0)[1] + 4 * total
    )
    stages = exchange_stages(groups, inner)
    big = pltpu.VMEM((total, WIDTH), F32)
    scratch = [
        pltpu.VMEM((pool_rows, WIDTH), BF16), big, big, big, big,
        pltpu.VMEM((total, WIDTH), BF16), pltpu.VMEM((total, WIDTH), BF16),
        pltpu.VMEM((TAPS, 2, HALF, GROUP_WIDTH), F32), pltpu.VMEM((104, WIDTH), F32),
        pltpu.VMEM((2, 48, WIDTH), F32), pltpu.VMEM((48, SQUEEZE_A), F32),
        pltpu.VMEM((2, 48, WIDTH), F32), pltpu.VMEM((48, SQUEEZE_B), F32),
        pltpu.VMEM((2 * len(stages), 24, 128), F32),
        pltpu.VMEM((2 * len(stages), max(stages) - 1, 24, 128), F32),
        pltpu.SemaphoreType.DMA((2 * len(stages),)), pltpu.SemaphoreType.DMA((2 * len(stages),)),
        pltpu.SemaphoreType.DMA((8,)),
    ]
    outs = pl.pallas_call(
        functools.partial(body, geo, groups, inner),
        out_shape=hbm_outs + vmem_outs,
        in_specs=[whole()] * 20 + [anywhere()],
        out_specs=[anywhere()] * 5 + [whole()] * len(vmem_outs),
        scratch_shapes=scratch,
        compiler_params=pltpu.CompilerParams(
            collective_id=0, has_side_effects=True, vmem_limit_bytes=LIMIT
        ),
    )(*ins)
    out, g1, gs, dwg1, dwg2 = outs[:5]
    d_in1, d_down1, d_downb1, d_up1, d_upb1, d_out1, d_short, d_norms1 = outs[5:13]
    d_in2, d_down2, d_downb2, d_up2, d_upb2, d_out2, d_norms2 = outs[13:]
    first_grads = [d_in1, dwg1, d_down1, d_downb1, d_up1, d_upb1, d_out1, d_short, d_norms1]
    second_grads = [d_in2, dwg2, d_down2, d_downb2, d_up2, d_upb2, d_out2, d_norms2]
    return out, g1, gs, first_grads, second_grads


def slab(width):
    return -(-width // 16) * 16


def image_permutation(side):
    padded = slab(4 * side)
    matrix = np.zeros((2, side, 8, 2, 8, padded), np.float32)
    for pc in range(2):
        for j in range(side):
            for k in range(8):
                for qc in range(2):
                    matrix[pc, j, k, qc, k, qc * 2 * side + 2 * j + pc] = 1.0
    return matrix.reshape(32 * side, 8 * padded)


def inner_permutation(side):
    padded = slab(2 * side)
    matrix = np.zeros((side, 8, 2, 8, padded), np.float32)
    for j in range(side):
        for k in range(8):
            for qc in range(2):
                matrix[j, k, qc, k, qc * side + j] = 1.0
    return matrix.reshape(16 * side, 8 * padded)


def arrange_body(geo, *refs):
    images, cots, mask = refs[0:3], refs[3:6], refs[6]
    image_perms, inner_perms = refs[7:10], refs[10:13]
    acts, cot = refs[13:15]
    stages = refs[15:21]
    for b, side in enumerate(geo.sides):
        for planes, source, perm, stage, width in (
            (2, images[b], image_perms[b], stages[b], 4 * side),
            (1, cots[b], inner_perms[b], stages[3 + b], 2 * side),
        ):
            stage[...] = jnp.zeros_like(stage)
            padded = slab(width)
            def line(i, carry, b=b, side=side, planes=planes, source=source, perm=perm, stage=stage, width=width, padded=padded):
                size = side * 16
                for pr in range(planes):
                    for k in range(8):
                        stage[k * padded : k * padded + width, :] = source[
                            k // 2, (k % 2) * planes * side + planes * i + pr
                        ]
                    moved = dot(perm[...], stage[...])
                    rows = aligned(geo.bases[b] + i * size, size)
                    for pc in range(planes):
                        part = moved[pc * size : (pc + 1) * size].reshape(side, 16, -1)
                        part = (part * mask[b][None, :, : part.shape[2]]).reshape(size, -1).astype(BF16)
                        if planes == 2:
                            acts[2 * pr + pc, rows, :] = part
                        else:
                            cot[rows, :] = part
                return carry
            lax.fori_loop(0, side, line, 0)


def arrange(geo, images, cots, mask):
    image_perms = [jnp.asarray(image_permutation(side), BF16) for side in geo.sides]
    inner_perms = [jnp.asarray(inner_permutation(side), BF16) for side in geo.sides]
    ins = [*images, *cots, mask, *image_perms, *inner_perms]
    return pl.pallas_call(
        functools.partial(arrange_body, geo),
        out_shape=[shape((4, geo.total, WIDTH_IN), BF16), shape((geo.total, WIDTH), BF16)],
        in_specs=[whole()] * len(ins),
        out_specs=[whole()] * 2,
        scratch_shapes=[pltpu.VMEM((8 * slab(4 * side), WIDTH_IN), BF16) for side in geo.sides]
        + [pltpu.VMEM((8 * slab(2 * side), WIDTH), BF16) for side in geo.sides],
        compiler_params=pltpu.CompilerParams(vmem_limit_bytes=LIMIT),
    )(*ins)


def restore_body(geo, *refs):
    g1, gs, out, w_in, w_short = refs[0:5]
    image_perms, inner_perms = refs[5:8], refs[8:11]
    outputs, image_grads = refs[11:14], refs[14:17]
    for b, side in enumerate(geo.sides):
        def line(i, carry, b=b, side=side):
            size = side * 16
            rows = aligned(geo.bases[b] + i * size, size)
            padded = slab(2 * side)
            moved = dot_tn(inner_perms[b][...], out[rows, :]).astype(BF16)
            for k in range(8):
                outputs[b][k // 2, (k % 2) * side + i] = moved[k * padded : k * padded + 2 * side]
            padded = slab(4 * side)
            for pr in range(2):
                values = [dot_nt(g1[2 * pr + pc, rows, :], w_in[...]) for pc in range(2)]
                if pr == 0:
                    values[0] = values[0] + dot_nt(gs[rows, :], w_short[...])
                value = jnp.concatenate(values, axis=0)
                high = value.astype(BF16)
                low = (value - high.astype(F32)).astype(BF16)
                moved = dot_tn(image_perms[b][...], high) + dot_tn(image_perms[b][...], low)
                for k in range(8):
                    image_grads[b][k // 2, (k % 2) * 2 * side + 2 * i + pr] = moved[
                        k * padded : k * padded + 4 * side
                    ]
            return carry
        lax.fori_loop(0, side, line, 0)


def restore(geo, g1, gs, out, w_in, w_short):
    image_perms = [jnp.asarray(image_permutation(side), BF16) for side in geo.sides]
    inner_perms = [jnp.asarray(inner_permutation(side), BF16) for side in geo.sides]
    ins = [g1, gs, out, w_in, w_short, *image_perms, *inner_perms]
    outs = [shape((4, 2 * side, 2 * side, WIDTH), BF16) for side in geo.sides]
    outs = outs + [shape((4, 4 * side, 4 * side, WIDTH_IN)) for side in geo.sides]
    return pl.pallas_call(
        functools.partial(restore_body, geo),
        out_shape=outs,
        in_specs=[whole()] * len(ins),
        out_specs=[whole()] * len(outs),
        compiler_params=pltpu.CompilerParams(vmem_limit_bytes=LIMIT),
    )(*ins)


def gather(shard):
    return lax.all_gather(shard.astype(BF16), ("dp", "fsdp"), axis=0, tiled=True)


def scatter_grads(flat):
    return lax.psum_scatter(flat, ("dp", "fsdp"), scatter_dimension=0, tiled=True)


def per_device(*args):
    images, counts = args[0:3], args[3]
    first_params, second_params = args[4:6]
    cots = args[6:9]
    geo = Geometry([image.shape[1] // 4 for image in images])
    slot = jnp.arange(16, dtype=jnp.int32) // 4
    mask = (slot[None, :, None] < counts[0][:, None, None]).astype(F32)
    mask = jnp.broadcast_to(mask, (3, 16, WIDTH))
    pixels = jnp.asarray([4 * side * side for side in geo.sides], jnp.int32)
    count = jnp.full((8, 128), 1.0, F32) * jnp.sum(counts[0] * pixels).astype(F32)
    acts, cot = arrange(geo, images, cots, mask)
    first_full, second_full = gather(first_params), gather(second_params)
    first, second = unflatten(first_full, True), unflatten(second_full, False)
    out, g1, gs, first_grads, second_grads = blocks(geo, acts, mask, count, first, second, cot)
    results = restore(geo, g1, gs, out, first[0], first[7])
    first_out = scatter_grads(flatten(first_grads, first_full.shape[0]))
    second_out = scatter_grads(flatten(second_grads, second_full.shape[0]))
    return (*results, first_out, second_out)


def solution(mesh):
    images = P(("dp", "fsdp"), None, None, None)
    flat = P(("dp", "fsdp"))
    in_specs = (images, images, images, P(("dp", "fsdp"), None), flat, flat, images, images, images)
    out_specs = (images,) * 6 + (flat, flat)
    return jax.shard_map(per_device, mesh=mesh, in_specs=in_specs, out_specs=out_specs, check_vma=False)
```

```python
import functools
import math

import jax
import jax.numpy as jnp
from jax import lax
from jax.experimental import pallas as pl
from jax.experimental.pallas import tpu as pltpu
from jax.sharding import PartitionSpec as P

WIDTH_IN = 192
GROUPS = 8
GROUP_WIDTH = 64
SQUEEZE_A = 48
SQUEEZE_B = 128
WIDTH = 512
HALF = 256
TAPS = 9
EPSILON = 1e-05
HIGHEST = lax.Precision.HIGHEST
MESH = pl.DeviceIdType.MESH
F32 = jnp.float32
BF16 = jnp.bfloat16
LIMIT = 63 * 2**20


def shapes_of(is_first):
    width_in, squeeze = (WIDTH_IN, SQUEEZE_A) if is_first else (WIDTH, SQUEEZE_B)
    shapes = [
        (width_in, WIDTH),
        (TAPS, GROUPS, GROUP_WIDTH, GROUP_WIDTH),
        (WIDTH, squeeze),
        (1, squeeze),
        (squeeze, WIDTH),
        (1, WIDTH),
        (WIDTH, WIDTH),
    ]
    if is_first:
        shapes.append((WIDTH_IN, WIDTH))
    shapes.append((8 if is_first else 6, WIDTH))
    return shapes


def diagonal(product):
    parts = []
    for g in range(4):
        lanes = slice(128 * (g // 2), 128 * (g // 2) + 128)
        parts.append(product[g * GROUP_WIDTH : (g + 1) * GROUP_WIDTH, lanes])
    return jnp.concatenate(parts, axis=0)


def dot(left, right):
    return jnp.dot(left, right, preferred_element_type=F32)


def dot_nt(left, right):
    return lax.dot_general(left, right, (((1,), (1,)), ((), ())), preferred_element_type=F32)


def dot_tn(left, right):
    return lax.dot_general(left, right, (((0,), (0,)), ((), ())), preferred_element_type=F32)


def exact(left, right, dims):
    return lax.dot_general(
        left, right, (dims, ((), ())), precision=HIGHEST, preferred_element_type=F32
    )


def half_silu(half):
    return half + half * jnp.tanh(half)


def half_silu_grad(half, tan):
    return (0.5 + 0.5 * tan) * (1.0 + half * (1.0 - tan))


def fold(values):
    return jnp.sum(values.reshape(-1, 8, WIDTH), axis=0)


def down_to_row(values):
    return jnp.sum(values, axis=0, keepdims=True)


class Geometry:
    def __init__(self, sides):
        self.sides = sides
        self.rows = [side * side * 16 for side in sides]
        self.bases = [sum(self.rows[:b]) for b in range(len(sides))]
        self.total = sum(self.rows)

    def grid(self, extra_rows, extra_cols, start):
        bases = []
        for side in self.sides:
            bases.append(start)
            start = start + (side + extra_rows) * (side + extra_cols) * 16
        return bases, start


def exchange_stages(groups, inner):
    return [groups * inner] if groups * inner <= 64 else [inner, groups]


def aligned(start, size):
    return pl.ds(pl.multiple_of(start, 16), size)


def body(geo, groups, inner, *refs):
    (
        acts, mask, count,
        w_in1, bd1, down1, downb1, up1, upb1, w_out1, w_short, norms1,
        w_in2, bd2, down2, downb2, up2, upb2, w_out2, norms2,
        cot_hbm,
        out_hbm, g1_hbm, gs_hbm, dwg1_hbm, dwg2_hbm,
        dw_in1, ddown1, ddownb1, dup1, dupb1, dw_out1, dw_short, dnorms1,
        dw_in2, ddown2, ddownb2, dup2, dupb2, dw_out2, dnorms2,
        pool, x0, x1, x2, x3, h2, mid, acc, vec, se1, sq1, se2, sq2,
        pay, slots, send_sem, recv_sem, sems,
    ) = refs
    sides, bases, rows_of, total = geo.sides, geo.bases, geo.rows, geo.total
    buckets = range(len(sides))
    devices = groups * inner

    outer_index, inner_index = lax.axis_index("dp"), lax.axis_index("fsdp")

    def any_partner(step):
        other = lax.rem(outer_index * inner + inner_index + step, devices)
        return (other // inner, lax.rem(other, inner))

    def inner_partner(step):
        return (outer_index, lax.rem(inner_index + step, inner))

    def outer_partner(step):
        return (lax.rem(outer_index + step, groups), inner_index)

    barrier = pltpu.get_barrier_semaphore()
    stages = exchange_stages(groups, inner)
    if len(stages) == 1:
        partners = [any_partner]
    else:
        partners = [inner_partner, outer_partner]
    for count_in_stage, partner in zip(stages, partners):

        def greet(step, carry, partner=partner):
            pl.semaphore_signal(barrier, inc=1, device_id=partner(step), device_id_type=MESH)
            return carry

        lax.fori_loop(1, count_in_stage, greet, 0)

    calls = []

    def all_sum(rows):
        parity = len(calls) % 2
        size = -(-len(rows) * 4 // 8) * 8
        if not calls:
            pl.semaphore_wait(barrier, sum(stages) - len(stages))
        calls.append(size)
        sums = None
        for stage, partner in enumerate(partners):
            at = 2 * stage + parity
            if sums is None:
                for r, row in enumerate(rows):
                    for c in range(4):
                        pay[at, 4 * r + c : 4 * r + c + 1, :] = row[:, c * 128 : (c + 1) * 128]
            else:
                pay[at, 0:size, :] = sums

            def send(step, carry, at=at, partner=partner):
                pltpu.make_async_remote_copy(
                    src_ref=pay.at[at, pl.ds(0, size)],
                    dst_ref=slots.at[at, step - 1, pl.ds(0, size)],
                    send_sem=send_sem.at[at],
                    recv_sem=recv_sem.at[at],
                    device_id=partner(step),
                    device_id_type=MESH,
                ).start()
                return carry

            others = stages[stage] - 1
            lax.fori_loop(1, others + 1, send, 0)
            landed = slots.at[at, pl.ds(0, others), pl.ds(0, size)]
            pltpu.make_async_copy(landed, landed, recv_sem.at[at]).wait()
            sums = pay[at, 0:size, :] + jnp.sum(slots[at, 0:others, 0:size, :], axis=0)
            pltpu.make_async_copy(landed, landed, send_sem.at[at]).wait()
        return [
            jnp.concatenate([sums[4 * r + c : 4 * r + c + 1, :] for c in range(4)], axis=1)
            for r in range(len(rows))
        ]

    def each(step, carry):
        for b in buckets:
            def line(i, kept, b=b):
                size = sides[b] * 16
                return step(b, aligned(bases[b] + i * size, size), i, kept)
            carry = lax.fori_loop(0, sides[b], line, carry)
        return carry

    zero8 = jnp.zeros((8, WIDTH), F32)

    def masked(values, b):
        return (values.reshape(-1, 16, WIDTH) * mask[b][None]).reshape(values.shape)

    def set_norm(k, sums, squares, norms, index, live):
        mean = sums / live
        inv_std = lax.rsqrt(squares / live - mean * mean + EPSILON)
        scale = inv_std * norms[2 * index : 2 * index + 1, :]
        offset = norms[2 * index + 1 : 2 * index + 2, :] - mean * scale
        for r, row in enumerate((mean, inv_std, scale, offset, 0.5 * scale, 0.5 * offset)):
            vec[6 * k + r : 6 * k + r + 1, :] = row

    def row(k, r):
        return vec[6 * k + r : 6 * k + r + 1, :]

    def half(k, u):
        return u * row(k, 4) + row(k, 5)

    def set_grad(k, sum_g, sum_d, live, at=48):
        scale, inv_std = row(k, 2), row(k, 1)
        on_u = -scale * inv_std * inv_std * sum_d / live
        vec[at : at + 1, :] = scale
        vec[at + 1 : at + 2, :] = on_u
        vec[at + 2 : at + 3, :] = -scale * sum_g / live - row(k, 0) * on_u

    def grad_u(g, u, b, at=48):
        inner_grad = g * vec[at : at + 1, :] + (u * vec[at + 1 : at + 2, :] + vec[at + 2 : at + 3, :])
        return masked(inner_grad, b).astype(BF16)

    def stats(x):
        def step(b, rows, i, carry):
            u = x[rows, :]
            return carry[0] + fold(u), carry[1] + fold(u * u)
        sums, squares = each(step, (zero8, zero8))
        return down_to_row(sums), down_to_row(squares)

    def window(base, width, b, r0, c0, lanes):
        side = sides[b]
        return jnp.concatenate(
            [
                pool[base + ((r0 + i) * width + c0) * 16 : base + ((r0 + i) * width + c0 + side) * 16, lanes]
                for i in range(side)
            ],
            axis=0,
        )

    lane_halves = [slice(0, HALF), slice(HALF, WIDTH)]

    def pattern(size, bit, value):
        index = lax.broadcasted_iota(jnp.int32, (size, WIDTH), 0)
        return ((index // bit) % 2 == value).astype(F32)

    def fill_halo(base, b, low_r, high_r, low_c, high_c):
        side = sides[b]
        width = side + low_c + high_c
        def cell(r, c, n=1):
            return slice(base + (r * width + c) * 16, base + (r * width + c + n) * 16)
        for i in range(side):
            r = i + low_r
            if low_c:
                value = pool[cell(r, side), :].astype(F32)
                pool[cell(r, 0), :] = (pltpu.roll(value, 4, 0) * pattern(16, 4, 1)).astype(BF16)
            if high_c:
                value = pool[cell(r, low_c), :].astype(F32)
                pool[cell(r, width - 1), :] = (pltpu.roll(value, 12, 0) * pattern(16, 4, 0)).astype(BF16)
        size = width * 16
        if low_r:
            value = pool[cell(side, 0, width), :].astype(F32)
            pool[cell(0, 0, width), :] = (pltpu.roll(value, 8, 0) * pattern(size, 8, 1)).astype(BF16)
        if high_r:
            value = pool[cell(low_r, 0, width), :].astype(F32)
            pool[cell(low_r + side, 0, width), :] = (
                pltpu.roll(value, size - 8, 0) * pattern(size, 8, 0)
            ).astype(BF16)

    index48 = [lax.broadcasted_iota(jnp.int32, (48, 48), axis) for axis in (0, 1)]
    image48 = [index // 16 * 4 + index % 4 for index in index48]
    same_image = (image48[0] == image48[1]).astype(F32)
    first_of_image = (lax.broadcasted_iota(jnp.int32, (48, WIDTH), 0) % 16 < 4).astype(F32)

    def squeeze_excite(x, k, down, downb, up, upb, se, sq):
        def step(b, rows, i, carry):
            v = half_silu(half(k, x[rows, :])).reshape(-1, 16, WIDTH)
            return tuple(c + jnp.sum(v, axis=0) if d == b else c for d, c in enumerate(carry))
        zero16 = jnp.zeros((16, WIDTH), F32)
        sums = each(step, tuple(zero16 for _ in buckets))
        scaled = jnp.concatenate([s * (1.0 / (4 * side * side)) for s, side in zip(sums, sides)], axis=0)
        pooled = exact(same_image, scaled, ((1,), (0,)))
        squeeze_pre = exact(pooled, down[...], ((1,), (0,))) + downb[...]
        squeezed = squeeze_pre * jax.nn.sigmoid(squeeze_pre)
        excite = jax.nn.sigmoid(exact(squeezed, up[...], ((1,), (0,))) + upb[...])
        se[0] = pooled
        sq[...] = squeeze_pre
        for b in buckets:
            se[1, 16 * b : 16 * b + 16, :] = excite[16 * b : 16 * b + 16, :] * mask[b]

    def gate(x, k, se, store):
        def step(b, rows, i, carry):
            v = half_silu(half(k, x[rows, :])).reshape(-1, 16, WIDTH)
            v = v * se[1, 16 * b : 16 * b + 16, :][None]
            store(rows, v.reshape(-1, WIDTH).astype(BF16))
            return carry
        each(step, 0)

    def squeeze_excite_back(g, u, k, down, up, se, sq, ddown, ddownb, dup, dupb):
        def step(b, rows, i, carry):
            v = half_silu(half(k, u[rows, :])) * g[rows, :]
            return tuple(
                c + jnp.sum(v.reshape(-1, 16, WIDTH), axis=0) if d == b else c
                for d, c in enumerate(carry)
            )
        zero16 = jnp.zeros((16, WIDTH), F32)
        sums = each(step, tuple(zero16 for _ in buckets))
        grad_excite = exact(same_image, jnp.concatenate(sums, axis=0), ((1,), (0,)))
        excite = se[1]
        grad_up = grad_excite * excite * (1.0 - excite)
        squeeze_pre = sq[...]
        sig = jax.nn.sigmoid(squeeze_pre)
        once = first_of_image
        dup[...] = exact(squeeze_pre * sig, grad_up * once, ((0,), (0,)))
        dupb[...] = down_to_row(grad_up * once)
        grad_pre = exact(grad_up, up[...], ((1,), (1,))) * (sig * (1.0 + squeeze_pre * (1.0 - sig)))
        ddown[...] = exact(se[0] * once, grad_pre, ((0,), (0,)))
        ddownb[...] = down_to_row(grad_pre * once[:, : grad_pre.shape[1]])
        pooled_grad = exact(grad_pre, down[...], ((1,), (1,)))
        for b in buckets:
            pixels = 4 * sides[b] * sides[b]
            vec[56 + 16 * b : 72 + 16 * b, :] = pooled_grad[16 * b : 16 * b + 16, :] * (1.0 / pixels)

        def apply(b, rows, i, carry):
            u_now = u[rows, :]
            y = half(k, u_now)
            slope = half_silu_grad(y, jnp.tanh(y))
            gv = g[rows, :].reshape(-1, 16, WIDTH) * se[1, 16 * b : 16 * b + 16, :][None]
            gv = (gv + vec[56 + 16 * b : 72 + 16 * b, :][None]).reshape(-1, WIDTH) * slope
            g[rows, :] = gv
            return carry[0] + fold(gv), carry[1] + fold(gv * (u_now - row(k, 0)))

        sum_g, sum_d = each(apply, (zero8, zero8))
        return down_to_row(sum_g), down_to_row(sum_d)

    def put_norm_grads(out, index, k, sum_g, sum_d):
        out[2 * index : 2 * index + 1, :] = row(k, 1) * sum_d
        out[2 * index + 1 : 2 * index + 2, :] = sum_g

    planes = [(0, 0), (0, 1), (1, 0), (1, 1)]

    chunk = total // 5
    def stat_dot(plane, weight, carry):
        def step(i, kept):
            u = dot(acts[plane, aligned(i * chunk, chunk), :], weight[...])
            return kept[0] + fold(u), kept[1] + fold(u * u)
        return lax.fori_loop(0, 5, step, carry)
    carry = (zero8, zero8)
    for plane in range(4):
        carry = stat_dot(plane, w_in1, carry)
    short = stat_dot(0, w_short, (zero8, zero8))
    local_count = jnp.concatenate([count[0:1, :]] * 4, axis=1)
    sums = all_sum([down_to_row(v) for v in carry] + [down_to_row(v) for v in short] + [local_count])
    live = sums[4]
    set_norm(0, sums[0], sums[1], norms1, 0, 4.0 * live)
    set_norm(3, sums[2], sums[3], norms1, 3, live)
    vec[54:55, :] = live

    end = 0
    h1_bases = []
    for pr, pc in planes:
        grid_bases, end = geo.grid(pr, pc, end)
        h1_bases.append(grid_bases)
    for plane, (pr, pc) in enumerate(planes):
        x1[...] = dot(acts[plane], w_in1[...])
        def step(b, rows, i, carry, plane=plane, pr=pr, pc=pc):
            width = sides[b] + pc
            start = h1_bases[plane][b] + ((i + pr) * width + pc) * 16
            pool[aligned(start, sides[b] * 16), :] = masked(half_silu(half(0, x1[rows, :])), b).astype(BF16)
            return carry
        each(step, 0)
        for b in buckets:
            fill_halo(h1_bases[plane][b], b, pr, 0, pc, 0)
    for b in buckets:
        for h, lanes in enumerate(lane_halves):
            parts = []
            for tap in range(TAPS):
                dy, dx = tap // 3, tap % 3
                pr, pc = int(dy != 1), int(dx != 1)
                parts.append(
                    window(h1_bases[2 * pr + pc][b], sides[b] + pc, b, int(dy == 2), int(dx == 2), lanes)
                )
            x0[bases[b] : bases[b] + rows_of[b], lanes] = dot(
                jnp.concatenate(parts, axis=1), bd1[h].reshape(TAPS * HALF, HALF)
            )
    h1b_bases, end = geo.grid(2, 2, 0)
    g2b_bases, end = geo.grid(2, 2, end)
    h2b, cot_at = end, end + total
    g3b = cot_at
    fetch = pltpu.make_async_copy(cot_hbm, pool.at[pl.ds(cot_at, total)], sems.at[0])
    fetch.start()
    live = vec[54:55, :]
    sums = all_sum(list(stats(x0)))
    set_norm(1, sums[0], sums[1], norms1, 1, live)
    squeeze_excite(x0, 1, down1, downb1, up1, upb1, se1, sq1)
    def keep_h2(rows, value):
        h2[rows, :] = value
    gate(x0, 1, se1, keep_h2)
    x1[...] = dot(h2[...], w_out1[...])
    sums = all_sum(list(stats(x1)))
    set_norm(2, sums[0], sums[1], norms1, 2, live)
    x2[...] = dot(acts[0], w_short[...])
    def middle(b, rows, i, carry):
        y = half(2, x1[rows, :]) + half(3, x2[rows, :])
        mid[rows, :] = masked(half_silu(y), b).astype(BF16)
        return carry
    each(middle, 0)

    x2[...] = dot(mid[...], w_in2[...])
    sums = all_sum(list(stats(x2)))
    set_norm(4, sums[0], sums[1], norms2, 0, live)
    def hidden(b, rows, i, carry):
        start = h1b_bases[b] + ((i + 1) * (sides[b] + 2) + 1) * 16
        pool[aligned(start, sides[b] * 16), :] = masked(half_silu(half(4, x2[rows, :])), b).astype(BF16)
        return carry
    each(hidden, 0)
    for b in buckets:
        fill_halo(h1b_bases[b], b, 1, 1, 1, 1)
        for h, lanes in enumerate(lane_halves):
            parts = [
                window(h1b_bases[b], sides[b] + 2, b, tap // 3, tap % 3, lanes) for tap in range(TAPS)
            ]
            x3[bases[b] : bases[b] + rows_of[b], lanes] = dot(
                jnp.concatenate(parts, axis=1), bd2[h].reshape(TAPS * HALF, HALF)
            )
    sums = all_sum(list(stats(x3)))
    set_norm(5, sums[0], sums[1], norms2, 1, live)
    squeeze_excite(x3, 5, down2, downb2, up2, upb2, se2, sq2)
    def keep_h2b(rows, value):
        pool[aligned(rows.start + h2b, rows.size), :] = value
    gate(x3, 5, se2, keep_h2b)
    x1[...] = dot(pool[h2b : h2b + total, :], w_out2[...])
    sums = all_sum(list(stats(x1)))
    set_norm(6, sums[0], sums[1], norms2, 2, live)
    fetch.wait()
    out_at = g2b_bases[0]
    def finish(b, rows, i, carry):
        u = x1[rows, :]
        y = half(6, u) + 0.5 * mid[rows, :].astype(F32)
        tan = jnp.tanh(y)
        pool[aligned(rows.start + out_at, rows.size), :] = masked(y + y * tan, b).astype(BF16)
        g = pool[aligned(rows.start + cot_at, rows.size), :].astype(F32) * half_silu_grad(y, tan)
        x2[rows, :] = g
        return carry[0] + fold(g), carry[1] + fold(g * (u - row(6, 0)))
    local = [down_to_row(v) for v in each(finish, (zero8, zero8))]
    put_out = pltpu.make_async_copy(pool.at[pl.ds(out_at, total)], out_hbm, sems.at[1])
    put_out.start()

    put_norm_grads(dnorms2, 2, 6, *local)
    set_grad(6, *all_sum(local), live)
    def third(b, rows, i, carry):
        pool[aligned(rows.start + g3b, rows.size), :] = grad_u(x2[rows, :], x1[rows, :], b)
        return carry
    each(third, 0)
    dw_out2[...] = dot_tn(pool[h2b : h2b + total, :], pool[g3b : g3b + total, :])
    x1[...] = dot_nt(pool[g3b : g3b + total, :], w_out2[...])
    local = squeeze_excite_back(x1, x3, 5, down2, up2, se2, sq2, ddown2, ddownb2, dup2, dupb2)
    put_norm_grads(dnorms2, 1, 5, *local)
    set_grad(5, *all_sum(list(local)), live)
    put_out.wait()
    def second(b, rows, i, carry):
        start = g2b_bases[b] + ((i + 1) * (sides[b] + 2) + 1) * 16
        pool[aligned(start, sides[b] * 16), :] = grad_u(x1[rows, :], x3[rows, :], b)
        return carry
    each(second, 0)
    for b in buckets:
        fill_halo(g2b_bases[b], b, 1, 1, 1, 1)
        for h, lanes in enumerate(lane_halves):
            parts = [
                window(g2b_bases[b], sides[b] + 2, b, 2 - tap // 3, 2 - tap % 3, lanes) for tap in range(TAPS)
            ]
            x1[bases[b] : bases[b] + rows_of[b], lanes] = dot_nt(
                jnp.concatenate(parts, axis=1),
                jnp.concatenate([bd2[h, tap] for tap in range(TAPS)], axis=1),
            )
    for h, lanes in enumerate(lane_halves):
        source = jnp.concatenate(
            [window(h1b_bases[b], sides[b] + 2, b, 1, 1, lanes) for b in buckets], axis=0
        )
        for tap in range(TAPS):
            target = jnp.concatenate(
                [window(g2b_bases[b], sides[b] + 2, b, 2 - tap // 3, 2 - tap % 3, lanes) for b in buckets],
                axis=0,
            )
            acc[tap, h] = diagonal(dot_tn(source, target))
    put_group2 = pltpu.make_async_copy(acc, dwg2_hbm, sems.at[2])
    put_group2.start()
    x3[...] = dot(mid[...], w_in2[...])
    def first(b, rows, i, carry):
        u = x3[rows, :]
        y = half(4, u)
        g = x1[rows, :] * half_silu_grad(y, jnp.tanh(y))
        x1[rows, :] = g
        return carry[0] + fold(g), carry[1] + fold(g * (u - row(4, 0)))
    local = [down_to_row(v) for v in each(first, (zero8, zero8))]
    put_norm_grads(dnorms2, 0, 4, *local)
    set_grad(4, *all_sum(local), live)
    def first_u(b, rows, i, carry):
        pool[aligned(rows.start + g3b, rows.size), :] = grad_u(x1[rows, :], x3[rows, :], b)
        return carry
    each(first_u, 0)
    dw_in2[...] = dot_tn(mid[...], pool[g3b : g3b + total, :])
    x2[...] = x2[...] + dot_nt(pool[g3b : g3b + total, :], w_in2[...])

    x3[...] = dot(h2[...], w_out1[...])
    x1[...] = dot(acts[0], w_short[...])
    def joined(b, rows, i, carry):
        u, s = x3[rows, :], x1[rows, :]
        y = half(2, u) + half(3, s)
        g = x2[rows, :] * half_silu_grad(y, jnp.tanh(y))
        x2[rows, :] = g
        return (
            carry[0] + fold(g),
            carry[1] + fold(g * (u - row(2, 0))),
            carry[2] + fold(g * (s - row(3, 0))),
        )
    local = [down_to_row(v) for v in each(joined, (zero8, zero8, zero8))]
    put_norm_grads(dnorms1, 2, 2, local[0], local[1])
    put_norm_grads(dnorms1, 3, 3, local[0], local[2])
    sums = all_sum(local)
    set_grad(2, sums[0], sums[1], live)
    set_grad(3, sums[0], sums[2], live, 51)
    def both(b, rows, i, carry):
        g = x2[rows, :]
        pool[rows, :] = grad_u(g, x3[rows, :], b)
        mid[rows, :] = grad_u(g, x1[rows, :], b, 51)
        return carry
    each(both, 0)
    put_short = pltpu.make_async_copy(mid, gs_hbm, sems.at[3])
    put_short.start()
    dw_short[...] = dot_tn(acts[0], mid[...])
    dw_out1[...] = dot_tn(h2[...], pool[0:total, :])
    x1[...] = dot_nt(pool[0:total, :], w_out1[...])
    local = squeeze_excite_back(x1, x0, 1, down1, up1, se1, sq1, ddown1, ddownb1, dup1, dupb1)
    put_norm_grads(dnorms1, 1, 1, *local)
    set_grad(1, *all_sum(list(local)), live)
    g2_bases, end = geo.grid(1, 1, 0)
    g1_at = end
    def second_one(b, rows, i, carry):
        start = g2_bases[b] + (i * (sides[b] + 1)) * 16
        pool[aligned(start, sides[b] * 16), :] = grad_u(x1[rows, :], x0[rows, :], b)
        return carry
    each(second_one, 0)
    for b in buckets:
        fill_halo(g2_bases[b], b, 0, 1, 0, 1)
    put_group2.wait()
    carry = (zero8, zero8)
    for plane, (pr, pc) in enumerate(planes):
        taps = [
            tap for tap in range(TAPS) if int(tap // 3 != 1) == pr and int(tap % 3 != 1) == pc
        ]
        for b in buckets:
            size = rows_of[b]
            x0[0:size, :] = dot(acts[plane, bases[b] : bases[b] + size, :], w_in1[...])
            for h, lanes in enumerate(lane_halves):
                parts = [
                    window(g2_bases[b], sides[b] + 1, b, int(tap // 3 == 0), int(tap % 3 == 0), lanes)
                    for tap in taps
                ]
                x1[0:size, lanes] = dot_nt(
                    jnp.concatenate(parts, axis=1), jnp.concatenate([bd1[h, tap] for tap in taps], axis=1)
                )
            def line(i, kept, b=b, plane=plane):
                rows = aligned(i * sides[b] * 16, sides[b] * 16)
                u = x0[rows, :]
                y = half(0, u)
                tan = jnp.tanh(y)
                h2[rows, :] = masked(y + y * tan, b).astype(BF16)
                g = x1[rows, :] * half_silu_grad(y, tan)
                start = g1_at + plane * total + bases[b] + i * sides[b] * 16
                pool[aligned(start, sides[b] * 16), :] = g.astype(BF16)
                return kept[0] + fold(g), kept[1] + fold(g * (u - row(0, 0)))
            carry = lax.fori_loop(0, sides[b], line, carry)
            for h, lanes in enumerate(lane_halves):
                source = h2[0:size, lanes]
                for tap in taps:
                    target = window(
                        g2_bases[b], sides[b] + 1, b, int(tap // 3 == 0), int(tap % 3 == 0), lanes
                    )
                    if b == 0:
                        acc[tap, h] = diagonal(dot_tn(source, target))
                    else:
                        acc[tap, h] += diagonal(dot_tn(source, target))
    put_group1 = pltpu.make_async_copy(acc, dwg1_hbm, sems.at[2])
    put_group1.start()
    local = [down_to_row(v) for v in carry]
    put_norm_grads(dnorms1, 0, 0, *local)
    set_grad(0, *all_sum(local), 4.0 * live)
    puts = []
    for plane in range(4):
        x0[...] = dot(acts[plane], w_in1[...])
        at = g1_at + plane * total
        def first_one(b, rows, i, carry, at=at):
            here = aligned(rows.start + at, rows.size)
            pool[here, :] = grad_u(pool[here, :].astype(F32), x0[rows, :], b)
            return carry
        each(first_one, 0)
        part = dot_tn(acts[plane], pool[at : at + total, :])
        if plane == 0:
            dw_in1[...] = part
        else:
            dw_in1[...] += part
        put = pltpu.make_async_copy(pool.at[pl.ds(at, total)], g1_hbm.at[plane], sems.at[4 + plane])
        put.start()
        puts.append(put)
    for put in puts:
        put.wait()
    put_short.wait()
    put_group1.wait()


def whole():
    return pl.BlockSpec(memory_space=pltpu.VMEM)


def anywhere():
    return pl.BlockSpec(memory_space=pl.ANY)


def shape(dims, dtype=F32):
    return jax.ShapeDtypeStruct(dims, dtype)


def blocks(geo, acts, mask, count, first, second, cot):
    groups, inner = lax.axis_size("dp"), lax.axis_size("fsdp")
    total = geo.total
    ins = [acts, mask, count, *first, *second, cot]
    hbm_outs = [
        shape((total, WIDTH), BF16), shape((4, total, WIDTH), BF16), shape((total, WIDTH), BF16),
        shape((TAPS, 2, HALF, 128)), shape((TAPS, 2, HALF, 128)),
    ]
    vmem_outs = []
    for is_first in (True, False):
        dims = shapes_of(is_first)
        vmem_outs.extend(shape(d) for j, d in enumerate(dims) if j != 1)
    pool_rows = 0
    for pr, pc in ((0, 0), (0, 1), (1, 0), (1, 1)):
        pool_rows = geo.grid(pr, pc, pool_rows)[1]
    pool_rows = max(
        pool_rows, geo.grid(2, 2, geo.grid(2, 2, 0)[1])[1] + 2 * total, geo.grid(1, 1, 0)[1] + 4 * total
    )
    stages = exchange_stages(groups, inner)
    big = pltpu.VMEM((total, WIDTH), F32)
    scratch = [
        pltpu.VMEM((pool_rows, WIDTH), BF16), big, big, big, big,
        pltpu.VMEM((total, WIDTH), BF16), pltpu.VMEM((total, WIDTH), BF16),
        pltpu.VMEM((TAPS, 2, HALF, 128), F32), pltpu.VMEM((104, WIDTH), F32),
        pltpu.VMEM((2, 48, WIDTH), F32), pltpu.VMEM((48, SQUEEZE_A), F32),
        pltpu.VMEM((2, 48, WIDTH), F32), pltpu.VMEM((48, SQUEEZE_B), F32),
        pltpu.VMEM((2 * len(stages), 24, 128), F32),
        pltpu.VMEM((2 * len(stages), max(stages) - 1, 24, 128), F32),
        pltpu.SemaphoreType.DMA((2 * len(stages),)), pltpu.SemaphoreType.DMA((2 * len(stages),)),
        pltpu.SemaphoreType.DMA((8,)),
    ]
    outs = pl.pallas_call(
        functools.partial(body, geo, groups, inner),
        out_shape=hbm_outs + vmem_outs,
        in_specs=[whole()] * 20 + [anywhere()],
        out_specs=[anywhere()] * 5 + [whole()] * len(vmem_outs),
        scratch_shapes=scratch,
        compiler_params=pltpu.CompilerParams(
            collective_id=0, has_side_effects=True, vmem_limit_bytes=LIMIT
        ),
    )(*ins)
    out, g1, gs, dwg1, dwg2 = outs[:5]
    first_grads = [outs[5], dwg1, *outs[6:13]]
    second_grads = [outs[13], dwg2, *outs[14:]]
    return out, g1, gs, first_grads, second_grads


class Flat:
    def __init__(self, is_first, full_length, devices):
        self.shapes = shapes_of(is_first)
        self.starts = []
        offset = 0
        for dims in self.shapes:
            self.starts.append(offset // 128)
            offset = offset + math.prod(dims)
        self.skew = offset % 128
        self.used = offset
        self.rows = full_length // 128
        self.share = self.rows // devices
        self.padded = -(-self.share // 16) * 16


def first_lanes(limit, dims):
    return lax.broadcasted_iota(jnp.int32, dims, 1) < limit


def column_pick(b):
    row = lax.broadcasted_iota(jnp.int32, (384, SQUEEZE_A), 0)
    column = lax.broadcasted_iota(jnp.int32, (384, SQUEEZE_A), 1)
    return (row == column + SQUEEZE_A * b).astype(F32)


def unskew(info, flat):
    row = info.starts[4]
    while row < info.rows:
        size = min(256, info.rows - row)
        here = pltpu.roll(flat[row : row + size, :], 128 - info.skew, 1)
        after = pltpu.roll(flat[row + 1 : row + size + 1, :], 128 - info.skew, 1)
        flat[row : row + size, :] = jnp.where(first_lanes(128 - info.skew, (size, 128)), here, after)
        row = row + size


def reskew(info, flat):
    row = info.rows
    first = info.starts[4]
    while row > first:
        size = min(256, row - first)
        start = row - size
        here = pltpu.roll(flat[start:row, :], info.skew, 1)
        if start == first:
            ahead = pltpu.roll(flat[start : row, :], info.skew, 1)
            ahead = pltpu.roll(ahead, 1, 0)
            keep = flat[info.rows + 8 : info.rows + 9, :]
            is_top = lax.broadcasted_iota(jnp.int32, (size, 128), 0) == 0
            ahead = jnp.where(is_top, jnp.broadcast_to(keep, (size, 128)), ahead)
        else:
            ahead = pltpu.roll(flat[start - 1 : row - 1, :], info.skew, 1)
        flat[start:row, :] = jnp.where(first_lanes(info.skew, (size, 128)), ahead, here)
        row = start


def unpack(info, flat, block_pad, outs):
    def wide(out, start):
        rows = out.shape[0]
        for c in range(4):
            out[:, c * 128 : (c + 1) * 128] = flat[pl.ds(start + c, rows, stride=4), :].astype(out.dtype)

    starts = info.starts
    w_in, bd, down, downb, up, upb, w_out = outs[:7]
    wide(w_in, starts[0])
    row = lax.broadcasted_iota(jnp.int32, (128, HALF), 0) // 32
    lane = lax.broadcasted_iota(jnp.int32, (128, HALF), 1) // GROUP_WIDTH
    on_diagonal = (row == lane).astype(F32)

    def spread(index, carry):
        rows = flat[pl.ds(pl.multiple_of(starts[1] + index * 128, 8), 128), :]
        turned = pltpu.roll(rows, GROUP_WIDTH, 1)
        left = first_lanes(GROUP_WIDTH, (128, 128))
        for parity, pair in enumerate((jnp.where(left, rows, turned), jnp.where(left, turned, rows))):
            tiled = jnp.concatenate([pair, pair], axis=1) * on_diagonal
            block_pad[pl.ds(parity, 128, stride=2), :] = tiled[:, :128]
            block_pad[pl.ds(HALF + parity, 128, stride=2), :] = tiled[:, 128:]
        bd[index % 2, index // 2, :, 0:128] = block_pad[0:HALF, :].astype(BF16)
        bd[index % 2, index // 2, :, 128:HALF] = block_pad[HALF : 2 * HALF, :].astype(BF16)
        return carry

    lax.fori_loop(0, 2 * TAPS, spread, 0)
    if down.shape[1] == 128:
        down[...] = flat[starts[2] : starts[2] + WIDTH, :]
    else:
        joined = jnp.concatenate([flat[pl.ds(starts[2] + q, 64, stride=3), :] for q in range(3)], axis=1)
        for b in range(8):
            block_pad[pl.ds(b, 64, stride=8), 0:SQUEEZE_A] = dot(joined, column_pick(b))
        down[...] = block_pad[:, 0:SQUEEZE_A]
    downb[...] = flat[starts[3] : starts[3] + 1, 0 : downb.shape[1]]
    if info.skew:
        unskew(info, flat)
    wide(up, starts[4])
    upb[...] = jnp.concatenate([flat[starts[5] + c : starts[5] + c + 1, :] for c in range(4)], axis=1)
    wide(w_out, starts[6])
    if len(outs) == 9:
        wide(outs[7], starts[7])
    wide(outs[-1], starts[-1])


def pack(info, flat, grads):
    def wide(value, start):
        rows = value.shape[0]
        for c in range(4):
            flat[pl.ds(start + c, rows, stride=4), :] = value[:, c * 128 : (c + 1) * 128]

    starts = info.starts
    d_in, dwg, ddown, ddownb, dup, dupb, d_out = grads[:7]
    flat[info.used // 128 // 8 * 8 : info.rows, :] = jnp.zeros_like(flat[info.used // 128 // 8 * 8 : info.rows, :])
    wide(d_in, starts[0])
    group_odd = lax.broadcasted_iota(jnp.int32, (128, 128), 0) // 32 % 2 == 1
    left = first_lanes(GROUP_WIDTH, (128, 128))

    def collect(index, carry):
        even = dwg[index // 2, index % 2, pl.ds(0, 128, stride=2), :]
        odd = dwg[index // 2, index % 2, pl.ds(1, 128, stride=2), :]
        even_turned, odd_turned = pltpu.roll(even, GROUP_WIDTH, 1), pltpu.roll(odd, GROUP_WIDTH, 1)
        rows = jnp.where(
            group_odd, jnp.where(left, even_turned, odd), jnp.where(left, even, odd_turned)
        )
        flat[pl.ds(pl.multiple_of(starts[1] + index * 128, 8), 128), :] = rows
        return carry

    lax.fori_loop(0, 2 * TAPS, collect, 0)
    if ddown.shape[1] == 128:
        flat[starts[2] : starts[2] + WIDTH, :] = ddown[...]
    else:
        joined = sum(
            exact(ddown[pl.ds(b, 64, stride=8), :], column_pick(b), ((1,), (1,))) for b in range(8)
        )
        for q in range(3):
            flat[pl.ds(starts[2] + q, 64, stride=3), :] = joined[:, q * 128 : (q + 1) * 128]
    wide(dup, starts[4])
    for c in range(4):
        flat[starts[5] + c : starts[5] + c + 1, :] = dupb[:, c * 128 : (c + 1) * 128]
    wide(d_out, starts[6])
    if len(grads) == 9:
        wide(grads[7], starts[7])
    wide(grads[-1], starts[-1])
    if info.skew:
        flat[info.rows + 8 : info.rows + 9, 0 : ddownb.shape[1]] = ddownb[...]
        reskew(info, flat)
    else:
        flat[starts[3] : starts[3] + 1, :] = ddownb[...]


class Places:
    def __init__(self, groups, inner):
        self.outer, self.inner = lax.axis_index("dp"), lax.axis_index("fsdp")
        self.chips, self.lines = groups // 2, inner
        self.chip, self.core = self.outer // 2, lax.rem(self.outer, 2)

    def along(self, step):
        return lax.rem(self.inner + step, self.lines)

    def across(self, step):
        return lax.rem(self.chip + step, self.chips)

    def line(self, step):
        return (self.outer, self.along(step))

    def other_chip(self, step):
        return (2 * self.across(step) + self.core, self.inner)

    def sibling(self):
        return (2 * self.chip + 1 - self.core, self.inner)

    def greet(self, barrier):
        for step in range(1, self.lines):
            pl.semaphore_signal(barrier, inc=1, device_id=self.line(step), device_id_type=MESH)
        for step in range(1, self.chips):
            pl.semaphore_signal(barrier, inc=1, device_id=self.other_chip(step), device_id_type=MESH)
        pl.semaphore_signal(barrier, inc=1, device_id=self.sibling(), device_id_type=MESH)

    def greeted(self, barrier):
        pl.semaphore_wait(barrier, self.lines + self.chips - 1)


def remote(source, target, send_sem, recv_sem, device):
    return pltpu.make_async_remote_copy(
        src_ref=source, dst_ref=target, send_sem=send_sem, recv_sem=recv_sem, device_id=device, device_id_type=MESH
    )


def gather_body(geo, infos, groups, inner, *refs):
    images, cots, mask = refs[0:3], refs[3:6], refs[6]
    shards = refs[7:9]
    acts, cot = refs[9:11]
    weights = [refs[11:20], refs[20:28]]
    scratch = refs[28:]
    wide_cell, cot_cell, block_pad = scratch[0:3]
    gathered, flats = scratch[3:5], scratch[5:7]
    own_sem, line_send, line_recv, chip_send, chip_recv, core_send, core_recv = scratch[7:]
    places = Places(groups, inner)
    barrier = pltpu.get_barrier_semaphore()
    places.greet(barrier)
    mine = [buf.at[places.chip, places.core, places.inner] for buf in gathered]
    own = [pltpu.make_async_copy(shards[k], mine[k], own_sem.at[k]) for k in range(2)]
    for copy in own:
        copy.start()
    places.greeted(barrier)
    started = []

    def begin(copy):
        copy.start()
        started.append(copy)
        return copy

    lines = [
        [begin(remote(shards[k], mine[k], line_send.at[k, step - 1], line_recv.at[k, step - 1], places.line(step))) for step in range(1, inner)]
        for k in range(2)
    ]
    chip_copies = [[], []]

    def forward(k):
        own[k].wait()
        for copy in lines[k]:
            copy.wait_recv()
        line = gathered[k].at[places.chip, places.core]
        for step in range(1, places.chips):
            chip_copies[k].append(
                begin(remote(line, line, chip_send.at[k, step - 1], chip_recv.at[k, step - 1], places.other_chip(step)))
            )
        begin(remote(line, line, core_send.at[k, 0], core_recv.at[k], places.sibling()))

    def pass_on(k):
        for step in range(1, places.chips):
            chip_copies[k][step - 1].wait_recv()
            line = gathered[k].at[places.across(places.chips - step), places.core]
            begin(remote(line, line, core_send.at[k, step], core_recv.at[k], places.sibling()))

    def complete(k):
        half = gathered[k].at[:, 0]
        pltpu.make_async_copy(half, half, core_recv.at[k]).wait()
        info = infos[k]
        for d in range(groups * inner):
            at = info.share * d
            piece = gathered[k][d // inner // 2, d // inner % 2, d % inner, 0 : info.share, :]
            flats[k][at : at + info.share, :] = piece.astype(F32)
        unpack(info, flats[k], block_pad, weights[k])

    def arrange(b):
        side = geo.sides[b]
        size = side * 16

        def line(i, carry):
            rows = aligned(geo.bases[b] + i * size, size)
            for pr in range(2):
                for pc in range(2):
                    for q in range(4):
                        wide_cell[0:side, 4 * q : 4 * q + 4, :] = images[b][q // 2, i, pr, q % 2, :, pc].astype(F32)
                    value = wide_cell[0:side] * mask[b][None, :, :WIDTH_IN]
                    acts[2 * pr + pc, rows, :] = value.reshape(size, WIDTH_IN).astype(BF16)
            for q in range(4):
                cot_cell[0:side, 4 * q : 4 * q + 4, :] = cots[b][q // 2, i, q % 2].astype(F32)
            value = cot_cell[0:side] * mask[b][None]
            cot[rows, :] = value.reshape(size, WIDTH).astype(BF16)
            return carry

        lax.fori_loop(0, side, line, 0)

    arrange(0)
    forward(0)
    arrange(1)
    forward(1)
    pass_on(0)
    arrange(2)
    pass_on(1)
    complete(0)
    complete(1)
    for copy in started:
        copy.wait_send()


def gather(geo, infos, images, cots, mask, shards):
    groups, inner = lax.axis_size("dp"), lax.axis_size("fsdp")
    padded = [
        jnp.pad(shard.astype(BF16).reshape(-1, 128), ((0, info.padded - info.share), (0, 0)))
        for shard, info in zip(shards, infos)
    ]
    ins = [*images, *cots, mask, *padded]
    outs = [shape((4, geo.total, WIDTH_IN), BF16), shape((geo.total, WIDTH), BF16)]
    for is_first in (True, False):
        dims = shapes_of(is_first)
        outs += [shape(dims[0], BF16), shape((2, TAPS, HALF, HALF), BF16)]
        outs += [shape(d) for d in dims[2:6]] + [shape(d, BF16) for d in dims[6:-1]] + [shape(dims[-1])]
    side = max(geo.sides)
    scratch = [
        pltpu.VMEM((side, 16, WIDTH_IN), F32), pltpu.VMEM((side, 16, WIDTH), F32), pltpu.VMEM((2 * HALF, 128), F32),
    ]
    scratch += [pltpu.VMEM((groups // 2, 2, inner, info.padded, 128), BF16) for info in infos]
    scratch += [pltpu.VMEM((info.rows + 16, 128), F32) for info in infos]
    chips = groups // 2
    scratch += [
        pltpu.SemaphoreType.DMA(dims)
        for dims in ((2,), (2, inner - 1), (2, inner - 1), (2, chips - 1), (2, chips - 1), (2, chips), (2,))
    ]
    results = pl.pallas_call(
        functools.partial(gather_body, geo, infos, groups, inner),
        out_shape=outs,
        in_specs=[whole()] * len(ins),
        out_specs=[whole()] * len(outs),
        scratch_shapes=scratch,
        compiler_params=pltpu.CompilerParams(
            collective_id=1, has_side_effects=True, vmem_limit_bytes=LIMIT
        ),
    )(*ins)
    return results[0], results[1], results[2:11], results[11:]


def scatter_body(infos, groups, inner, *refs):
    grads = [refs[0:9], refs[9:17]]
    outs = refs[17:19]
    flat, parts, core_in, chip_sum, chip_in, line_sum, line_in = refs[19:26]
    core_send, core_recv, chip_send, chip_recv, line_send, line_recv = refs[26:]
    places = Places(groups, inner)
    barrier = pltpu.get_barrier_semaphore()
    places.greet(barrier)
    devices = groups * inner
    offsets = [0, infos[0].padded]
    for k, info in enumerate(infos):
        pack(info, flat, grads[k])
        for d in range(devices):
            place = parts.at[d // inner % 2, d // inner // 2, d % inner]
            place[offsets[k] : offsets[k] + info.share, :] = flat[info.share * d : info.share * (d + 1), :].astype(BF16)
            if info.share < info.padded:
                gap = info.padded - info.share
                place[offsets[k] + info.share : offsets[k] + info.padded, :] = jnp.zeros((gap, 128), BF16)
    places.greeted(barrier)
    core = remote(parts.at[1 - places.core], core_in, core_send, core_recv, places.sibling())
    core.start()
    core.wait_recv()

    def add(index, carry):
        chip, z = index // inner, index % inner
        chip_sum[chip, z] = (parts[places.core, chip, z].astype(F32) + core_in[chip, z].astype(F32)).astype(BF16)
        return carry

    lax.fori_loop(0, places.chips * inner, add, 0)
    copies = []
    for step in range(1, places.chips):
        copies.append(
            remote(chip_sum.at[places.across(step)], chip_in.at[step - 1], chip_send.at[step - 1], chip_recv.at[step - 1], places.other_chip(step))
        )
        copies[-1].start()
    for copy in copies:
        copy.wait_recv()

    def add_chips(z, carry):
        value = chip_sum[places.chip, z].astype(F32)
        for step in range(places.chips - 1):
            value = value + chip_in[step, z].astype(F32)
        line_sum[z] = value.astype(BF16)
        return carry

    lax.fori_loop(0, inner, add_chips, 0)
    lines = []
    for step in range(1, inner):
        lines.append(
            remote(line_sum.at[places.along(step)], line_in.at[step - 1], line_send.at[step - 1], line_recv.at[step - 1], places.line(step))
        )
        lines[-1].start()
    for copy in lines:
        copy.wait_recv()
    value = line_sum[places.inner].astype(F32)
    for step in range(inner - 1):
        value = value + line_in[step].astype(F32)
    for k, info in enumerate(infos):
        outs[k][...] = value[offsets[k] : offsets[k] + info.share, :]
    core.wait_send()
    for copy in copies + lines:
        copy.wait_send()


def scatter(infos, first_grads, second_grads):
    groups, inner = lax.axis_size("dp"), lax.axis_size("fsdp")
    ins = [*first_grads, *second_grads]
    chips = groups // 2
    size = sum(info.padded for info in infos)
    def part(*lead):
        return pltpu.VMEM((*lead, size, 128), BF16)
    outs = pl.pallas_call(
        functools.partial(scatter_body, infos, groups, inner),
        out_shape=[shape((info.share, 128)) for info in infos],
        in_specs=[whole()] * len(ins),
        out_specs=[whole()] * 2,
        scratch_shapes=[
            pltpu.VMEM((max(info.rows for info in infos) + 16, 128), F32),
            part(2, chips, inner), part(chips, inner), part(chips, inner), part(chips - 1, inner), part(inner),
            part(inner - 1),
        ]
        + [pltpu.SemaphoreType.DMA(dims) for dims in ((), (), (chips - 1,), (chips - 1,), (inner - 1,), (inner - 1,))],
        compiler_params=pltpu.CompilerParams(
            collective_id=2, has_side_effects=True, vmem_limit_bytes=LIMIT
        ),
    )(*ins)
    return [out.reshape(-1) for out in outs]


def restore_body(geo, *refs):
    g1, gs, out, w_in, w_short = refs[0:5]
    outputs, image_grads = refs[5:8], refs[8:11]
    grad_cell, out_cell = refs[11:]
    for b, side in enumerate(geo.sides):
        def line(i, carry, b=b, side=side):
            size = side * 16
            rows = aligned(geo.bases[b] + i * size, size)
            out_cell[0:side] = out[rows, :].astype(F32).reshape(side, 16, WIDTH)
            for q in range(4):
                outputs[b][q // 2, i, q % 2] = out_cell[0:side, 4 * q : 4 * q + 4, :].astype(BF16)
            for plane in range(4):
                value = dot_nt(g1[plane, rows, :], w_in[...])
                if plane == 0:
                    value = value + dot_nt(gs[rows, :], w_short[...])
                grad_cell[plane, 0:side] = value.reshape(side, 16, WIDTH_IN)
                for q in range(4):
                    image_grads[b][q // 2, i, plane // 2, q % 2, :, plane % 2] = grad_cell[
                        plane, 0:side, 4 * q : 4 * q + 4, :
                    ]
            return carry
        lax.fori_loop(0, side, line, 0)


def restore(geo, g1, gs, out, w_in, w_short):
    ins = [g1, gs, out, w_in, w_short]
    outs = [shape((2, side, 2, side, 4, WIDTH), BF16) for side in geo.sides]
    outs = outs + [shape((2, side, 2, 2, side, 2, 4, WIDTH_IN)) for side in geo.sides]
    side = max(geo.sides)
    results = pl.pallas_call(
        functools.partial(restore_body, geo),
        out_shape=outs,
        in_specs=[whole()] * len(ins),
        out_specs=[whole()] * len(outs),
        scratch_shapes=[pltpu.VMEM((4, side, 16, WIDTH_IN), F32), pltpu.VMEM((side, 16, WIDTH), F32)],
        compiler_params=pltpu.CompilerParams(vmem_limit_bytes=LIMIT),
    )(*ins)
    whole_grids = [
        result.reshape(scale * side, scale * side, 4, -1)
        for result, side, scale in zip(results, geo.sides * 2, [2] * 3 + [4] * 3)
    ]
    return [grid.transpose(2, 0, 1, 3) for grid in whole_grids]


def per_device(*args):
    images, counts = args[0:3], args[3]
    cots = args[6:9]
    geo = Geometry([image.shape[1] // 4 for image in images])
    devices = lax.axis_size("dp") * lax.axis_size("fsdp")
    infos = [Flat(k == 0, args[4 + k].shape[0] * devices, devices) for k in range(2)]
    slot = jnp.arange(16, dtype=jnp.int32) % 4
    mask = (slot[None, :, None] < counts[0][:, None, None]).astype(F32)
    mask = jnp.broadcast_to(mask, (3, 16, WIDTH))
    pixels = jnp.asarray([4 * side * side for side in geo.sides], jnp.int32)
    count = jnp.full((8, 128), 1.0, F32) * jnp.sum(counts[0] * pixels).astype(F32)
    split_images = [
        image.transpose(1, 2, 0, 3).reshape(2, side, 2, 2, side, 2, 4, WIDTH_IN)
        for image, side in zip(images, geo.sides)
    ]
    split_cots = [
        value.transpose(1, 2, 0, 3).reshape(2, side, 2, side, 4, WIDTH) for value, side in zip(cots, geo.sides)
    ]
    acts, cot, first, second = gather(geo, infos, split_images, split_cots, mask, args[4:6])
    out, g1, gs, first_grads, second_grads = blocks(geo, acts, mask, count, first, second, cot)
    results = restore(geo, g1, gs, out, first[0], first[7])
    return (*results, *scatter(infos, first_grads, second_grads))


def solution(mesh):
    images = P(("dp", "fsdp"), None, None, None)
    flat = P(("dp", "fsdp"))
    in_specs = (images, images, images, P(("dp", "fsdp"), None), flat, flat, images, images, images)
    out_specs = (images,) * 6 + (flat, flat)
    return jax.shard_map(per_device, mesh=mesh, in_specs=in_specs, out_specs=out_specs, check_vma=False)
```

```python
import functools
import math

import jax
import jax.numpy as jnp
from jax import lax
from jax.experimental import pallas as pl
from jax.experimental.pallas import tpu as pltpu
from jax.sharding import PartitionSpec as P

WIDTH_IN = 192
GROUPS = 8
GROUP_WIDTH = 64
SQUEEZE_A = 48
SQUEEZE_B = 128
WIDTH = 512
HALF = 256
TAPS = 9
EPSILON = 1e-05
HIGHEST = lax.Precision.HIGHEST
MESH = pl.DeviceIdType.MESH
F32 = jnp.float32
BF16 = jnp.bfloat16
LIMIT = 63 * 2**20


def shapes_of(is_first):
    width_in, squeeze = (WIDTH_IN, SQUEEZE_A) if is_first else (WIDTH, SQUEEZE_B)
    shapes = [
        (width_in, WIDTH),
        (TAPS, GROUPS, GROUP_WIDTH, GROUP_WIDTH),
        (WIDTH, squeeze),
        (1, squeeze),
        (squeeze, WIDTH),
        (1, WIDTH),
        (WIDTH, WIDTH),
    ]
    if is_first:
        shapes.append((WIDTH_IN, WIDTH))
    shapes.append((8 if is_first else 6, WIDTH))
    return shapes


def diagonal(product):
    parts = []
    for g in range(4):
        lanes = slice(128 * (g // 2), 128 * (g // 2) + 128)
        parts.append(product[g * GROUP_WIDTH : (g + 1) * GROUP_WIDTH, lanes])
    return jnp.concatenate(parts, axis=0)


def dot(left, right):
    return jnp.dot(left, right, preferred_element_type=F32)


def dot_nt(left, right):
    return lax.dot_general(left, right, (((1,), (1,)), ((), ())), preferred_element_type=F32)


def dot_tn(left, right):
    return lax.dot_general(left, right, (((0,), (0,)), ((), ())), preferred_element_type=F32)


def exact(left, right, dims):
    return lax.dot_general(
        left, right, (dims, ((), ())), precision=HIGHEST, preferred_element_type=F32
    )


def by_parts(product, left, right):
    high = left.astype(BF16)
    rest = left - high.astype(F32)
    middle = rest.astype(BF16)
    low = (rest - middle.astype(F32)).astype(BF16)
    rows = left.shape[0]
    full = product(jnp.concatenate([high, middle, low], axis=0), right)
    return full[:rows] + full[rows : 2 * rows] + full[2 * rows :]


def half_silu(half):
    return half + half * jnp.tanh(half)


def half_silu_grad(half, tan):
    return (0.5 + 0.5 * tan) * (1.0 + half * (1.0 - tan))


def fold(values):
    return jnp.sum(values.reshape(-1, 8, WIDTH), axis=0)


def down_to_row(values):
    return jnp.sum(values, axis=0, keepdims=True)


class Geometry:
    def __init__(self, sides):
        self.sides = sides
        self.rows = [side * side * 16 for side in sides]
        self.bases = [sum(self.rows[:b]) for b in range(len(sides))]
        self.total = sum(self.rows)

    def grid(self, extra_rows, extra_cols, start):
        bases = []
        for side in self.sides:
            bases.append(start)
            start = start + (side + extra_rows) * (side + extra_cols) * 16
        return bases, start


def exchange_stages(groups, inner):
    return [groups * inner] if groups * inner <= 64 else [inner, groups]


def aligned(start, size):
    return pl.ds(pl.multiple_of(start, 16), size)


def body(geo, groups, inner, *refs):
    (
        acts, mask, count,
        w_in1, bd1, down1, downb1, up1, upb1, w_out1, w_short, norms1,
        w_in2, bd2, down2, downb2, up2, upb2, w_out2, norms2,
        cot_hbm,
    ) = refs[:21]
    out_hbm, g1_hbm, gs_hbm = refs[21:24], refs[24:27], refs[27:30]
    (
        dwg1_hbm, dwg2_hbm,
        dw_in1, ddown1, ddownb1, dup1, dupb1, dw_out1, dw_short, dnorms1,
        dw_in2, ddown2, ddownb2, dup2, dupb2, dw_out2, dnorms2,
        pool, x0, x1, x2, x3, h2, mid, acc, vec, se1, sq1, se2, sq2,
        pay, slots, send_sem, recv_sem, sems,
    ) = refs[30:]
    sides, bases, rows_of, total = geo.sides, geo.bases, geo.rows, geo.total
    buckets = range(len(sides))
    devices = groups * inner

    outer_index, inner_index = lax.axis_index("dp"), lax.axis_index("fsdp")

    def any_partner(step):
        other = lax.rem(outer_index * inner + inner_index + step, devices)
        return (other // inner, lax.rem(other, inner))

    def inner_partner(step):
        return (outer_index, lax.rem(inner_index + step, inner))

    def outer_partner(step):
        return (lax.rem(outer_index + step, groups), inner_index)

    barrier = pltpu.get_barrier_semaphore()
    stages = exchange_stages(groups, inner)
    if len(stages) == 1:
        partners = [any_partner]
    else:
        partners = [inner_partner, outer_partner]
    for count_in_stage, partner in zip(stages, partners):

        def greet(step, carry, partner=partner):
            pl.semaphore_signal(barrier, inc=1, device_id=partner(step), device_id_type=MESH)
            return carry

        lax.fori_loop(1, count_in_stage, greet, 0)

    calls = []

    def put_rows(at, sums):
        for c in range(4):
            for r, row in enumerate(sums):
                pay[at, 4 * r + c : 4 * r + c + 1, :] = row[:, c * 128 : (c + 1) * 128]

    def send_stage(stage, at):
        def send(step, carry):
            pltpu.make_async_remote_copy(
                src_ref=pay.at[at],
                dst_ref=slots.at[at, step - 1],
                send_sem=send_sem.at[at],
                recv_sem=recv_sem.at[at],
                device_id=partners[stage](step),
                device_id_type=MESH,
            ).start()
            return carry

        lax.fori_loop(1, stages[stage], send, 0)

    def land_stage(stage, at):
        landed = slots.at[at, pl.ds(0, stages[stage] - 1)]
        pltpu.make_async_copy(landed, landed, recv_sem.at[at]).wait()
        sums = pay[at] + jnp.sum(slots[at, 0 : stages[stage] - 1], axis=0)
        pltpu.make_async_copy(landed, landed, send_sem.at[at]).wait()
        return sums

    def begin_sum(rows, place=None):
        if not calls:
            pl.semaphore_wait(barrier, sum(stages) - len(stages))
        if place is None:
            place = sum(p < 2 for p in calls) % 2
        calls.append(place)
        put_rows(place * len(stages), rows)
        send_stage(0, place * len(stages))
        return place, len(rows)

    def finish_sum(begun):
        place, number = begun
        for stage in range(len(stages)):
            at = place * len(stages) + stage
            if stage:
                pay[at] = sums
                send_stage(stage, at)
            sums = land_stage(stage, at)
        return [
            jnp.concatenate([sums[4 * r + c : 4 * r + c + 1, :] for c in range(4)], axis=1) for r in range(number)
        ]

    def all_sum(rows):
        return finish_sum(begin_sum(rows))

    def each(step, carry):
        for b in buckets:
            def line(i, kept, b=b):
                size = sides[b] * 16
                return step(b, aligned(bases[b] + i * size, size), i, kept)
            carry = lax.fori_loop(0, sides[b], line, carry)
        return carry

    zero8 = jnp.zeros((8, WIDTH), F32)

    def masked(values, b):
        return (values.reshape(-1, 16, WIDTH) * mask[b][None]).reshape(values.shape)

    def set_norm(k, sums, squares, norms, index, live):
        mean = sums / live
        inv_std = lax.rsqrt(squares / live - mean * mean + EPSILON)
        scale = inv_std * norms[2 * index : 2 * index + 1, :]
        offset = norms[2 * index + 1 : 2 * index + 2, :] - mean * scale
        for r, row in enumerate((mean, inv_std, scale, offset, 0.5 * scale, 0.5 * offset)):
            vec[6 * k + r : 6 * k + r + 1, :] = row

    def row(k, r):
        return vec[6 * k + r : 6 * k + r + 1, :]

    def half(k, u):
        return u * row(k, 4) + row(k, 5)

    def set_grad(k, sum_g, sum_d, live, at=48):
        scale, inv_std = row(k, 2), row(k, 1)
        on_u = -scale * inv_std * inv_std * sum_d / live
        vec[at : at + 1, :] = scale
        vec[at + 1 : at + 2, :] = on_u
        vec[at + 2 : at + 3, :] = -scale * sum_g / live - row(k, 0) * on_u

    def grad_u(g, u, b, at=48):
        inner_grad = g * vec[at : at + 1, :] + (u * vec[at + 1 : at + 2, :] + vec[at + 2 : at + 3, :])
        return masked(inner_grad, b).astype(BF16)

    def stats(x):
        def step(b, rows, i, carry):
            u = x[rows, :]
            return carry[0] + fold(u), carry[1] + fold(u * u)
        sums, squares = each(step, (zero8, zero8))
        return down_to_row(sums), down_to_row(squares)

    def window(base, width, b, r0, c0, lanes):
        side = sides[b]
        return jnp.concatenate(
            [
                pool[base + ((r0 + i) * width + c0) * 16 : base + ((r0 + i) * width + c0 + side) * 16, lanes]
                for i in range(side)
            ],
            axis=0,
        )

    lane_halves = [slice(0, HALF), slice(HALF, WIDTH)]

    def pattern(size, bit, value):
        index = lax.broadcasted_iota(jnp.int32, (size, WIDTH), 0)
        return ((index // bit) % 2 == value).astype(F32)

    def fill_halo(base, b, low_r, high_r, low_c, high_c):
        side = sides[b]
        width = side + low_c + high_c
        def cell(r, c, n=1):
            return slice(base + (r * width + c) * 16, base + (r * width + c + n) * 16)
        for i in range(side):
            r = i + low_r
            if low_c:
                value = pool[cell(r, side), :].astype(F32)
                pool[cell(r, 0), :] = (pltpu.roll(value, 4, 0) * pattern(16, 4, 1)).astype(BF16)
            if high_c:
                value = pool[cell(r, low_c), :].astype(F32)
                pool[cell(r, width - 1), :] = (pltpu.roll(value, 12, 0) * pattern(16, 4, 0)).astype(BF16)
        size = width * 16
        if low_r:
            value = pool[cell(side, 0, width), :].astype(F32)
            pool[cell(0, 0, width), :] = (pltpu.roll(value, 8, 0) * pattern(size, 8, 1)).astype(BF16)
        if high_r:
            value = pool[cell(low_r, 0, width), :].astype(F32)
            pool[cell(low_r + side, 0, width), :] = (
                pltpu.roll(value, size - 8, 0) * pattern(size, 8, 0)
            ).astype(BF16)

    first_of_image = (lax.broadcasted_iota(jnp.int32, (48, WIDTH), 0) % 16 < 4).astype(F32)

    def over_quadrants(v):
        return v + pltpu.roll(v, 4, 0) + pltpu.roll(v, 8, 0) + pltpu.roll(v, 12, 0)

    def squeeze_excite(x, k, down, downb, up, upb, se, sq):
        def step(b, rows, i, carry):
            v = half_silu(half(k, x[rows, :])).reshape(-1, 16, WIDTH)
            return tuple(c + jnp.sum(v, axis=0) if d == b else c for d, c in enumerate(carry))
        zero16 = jnp.zeros((16, WIDTH), F32)
        sums = each(step, tuple(zero16 for _ in buckets))
        pooled = jnp.concatenate(
            [over_quadrants(s) * (1.0 / (4 * side * side)) for s, side in zip(sums, sides)], axis=0
        )
        squeeze_pre = by_parts(dot, pooled, down[...]) + downb[...]
        squeezed = squeeze_pre * jax.nn.sigmoid(squeeze_pre)
        excite = jax.nn.sigmoid(by_parts(dot, squeezed, up[...]) + upb[...])
        se[0] = pooled
        sq[...] = squeeze_pre
        for b in buckets:
            se[1, 16 * b : 16 * b + 16, :] = excite[16 * b : 16 * b + 16, :] * mask[b]

    def gate(x, k, se, store):
        def step(b, rows, i, carry):
            v = half_silu(half(k, x[rows, :])).reshape(-1, 16, WIDTH)
            v = v * se[1, 16 * b : 16 * b + 16, :][None]
            store(rows, v.reshape(-1, WIDTH).astype(BF16))
            return carry
        each(step, 0)

    def squeeze_excite_back(g, u, k, down, up, se, sq, ddown, ddownb, dup, dupb):
        def step(b, rows, i, carry):
            v = half_silu(half(k, u[rows, :])) * g[rows, :]
            return tuple(
                c + jnp.sum(v.reshape(-1, 16, WIDTH), axis=0) if d == b else c
                for d, c in enumerate(carry)
            )
        zero16 = jnp.zeros((16, WIDTH), F32)
        sums = each(step, tuple(zero16 for _ in buckets))
        grad_excite = jnp.concatenate([over_quadrants(s) for s in sums], axis=0)
        excite = se[1]
        grad_up = grad_excite * excite * (1.0 - excite)
        squeeze_pre = sq[...]
        sig = jax.nn.sigmoid(squeeze_pre)
        once = first_of_image
        dup[...] = exact(squeeze_pre * sig, grad_up * once, ((0,), (0,)))
        dupb[...] = down_to_row(grad_up * once)
        grad_pre = by_parts(dot_nt, grad_up, up[...]) * (sig * (1.0 + squeeze_pre * (1.0 - sig)))
        ddown[...] = exact(se[0] * once, grad_pre, ((0,), (0,)))
        ddownb[...] = down_to_row(grad_pre * once[:, : grad_pre.shape[1]])
        pooled_grad = by_parts(dot_nt, grad_pre, down[...])
        for b in buckets:
            pixels = 4 * sides[b] * sides[b]
            vec[56 + 16 * b : 72 + 16 * b, :] = pooled_grad[16 * b : 16 * b + 16, :] * (1.0 / pixels)

        def apply(b, rows, i, carry):
            u_now = u[rows, :]
            y = half(k, u_now)
            slope = half_silu_grad(y, jnp.tanh(y))
            gv = g[rows, :].reshape(-1, 16, WIDTH) * se[1, 16 * b : 16 * b + 16, :][None]
            gv = (gv + vec[56 + 16 * b : 72 + 16 * b, :][None]).reshape(-1, WIDTH) * slope
            g[rows, :] = gv
            return carry[0] + fold(gv), carry[1] + fold(gv * (u_now - row(k, 0)))

        sum_g, sum_d = each(apply, (zero8, zero8))
        return down_to_row(sum_g), down_to_row(sum_d)

    def put_norm_grads(out, index, k, sum_g, sum_d):
        out[2 * index : 2 * index + 1, :] = row(k, 1) * sum_d
        out[2 * index + 1 : 2 * index + 2, :] = sum_g

    planes = [(0, 0), (0, 1), (1, 0), (1, 1)]

    chunk = total // 5
    wide = [x0, x1, x2, x3]

    def stat_dot(plane, weight, out, carry):
        def step(i, kept):
            rows = aligned(i * chunk, chunk)
            u = dot(acts[plane, rows, :], weight[...])
            if out is not None:
                out[rows, :] = u
            return kept[0] + fold(u), kept[1] + fold(u * u)
        return lax.fori_loop(0, 5, step, carry)

    carry = (zero8, zero8)
    for plane in range(4):
        carry = stat_dot(plane, w_in1, wide[plane], carry)
    one = begin_sum([down_to_row(v) for v in carry])
    short = begin_sum([down_to_row(v) for v in stat_dot(0, w_short, None, (zero8, zero8))], 2)
    live = count[...]
    vec[54:55, :] = live
    sums = finish_sum(one)
    set_norm(0, sums[0], sums[1], norms1, 0, 4.0 * live)

    end = 0
    h1_bases = []
    for pr, pc in planes:
        grid_bases, end = geo.grid(pr, pc, end)
        h1_bases.append(grid_bases)
    for plane, (pr, pc) in enumerate(planes):
        def step(b, rows, i, carry, plane=plane, pr=pr, pc=pc):
            width = sides[b] + pc
            start = h1_bases[plane][b] + ((i + pr) * width + pc) * 16
            pool[aligned(start, sides[b] * 16), :] = masked(half_silu(half(0, wide[plane][rows, :])), b).astype(BF16)
            return carry
        each(step, 0)
        for b in buckets:
            fill_halo(h1_bases[plane][b], b, pr, 0, pc, 0)
    for b in buckets:
        for h, lanes in enumerate(lane_halves):
            parts = []
            for tap in range(TAPS):
                dy, dx = tap // 3, tap % 3
                pr, pc = int(dy != 1), int(dx != 1)
                parts.append(
                    window(h1_bases[2 * pr + pc][b], sides[b] + pc, b, int(dy == 2), int(dx == 2), lanes)
                )
            x0[bases[b] : bases[b] + rows_of[b], lanes] = dot(
                jnp.concatenate(parts, axis=1), bd1[h].reshape(TAPS * HALF, HALF)
            )
    h1b_bases, end = geo.grid(2, 2, 0)
    g2b_bases, end = geo.grid(2, 2, end)
    h2b, cot_at = end, end + total
    g3b = cot_at
    fetch = pltpu.make_async_copy(cot_hbm, pool.at[pl.ds(cot_at, total)], sems.at[0])
    fetch.start()
    live = vec[54:55, :]
    sums = all_sum(stats(x0))
    set_norm(1, sums[0], sums[1], norms1, 1, live)
    squeeze_excite(x0, 1, down1, downb1, up1, upb1, se1, sq1)
    def keep_h2(rows, value):
        h2[rows, :] = value
    gate(x0, 1, se1, keep_h2)
    x1[...] = dot(h2[...], w_out1[...])
    begun = begin_sum(stats(x1))
    x2[...] = dot(acts[0], w_short[...])
    sums = finish_sum(short)
    set_norm(3, sums[0], sums[1], norms1, 3, live)
    sums = finish_sum(begun)
    set_norm(2, sums[0], sums[1], norms1, 2, live)
    def middle(b, rows, i, carry):
        y = half(2, x1[rows, :]) + half(3, x2[rows, :])
        mid[rows, :] = masked(half_silu(y), b).astype(BF16)
        return carry
    each(middle, 0)

    x2[...] = dot(mid[...], w_in2[...])
    sums = all_sum(stats(x2))
    set_norm(4, sums[0], sums[1], norms2, 0, live)
    def hidden(b, rows, i, carry):
        start = h1b_bases[b] + ((i + 1) * (sides[b] + 2) + 1) * 16
        pool[aligned(start, sides[b] * 16), :] = masked(half_silu(half(4, x2[rows, :])), b).astype(BF16)
        return carry
    each(hidden, 0)
    for b in buckets:
        fill_halo(h1b_bases[b], b, 1, 1, 1, 1)
        for h, lanes in enumerate(lane_halves):
            parts = [
                window(h1b_bases[b], sides[b] + 2, b, tap // 3, tap % 3, lanes) for tap in range(TAPS)
            ]
            x3[bases[b] : bases[b] + rows_of[b], lanes] = dot(
                jnp.concatenate(parts, axis=1), bd2[h].reshape(TAPS * HALF, HALF)
            )
    sums = all_sum(stats(x3))
    set_norm(5, sums[0], sums[1], norms2, 1, live)
    squeeze_excite(x3, 5, down2, downb2, up2, upb2, se2, sq2)
    def keep_h2b(rows, value):
        pool[aligned(rows.start + h2b, rows.size), :] = value
    gate(x3, 5, se2, keep_h2b)
    x1[...] = dot(pool[h2b : h2b + total, :], w_out2[...])
    sums = all_sum(stats(x1))
    set_norm(6, sums[0], sums[1], norms2, 2, live)
    fetch.wait()
    out_at = g2b_bases[0]
    def finish(b, rows, i, carry):
        u = x1[rows, :]
        y = half(6, u) + 0.5 * mid[rows, :].astype(F32)
        tan = jnp.tanh(y)
        pool[aligned(rows.start + out_at, rows.size), :] = masked(y + y * tan, b).astype(BF16)
        g = pool[aligned(rows.start + cot_at, rows.size), :].astype(F32) * half_silu_grad(y, tan)
        x2[rows, :] = g
        return carry[0] + fold(g), carry[1] + fold(g * (u - row(6, 0)))
    local = [down_to_row(v) for v in each(finish, (zero8, zero8))]
    puts = [
        pltpu.make_async_copy(pool.at[pl.ds(out_at + bases[b], rows_of[b])], out_hbm[b], sems.at[2 + b])
        for b in buckets
    ]
    for put in puts:
        put.start()

    put_norm_grads(dnorms2, 2, 6, *local)
    set_grad(6, *all_sum(local), live)
    def third(b, rows, i, carry):
        pool[aligned(rows.start + g3b, rows.size), :] = grad_u(x2[rows, :], x1[rows, :], b)
        return carry
    each(third, 0)
    x1[...] = dot_nt(pool[g3b : g3b + total, :], w_out2[...])
    local = squeeze_excite_back(x1, x3, 5, down2, up2, se2, sq2, ddown2, ddownb2, dup2, dupb2)
    put_norm_grads(dnorms2, 1, 5, *local)
    begun = begin_sum(local)
    dw_out2[...] = dot_tn(pool[h2b : h2b + total, :], pool[g3b : g3b + total, :])
    set_grad(5, *finish_sum(begun), live)
    for put in puts:
        put.wait()
    def second(b, rows, i, carry):
        start = g2b_bases[b] + ((i + 1) * (sides[b] + 2) + 1) * 16
        pool[aligned(start, sides[b] * 16), :] = grad_u(x1[rows, :], x3[rows, :], b)
        return carry
    each(second, 0)
    for b in buckets:
        fill_halo(g2b_bases[b], b, 1, 1, 1, 1)
        for h, lanes in enumerate(lane_halves):
            parts = [
                window(g2b_bases[b], sides[b] + 2, b, 2 - tap // 3, 2 - tap % 3, lanes) for tap in range(TAPS)
            ]
            x1[bases[b] : bases[b] + rows_of[b], lanes] = dot_nt(
                jnp.concatenate(parts, axis=1),
                jnp.concatenate([bd2[h, tap] for tap in range(TAPS)], axis=1),
            )
    x3[...] = dot(mid[...], w_in2[...])
    def first(b, rows, i, carry):
        u = x3[rows, :]
        y = half(4, u)
        g = x1[rows, :] * half_silu_grad(y, jnp.tanh(y))
        x1[rows, :] = g
        return carry[0] + fold(g), carry[1] + fold(g * (u - row(4, 0)))
    local = [down_to_row(v) for v in each(first, (zero8, zero8))]
    put_norm_grads(dnorms2, 0, 4, *local)
    begun = begin_sum(local)
    for h, lanes in enumerate(lane_halves):
        source = jnp.concatenate(
            [window(h1b_bases[b], sides[b] + 2, b, 1, 1, lanes) for b in buckets], axis=0
        )
        for tap in range(TAPS):
            target = jnp.concatenate(
                [window(g2b_bases[b], sides[b] + 2, b, 2 - tap // 3, 2 - tap % 3, lanes) for b in buckets],
                axis=0,
            )
            acc[tap, h] = diagonal(dot_tn(source, target))
    put_group2 = pltpu.make_async_copy(acc, dwg2_hbm, sems.at[1])
    put_group2.start()
    set_grad(4, *finish_sum(begun), live)
    def first_u(b, rows, i, carry):
        pool[aligned(rows.start + g3b, rows.size), :] = grad_u(x1[rows, :], x3[rows, :], b)
        return carry
    each(first_u, 0)
    x2[...] = x2[...] + dot_nt(pool[g3b : g3b + total, :], w_in2[...])

    x3[...] = dot(h2[...], w_out1[...])
    x1[...] = dot(acts[0], w_short[...])
    def joined(b, rows, i, carry):
        u, s = x3[rows, :], x1[rows, :]
        y = half(2, u) + half(3, s)
        g = x2[rows, :] * half_silu_grad(y, jnp.tanh(y))
        x2[rows, :] = g
        return (
            carry[0] + fold(g),
            carry[1] + fold(g * (u - row(2, 0))),
            carry[2] + fold(g * (s - row(3, 0))),
        )
    local = [down_to_row(v) for v in each(joined, (zero8, zero8, zero8))]
    put_norm_grads(dnorms1, 2, 2, local[0], local[1])
    put_norm_grads(dnorms1, 3, 3, local[0], local[2])
    begun = begin_sum(local[:2])
    short = begin_sum(local[2:], 3)
    dw_in2[...] = dot_tn(mid[...], pool[g3b : g3b + total, :])
    sums = finish_sum(begun)
    set_grad(2, *sums, live)
    sum_g = sums[0]
    def third_one(b, rows, i, carry):
        pool[rows, :] = grad_u(x2[rows, :], x3[rows, :], b)
        return carry
    each(third_one, 0)
    x3[...] = dot_nt(pool[0:total, :], w_out1[...])
    local = squeeze_excite_back(x3, x0, 1, down1, up1, se1, sq1, ddown1, ddownb1, dup1, dupb1)
    put_norm_grads(dnorms1, 1, 1, *local)
    begun = begin_sum(local)
    set_grad(3, sum_g, *finish_sum(short), live, 51)
    def shortcut(b, rows, i, carry):
        mid[rows, :] = grad_u(x2[rows, :], x1[rows, :], b, 51)
        return carry
    each(shortcut, 0)
    puts = [
        pltpu.make_async_copy(mid.at[pl.ds(bases[b], rows_of[b])], gs_hbm[b], sems.at[2 + b]) for b in buckets
    ]
    for put in puts:
        put.start()
    dw_short[...] = dot_tn(acts[0], mid[...])
    dw_out1[...] = dot_tn(h2[...], pool[0:total, :])
    set_grad(1, *finish_sum(begun), live)
    g2_bases, end = geo.grid(1, 1, 0)
    g1_at = end
    def second_one(b, rows, i, carry):
        start = g2_bases[b] + (i * (sides[b] + 1)) * 16
        pool[aligned(start, sides[b] * 16), :] = grad_u(x3[rows, :], x0[rows, :], b)
        return carry
    each(second_one, 0)
    for b in buckets:
        fill_halo(g2_bases[b], b, 0, 1, 0, 1)
    put_group2.wait()

    def group_grads(taps, b, h2_at):
        for h, lanes in enumerate(lane_halves):
            source = h2[h2_at : h2_at + rows_of[b], lanes]
            for tap in taps:
                target = window(g2_bases[b], sides[b] + 1, b, int(tap // 3 == 0), int(tap % 3 == 0), lanes)
                if b == 0:
                    acc[tap, h] = diagonal(dot_tn(source, target))
                else:
                    acc[tap, h] += diagonal(dot_tn(source, target))

    carry = (zero8, zero8)
    for plane, (pr, pc) in enumerate(planes):
        taps = [
            tap for tap in range(TAPS) if int(tap // 3 != 1) == pr and int(tap % 3 != 1) == pc
        ]
        for b in buckets:
            size = rows_of[b]
            x0[0:size, :] = dot(acts[plane, bases[b] : bases[b] + size, :], w_in1[...])
            for h, lanes in enumerate(lane_halves):
                parts = [
                    window(g2_bases[b], sides[b] + 1, b, int(tap // 3 == 0), int(tap % 3 == 0), lanes)
                    for tap in taps
                ]
                x1[0:size, lanes] = dot_nt(
                    jnp.concatenate(parts, axis=1), jnp.concatenate([bd1[h, tap] for tap in taps], axis=1)
                )
            h2_at = bases[b] if plane == 3 else 0
            def line(i, kept, b=b, plane=plane, h2_at=h2_at):
                rows = aligned(i * sides[b] * 16, sides[b] * 16)
                u = x0[rows, :]
                y = half(0, u)
                tan = jnp.tanh(y)
                h2[aligned(h2_at + i * sides[b] * 16, sides[b] * 16), :] = masked(y + y * tan, b).astype(BF16)
                g = x1[rows, :] * half_silu_grad(y, tan)
                start = g1_at + plane * total + bases[b] + i * sides[b] * 16
                pool[aligned(start, sides[b] * 16), :] = g.astype(BF16)
                return kept[0] + fold(g), kept[1] + fold(g * (u - row(0, 0)))
            carry = lax.fori_loop(0, sides[b], line, carry)
            if plane < 3:
                group_grads(taps, b, 0)
    local = [down_to_row(v) for v in carry]
    put_norm_grads(dnorms1, 0, 0, *local)
    begun = begin_sum(local)
    for b in buckets:
        group_grads(taps, b, bases[b])
    put_group1 = pltpu.make_async_copy(acc, dwg1_hbm, sems.at[1])
    put_group1.start()
    set_grad(0, *finish_sum(begun), 4.0 * live)
    for plane in range(4):
        x0[...] = dot(acts[plane], w_in1[...])
        at = g1_at + plane * total
        def first_one(b, rows, i, carry, at=at):
            here = aligned(rows.start + at, rows.size)
            pool[here, :] = grad_u(pool[here, :].astype(F32), x0[rows, :], b)
            return carry
        each(first_one, 0)
        part = dot_tn(acts[plane], pool[at : at + total, :])
        if plane == 0:
            dw_in1[...] = part
        else:
            dw_in1[...] += part
        for b in buckets:
            put = pltpu.make_async_copy(
                pool.at[pl.ds(at + bases[b], rows_of[b])], g1_hbm[b].at[plane], sems.at[5 + 3 * plane + b]
            )
            put.start()
            puts.append(put)
    for put in puts:
        put.wait()
    put_group1.wait()


def whole():
    return pl.BlockSpec(memory_space=pltpu.VMEM)


def anywhere():
    return pl.BlockSpec(memory_space=pl.ANY)


def shape(dims, dtype=F32):
    return jax.ShapeDtypeStruct(dims, dtype)


def blocks(geo, acts, mask, count, first, second, cot):
    groups, inner = lax.axis_size("dp"), lax.axis_size("fsdp")
    total = geo.total
    ins = [acts, mask, count, *first, *second, cot]
    hbm_outs = [
        *[shape((rows, WIDTH), BF16) for rows in geo.rows],
        *[shape((4, rows, WIDTH), BF16) for rows in geo.rows],
        *[shape((rows, WIDTH), BF16) for rows in geo.rows],
        shape((TAPS, 2, HALF, 128)), shape((TAPS, 2, HALF, 128)),
    ]
    vmem_outs = []
    for is_first in (True, False):
        dims = shapes_of(is_first)
        vmem_outs.extend(shape(d) for j, d in enumerate(dims) if j != 1)
    pool_rows = 0
    for pr, pc in ((0, 0), (0, 1), (1, 0), (1, 1)):
        pool_rows = geo.grid(pr, pc, pool_rows)[1]
    pool_rows = max(
        pool_rows, geo.grid(2, 2, geo.grid(2, 2, 0)[1])[1] + 2 * total, geo.grid(1, 1, 0)[1] + 4 * total
    )
    stages = exchange_stages(groups, inner)
    big = pltpu.VMEM((total, WIDTH), F32)
    scratch = [
        pltpu.VMEM((pool_rows, WIDTH), BF16), big, big, big, big,
        pltpu.VMEM((total, WIDTH), BF16), pltpu.VMEM((total, WIDTH), BF16),
        pltpu.VMEM((TAPS, 2, HALF, 128), F32), pltpu.VMEM((104, WIDTH), F32),
        pltpu.VMEM((2, 48, WIDTH), F32), pltpu.VMEM((48, SQUEEZE_A), F32),
        pltpu.VMEM((2, 48, WIDTH), F32), pltpu.VMEM((48, SQUEEZE_B), F32),
        pltpu.VMEM((4 * len(stages), 8, 128), F32),
        pltpu.VMEM((4 * len(stages), max(stages) - 1, 8, 128), F32),
        pltpu.SemaphoreType.DMA((4 * len(stages),)), pltpu.SemaphoreType.DMA((4 * len(stages),)),
        pltpu.SemaphoreType.DMA((17,)),
    ]
    outs = pl.pallas_call(
        functools.partial(body, geo, groups, inner),
        out_shape=hbm_outs + vmem_outs,
        in_specs=[whole()] * 20 + [anywhere()],
        out_specs=[anywhere()] * len(hbm_outs) + [whole()] * len(vmem_outs),
        scratch_shapes=scratch,
        compiler_params=pltpu.CompilerParams(
            collective_id=0, has_side_effects=True, vmem_limit_bytes=LIMIT
        ),
    )(*ins)
    dwg1, dwg2 = outs[9:11]
    first_grads = [outs[11], dwg1, *outs[12:19]]
    second_grads = [outs[19], dwg2, *outs[20:]]
    return outs[0:3], outs[3:6], outs[6:9], first_grads, second_grads


class Flat:
    def __init__(self, is_first, full_length, devices):
        self.shapes = shapes_of(is_first)
        self.starts = []
        offset = 0
        for dims in self.shapes:
            self.starts.append(offset // 128)
            offset = offset + math.prod(dims)
        self.skew = offset % 128
        self.used = offset
        self.rows = full_length // 128
        self.share = self.rows // devices
        self.padded = -(-(self.share + 3) // 16) * 16


def first_lanes(limit, dims):
    return lax.broadcasted_iota(jnp.int32, dims, 1) < limit


def column_pick(b):
    row = lax.broadcasted_iota(jnp.int32, (384, SQUEEZE_A), 0)
    column = lax.broadcasted_iota(jnp.int32, (384, SQUEEZE_A), 1)
    return (row == column + SQUEEZE_A * b).astype(F32)


def unskew(info, flat):
    row = info.starts[4]
    while row < info.rows:
        size = min(256, info.rows - row)
        here = pltpu.roll(flat[row : row + size, :], 128 - info.skew, 1)
        after = pltpu.roll(flat[row + 1 : row + size + 1, :], 128 - info.skew, 1)
        flat[row : row + size, :] = jnp.where(first_lanes(128 - info.skew, (size, 128)), here, after)
        row = row + size


def reskew(info, flat):
    row = info.rows
    first = info.starts[4]
    while row > first:
        size = min(256, row - first)
        start = row - size
        here = pltpu.roll(flat[start:row, :], info.skew, 1)
        if start == first:
            ahead = pltpu.roll(flat[start : row, :], info.skew, 1)
            ahead = pltpu.roll(ahead, 1, 0)
            keep = flat[info.rows + 8 : info.rows + 9, :]
            is_top = lax.broadcasted_iota(jnp.int32, (size, 128), 0) == 0
            ahead = jnp.where(is_top, jnp.broadcast_to(keep, (size, 128)), ahead)
        else:
            ahead = pltpu.roll(flat[start - 1 : row - 1, :], info.skew, 1)
        flat[start:row, :] = jnp.where(first_lanes(info.skew, (size, 128)), ahead, here)
        row = start


def unpack(info, flat, block_pad, outs):
    def wide(out, start):
        rows = out.shape[0]
        for c in range(4):
            out[:, c * 128 : (c + 1) * 128] = flat[pl.ds(start + c, rows, stride=4), :].astype(out.dtype)

    starts = info.starts
    w_in, bd, down, downb, up, upb, w_out = outs[:7]
    wide(w_in, starts[0])
    row = lax.broadcasted_iota(jnp.int32, (128, HALF), 0) // 32
    lane = lax.broadcasted_iota(jnp.int32, (128, HALF), 1) // GROUP_WIDTH
    on_diagonal = (row == lane).astype(F32)

    def spread(index, carry):
        rows = flat[pl.ds(pl.multiple_of(starts[1] + index * 128, 8), 128), :]
        turned = pltpu.roll(rows, GROUP_WIDTH, 1)
        left = first_lanes(GROUP_WIDTH, (128, 128))
        for parity, pair in enumerate((jnp.where(left, rows, turned), jnp.where(left, turned, rows))):
            tiled = jnp.concatenate([pair, pair], axis=1) * on_diagonal
            block_pad[pl.ds(parity, 128, stride=2), :] = tiled[:, :128]
            block_pad[pl.ds(HALF + parity, 128, stride=2), :] = tiled[:, 128:]
        bd[index % 2, index // 2, :, 0:128] = block_pad[0:HALF, :].astype(BF16)
        bd[index % 2, index // 2, :, 128:HALF] = block_pad[HALF : 2 * HALF, :].astype(BF16)
        return carry

    lax.fori_loop(0, 2 * TAPS, spread, 0)
    if down.shape[1] == 128:
        down[...] = flat[starts[2] : starts[2] + WIDTH, :].astype(BF16)
    else:
        joined = jnp.concatenate([flat[pl.ds(starts[2] + q, 64, stride=3), :] for q in range(3)], axis=1)
        for b in range(8):
            block_pad[pl.ds(b, 64, stride=8), 0:SQUEEZE_A] = dot(joined, column_pick(b))
        down[...] = block_pad[:, 0:SQUEEZE_A].astype(BF16)
    downb[...] = flat[starts[3] : starts[3] + 1, 0 : downb.shape[1]]
    if info.skew:
        unskew(info, flat)
    wide(up, starts[4])
    upb[...] = jnp.concatenate([flat[starts[5] + c : starts[5] + c + 1, :] for c in range(4)], axis=1)
    wide(w_out, starts[6])
    if len(outs) == 9:
        wide(outs[7], starts[7])
    wide(outs[-1], starts[-1])


def pack(info, flat, grads):
    def wide(value, start):
        rows = value.shape[0]
        for c in range(4):
            flat[pl.ds(start + c, rows, stride=4), :] = value[:, c * 128 : (c + 1) * 128]

    starts = info.starts
    d_in, dwg, ddown, ddownb, dup, dupb, d_out = grads[:7]
    flat[info.used // 128 // 8 * 8 : info.rows, :] = jnp.zeros_like(flat[info.used // 128 // 8 * 8 : info.rows, :])
    wide(d_in, starts[0])
    group_odd = lax.broadcasted_iota(jnp.int32, (128, 128), 0) // 32 % 2 == 1
    left = first_lanes(GROUP_WIDTH, (128, 128))

    def collect(index, carry):
        even = dwg[index // 2, index % 2, pl.ds(0, 128, stride=2), :]
        odd = dwg[index // 2, index % 2, pl.ds(1, 128, stride=2), :]
        even_turned, odd_turned = pltpu.roll(even, GROUP_WIDTH, 1), pltpu.roll(odd, GROUP_WIDTH, 1)
        rows = jnp.where(
            group_odd, jnp.where(left, even_turned, odd), jnp.where(left, even, odd_turned)
        )
        flat[pl.ds(pl.multiple_of(starts[1] + index * 128, 8), 128), :] = rows
        return carry

    lax.fori_loop(0, 2 * TAPS, collect, 0)
    if ddown.shape[1] == 128:
        flat[starts[2] : starts[2] + WIDTH, :] = ddown[...]
    else:
        joined = sum(
            exact(ddown[pl.ds(b, 64, stride=8), :], column_pick(b), ((1,), (1,))) for b in range(8)
        )
        for q in range(3):
            flat[pl.ds(starts[2] + q, 64, stride=3), :] = joined[:, q * 128 : (q + 1) * 128]
    wide(dup, starts[4])
    for c in range(4):
        flat[starts[5] + c : starts[5] + c + 1, :] = dupb[:, c * 128 : (c + 1) * 128]
    wide(d_out, starts[6])
    if len(grads) == 9:
        wide(grads[7], starts[7])
    wide(grads[-1], starts[-1])
    if info.skew:
        flat[info.rows + 8 : info.rows + 9, 0 : ddownb.shape[1]] = ddownb[...]
        reskew(info, flat)
    else:
        flat[starts[3] : starts[3] + 1, :] = ddownb[...]


class Places:
    def __init__(self, groups, inner):
        self.outer, self.inner = lax.axis_index("dp"), lax.axis_index("fsdp")
        self.chips, self.lines = groups // 2, inner
        self.chip, self.core = self.outer // 2, lax.rem(self.outer, 2)

    def along(self, step):
        return lax.rem(self.inner + step, self.lines)

    def across(self, step):
        return lax.rem(self.chip + step, self.chips)

    def line(self, step):
        return (self.outer, self.along(step))

    def other_chip(self, step):
        return (2 * self.across(step) + self.core, self.inner)

    def sibling(self):
        return (2 * self.chip + 1 - self.core, self.inner)

    def greet(self, barrier):
        for step in range(1, self.lines):
            pl.semaphore_signal(barrier, inc=1, device_id=self.line(step), device_id_type=MESH)
        for step in range(1, self.chips):
            pl.semaphore_signal(barrier, inc=1, device_id=self.other_chip(step), device_id_type=MESH)
        pl.semaphore_signal(barrier, inc=1, device_id=self.sibling(), device_id_type=MESH)

    def greeted(self, barrier):
        pl.semaphore_wait(barrier, self.lines + self.chips - 1)


def remote(source, target, send_sem, recv_sem, device):
    return pltpu.make_async_remote_copy(
        src_ref=source, dst_ref=target, send_sem=send_sem, recv_sem=recv_sem, device_id=device, device_id_type=MESH
    )


def gather_body(geo, infos, groups, inner, *refs):
    images, cots, counts = refs[0:3], refs[3:6], refs[6]
    shards = refs[7:9]
    acts, cot, mask, live = refs[9:13]
    weights = [refs[13:22], refs[22:30]]
    scratch = refs[30:]
    wide_cell, cot_cell, block_pad = scratch[0:3]
    gathered, flats = scratch[3:5], scratch[5:7]
    line_send, line_recv, chip_send, chip_recv, core_send, core_recv = scratch[7:]
    places = Places(groups, inner)
    barrier = pltpu.get_barrier_semaphore()
    places.greet(barrier)
    mine = [buf.at[places.chip, places.core, places.inner] for buf in gathered]
    slot = lax.broadcasted_iota(jnp.int32, (16, WIDTH), 0) % 4
    for b in range(3):
        mask[b] = jnp.where(slot < counts[0, b], 1.0, 0.0)
    for k, info in enumerate(infos):
        stage = flats[k].at[pl.ds(0, info.padded)]
        stage[info.padded - 16 : info.padded, :] = jnp.zeros((16, 128), F32)
        stage[0 : info.share, :] = shards[k][...]
        for b in range(3):
            value = jnp.broadcast_to(counts[0, b].astype(F32), (1, 128))
            stage[info.share + b : info.share + b + 1, :] = value
        mine[k][...] = stage[...].astype(BF16)
    places.greeted(barrier)
    started = []

    def begin(copy):
        copy.start()
        started.append(copy)
        return copy

    lines = [
        [begin(remote(mine[k], mine[k], line_send.at[k, step - 1], line_recv.at[k, step - 1], places.line(step))) for step in range(1, inner)]
        for k in range(2)
    ]
    chip_copies = [[], []]

    def forward(k):
        for copy in lines[k]:
            copy.wait_recv()
        line = gathered[k].at[places.chip, places.core]
        for step in range(1, places.chips):
            chip_copies[k].append(
                begin(remote(line, line, chip_send.at[k, step - 1], chip_recv.at[k, step - 1], places.other_chip(step)))
            )
        begin(remote(line, line, core_send.at[k, 0], core_recv.at[k], places.sibling()))

    def pass_on(k):
        for step in range(1, places.chips):
            chip_copies[k][step - 1].wait_recv()
            line = gathered[k].at[places.across(places.chips - step), places.core]
            begin(remote(line, line, core_send.at[k, step], core_recv.at[k], places.sibling()))

    def complete(k):
        half = gathered[k].at[:, 0]
        pltpu.make_async_copy(half, half, core_recv.at[k]).wait()
        info = infos[k]
        found = jnp.zeros((3, 128), F32)
        for d in range(groups * inner):
            at = info.share * d
            piece = gathered[k][d // inner // 2, d // inner % 2, d % inner].astype(F32)
            flats[k][at : at + info.share, :] = piece[0 : info.share]
            found = found + piece[info.share : info.share + 3]
        if k == 0:
            total = sum(found[b : b + 1, :] * (4.0 * side * side) for b, side in enumerate(geo.sides))
            live[...] = jnp.concatenate([total] * 4, axis=1)
        unpack(info, flats[k], block_pad, weights[k])

    def arrange(b):
        side = geo.sides[b]
        size = side * 16

        def line(i, carry):
            rows = aligned(geo.bases[b] + i * size, size)
            for pr in range(2):
                for pc in range(2):
                    for q in range(4):
                        wide_cell[0:side, 4 * q : 4 * q + 4, :] = images[b][q // 2, i, pr, q % 2, :, pc].astype(F32)
                    value = wide_cell[0:side] * mask[b][None, :, :WIDTH_IN]
                    acts[2 * pr + pc, rows, :] = value.reshape(size, WIDTH_IN).astype(BF16)
            for q in range(4):
                cot_cell[0:side, 4 * q : 4 * q + 4, :] = cots[b][q // 2, i, q % 2].astype(F32)
            value = cot_cell[0:side] * mask[b][None]
            cot[rows, :] = value.reshape(size, WIDTH).astype(BF16)
            return carry

        lax.fori_loop(0, side, line, 0)

    arrange(0)
    forward(0)
    arrange(1)
    forward(1)
    pass_on(0)
    arrange(2)
    pass_on(1)
    complete(0)
    complete(1)
    for copy in started:
        copy.wait_send()


def gather(geo, infos, images, cots, counts, shards):
    groups, inner = lax.axis_size("dp"), lax.axis_size("fsdp")
    ins = [*images, *cots, counts, *[shard.reshape(-1, 128) for shard in shards]]
    outs = [shape((4, geo.total, WIDTH_IN), BF16), shape((geo.total, WIDTH), BF16)]
    outs += [shape((3, 16, WIDTH)), shape((1, WIDTH))]
    for is_first in (True, False):
        dims = shapes_of(is_first)
        outs += [shape(dims[0], BF16), shape((2, TAPS, HALF, HALF), BF16)]
        outs += [shape(d, F32 if d[0] == 1 else BF16) for d in dims[2:-1]] + [shape(dims[-1])]
    side = max(geo.sides)
    scratch = [
        pltpu.VMEM((side, 16, WIDTH_IN), F32), pltpu.VMEM((side, 16, WIDTH), F32), pltpu.VMEM((2 * HALF, 128), F32),
    ]
    scratch += [pltpu.VMEM((groups // 2, 2, inner, info.padded, 128), BF16) for info in infos]
    scratch += [pltpu.VMEM((info.rows + 16, 128), F32) for info in infos]
    chips = groups // 2
    scratch += [
        pltpu.SemaphoreType.DMA(dims)
        for dims in ((2, inner - 1), (2, inner - 1), (2, chips - 1), (2, chips - 1), (2, chips), (2,))
    ]
    results = pl.pallas_call(
        functools.partial(gather_body, geo, infos, groups, inner),
        out_shape=outs,
        in_specs=[whole()] * 6 + [pl.BlockSpec(memory_space=pltpu.SMEM)] + [whole()] * 2,
        out_specs=[whole()] * len(outs),
        scratch_shapes=scratch,
        compiler_params=pltpu.CompilerParams(
            collective_id=1, has_side_effects=True, vmem_limit_bytes=LIMIT
        ),
    )(*ins)
    return results[:4], results[4:13], results[13:]


def scatter_body(infos, groups, inner, *refs):
    grads = [refs[0:9], refs[9:17]]
    outs = refs[17:19]
    flat, parts, core_in, chip_sum, chip_in, line_sum, line_in = refs[19:26]
    core_send, core_recv, chip_send, chip_recv, line_send, line_recv = refs[26:]
    places = Places(groups, inner)
    barrier = pltpu.get_barrier_semaphore()
    places.greet(barrier)
    devices = groups * inner
    offsets = [0, infos[0].padded]
    for k, info in enumerate(infos):
        pack(info, flat, grads[k])
        for d in range(devices):
            place = parts.at[d // inner % 2, d // inner // 2, d % inner]
            place[offsets[k] : offsets[k] + info.share, :] = flat[info.share * d : info.share * (d + 1), :].astype(BF16)
            if info.share < info.padded:
                gap = info.padded - info.share
                place[offsets[k] + info.share : offsets[k] + info.padded, :] = jnp.zeros((gap, 128), BF16)
    places.greeted(barrier)
    core = remote(parts.at[1 - places.core], core_in, core_send, core_recv, places.sibling())
    core.start()
    core.wait_recv()

    def add(index, carry):
        chip, z = index // inner, index % inner
        chip_sum[chip, z] = (parts[places.core, chip, z].astype(F32) + core_in[chip, z].astype(F32)).astype(BF16)
        return carry

    lax.fori_loop(0, places.chips * inner, add, 0)
    copies = []
    for step in range(1, places.chips):
        copies.append(
            remote(chip_sum.at[places.across(step)], chip_in.at[step - 1], chip_send.at[step - 1], chip_recv.at[step - 1], places.other_chip(step))
        )
        copies[-1].start()
    for copy in copies:
        copy.wait_recv()

    def add_chips(z, carry):
        value = chip_sum[places.chip, z].astype(F32)
        for step in range(places.chips - 1):
            value = value + chip_in[step, z].astype(F32)
        line_sum[z] = value.astype(BF16)
        return carry

    lax.fori_loop(0, inner, add_chips, 0)
    lines = []
    for step in range(1, inner):
        lines.append(
            remote(line_sum.at[places.along(step)], line_in.at[step - 1], line_send.at[step - 1], line_recv.at[step - 1], places.line(step))
        )
        lines[-1].start()
    for copy in lines:
        copy.wait_recv()
    value = line_sum[places.inner].astype(F32)
    for step in range(inner - 1):
        value = value + line_in[step].astype(F32)
    for k, info in enumerate(infos):
        outs[k][...] = value[offsets[k] : offsets[k] + info.share, :]
    core.wait_send()
    for copy in copies + lines:
        copy.wait_send()


def scatter(infos, first_grads, second_grads):
    groups, inner = lax.axis_size("dp"), lax.axis_size("fsdp")
    ins = [*first_grads, *second_grads]
    chips = groups // 2
    size = sum(info.padded for info in infos)
    def part(*lead):
        return pltpu.VMEM((*lead, size, 128), BF16)
    outs = pl.pallas_call(
        functools.partial(scatter_body, infos, groups, inner),
        out_shape=[shape((info.share, 128)) for info in infos],
        in_specs=[whole()] * len(ins),
        out_specs=[whole()] * 2,
        scratch_shapes=[
            pltpu.VMEM((max(info.rows for info in infos) + 16, 128), F32),
            part(2, chips, inner), part(chips, inner), part(chips, inner), part(chips - 1, inner), part(inner),
            part(inner - 1),
        ]
        + [pltpu.SemaphoreType.DMA(dims) for dims in ((), (), (chips - 1,), (chips - 1,), (inner - 1,), (inner - 1,))],
        compiler_params=pltpu.CompilerParams(
            collective_id=2, has_side_effects=True, vmem_limit_bytes=LIMIT
        ),
    )(*ins)
    return [out.reshape(-1) for out in outs]


def restore_body(side, g1, gs, out, w_in, w_short, outputs, image_grads, grad_cell, out_cell):
    size = side * 16
    out_cell[...] = out[...].astype(F32).reshape(side, 16, WIDTH)
    for q in range(4):
        outputs[q // 2, 0, q % 2] = out_cell[:, 4 * q : 4 * q + 4, :].astype(BF16)
    value = dot_nt(g1[...].reshape(4 * size, WIDTH), w_in[...])
    grad_cell[...] = value.reshape(4, side, 16, WIDTH_IN)
    grad_cell[0] += dot_nt(gs[...], w_short[...]).reshape(side, 16, WIDTH_IN)
    for plane in range(4):
        for q in range(4):
            image_grads[q // 2, 0, plane // 2, q % 2, :, plane % 2] = grad_cell[plane, :, 4 * q : 4 * q + 4, :]


def restore(side, g1, gs, out, w_in, w_short):
    size = side * 16
    def line(dims):
        return pl.BlockSpec(dims, lambda i: (0, i) + (0,) * (len(dims) - 2))
    rows = pl.BlockSpec((size, WIDTH), lambda i: (i, 0))
    output, grad = pl.pallas_call(
        functools.partial(restore_body, side),
        grid=(side,),
        out_shape=[shape((2, side, 2, side, 4, WIDTH), BF16), shape((2, side, 2, 2, side, 2, 4, WIDTH_IN))],
        in_specs=[line((4, size, WIDTH)), rows, rows, whole(), whole()],
        out_specs=[line((2, 1, 2, side, 4, WIDTH)), line((2, 1, 2, 2, side, 2, 4, WIDTH_IN))],
        scratch_shapes=[pltpu.VMEM((4, side, 16, WIDTH_IN), F32), pltpu.VMEM((side, 16, WIDTH), F32)],
        compiler_params=pltpu.CompilerParams(vmem_limit_bytes=LIMIT),
    )(g1, gs, out, w_in, w_short)
    output = output.reshape(2 * side, 2 * side, 4, WIDTH).transpose(2, 0, 1, 3)
    return output, grad.reshape(4 * side, 4 * side, 4, WIDTH_IN).transpose(2, 0, 1, 3)


def per_device(*args):
    images, counts = args[0:3], args[3]
    cots = args[6:9]
    geo = Geometry([image.shape[1] // 4 for image in images])
    devices = lax.axis_size("dp") * lax.axis_size("fsdp")
    infos = [Flat(k == 0, args[4 + k].shape[0] * devices, devices) for k in range(2)]
    split_images = [
        image.transpose(1, 2, 0, 3).reshape(2, side, 2, 2, side, 2, 4, WIDTH_IN)
        for image, side in zip(images, geo.sides)
    ]
    split_cots = [
        value.transpose(1, 2, 0, 3).reshape(2, side, 2, side, 4, WIDTH) for value, side in zip(cots, geo.sides)
    ]
    (acts, cot, mask, live), first, second = gather(geo, infos, split_images, split_cots, counts, args[4:6])
    out, g1, gs, first_grads, second_grads = blocks(geo, acts, mask, live, first, second, cot)
    results = [
        restore(side, g1[b], gs[b], out[b], first[0], first[7]) for b, side in enumerate(geo.sides)
    ]
    return (
        *[result[0] for result in results],
        *[result[1] for result in results],
        *scatter(infos, first_grads, second_grads),
    )


def solution(mesh):
    images = P(("dp", "fsdp"), None, None, None)
    flat = P(("dp", "fsdp"))
    in_specs = (images, images, images, P(("dp", "fsdp"), None), flat, flat, images, images, images)
    out_specs = (images,) * 6 + (flat, flat)
    return jax.shard_map(per_device, mesh=mesh, in_specs=in_specs, out_specs=out_specs, check_vma=False)
```

```python
import functools
import math

import jax
import jax.numpy as jnp
from jax import lax
from jax.experimental import pallas as pl
from jax.experimental.pallas import tpu as pltpu
from jax.sharding import PartitionSpec as P

WIDTH_IN = 192
GROUPS = 8
GROUP_WIDTH = 64
SQUEEZE_A = 48
SQUEEZE_B = 128
WIDTH = 512
HALF = 256
TAPS = 9
EPSILON = 1e-05
HIGHEST = lax.Precision.HIGHEST
MESH = pl.DeviceIdType.MESH
F32 = jnp.float32
BF16 = jnp.bfloat16
LIMIT = 63 * 2**20


def shapes_of(is_first):
    width_in, squeeze = (WIDTH_IN, SQUEEZE_A) if is_first else (WIDTH, SQUEEZE_B)
    shapes = [
        (width_in, WIDTH),
        (TAPS, GROUPS, GROUP_WIDTH, GROUP_WIDTH),
        (WIDTH, squeeze),
        (1, squeeze),
        (squeeze, WIDTH),
        (1, WIDTH),
        (WIDTH, WIDTH),
    ]
    if is_first:
        shapes.append((WIDTH_IN, WIDTH))
    shapes.append((8 if is_first else 6, WIDTH))
    return shapes


def diagonal(product):
    parts = []
    for g in range(4):
        lanes = slice(128 * (g // 2), 128 * (g // 2) + 128)
        parts.append(product[g * GROUP_WIDTH : (g + 1) * GROUP_WIDTH, lanes])
    return jnp.concatenate(parts, axis=0)


def dot(left, right):
    return jnp.dot(left, right, preferred_element_type=F32)


def dot_nt(left, right):
    return lax.dot_general(left, right, (((1,), (1,)), ((), ())), preferred_element_type=F32)


def dot_tn(left, right):
    return lax.dot_general(left, right, (((0,), (0,)), ((), ())), preferred_element_type=F32)


def exact(left, right, dims):
    return lax.dot_general(
        left, right, (dims, ((), ())), precision=HIGHEST, preferred_element_type=F32
    )


def by_parts(product, left, right):
    high = left.astype(BF16)
    rest = left - high.astype(F32)
    middle = rest.astype(BF16)
    low = (rest - middle.astype(F32)).astype(BF16)
    rows = left.shape[0]
    full = product(jnp.concatenate([high, middle, low], axis=0), right)
    return full[:rows] + full[rows : 2 * rows] + full[2 * rows :]


def half_silu(half):
    return half + half * jnp.tanh(half)


def half_silu_grad(half, tan):
    return (0.5 + 0.5 * tan) * (1.0 + half * (1.0 - tan))


def fold(values):
    return jnp.sum(values.reshape(-1, 8, WIDTH), axis=0)


def down_to_row(values):
    return jnp.sum(values, axis=0, keepdims=True)


class Geometry:
    def __init__(self, sides):
        self.sides = sides
        self.rows = [side * side * 16 for side in sides]
        self.bases = [sum(self.rows[:b]) for b in range(len(sides))]
        self.total = sum(self.rows)

    def grid(self, extra_rows, extra_cols, start):
        bases = []
        for side in self.sides:
            bases.append(start)
            start = start + (side + extra_rows) * (side + extra_cols) * 16
        return bases, start


def exchange_stages(groups, inner):
    return [groups * inner] if groups * inner <= 64 else [inner, groups]


def aligned(start, size):
    return pl.ds(pl.multiple_of(start, 16), size)


def body(geo, info, groups, inner, *refs):
    (
        acts_hbm, mask, count, w_in1, bd1, down1, downb1, up1, upb1, w_out1, w_short, norms1, line2, cot_hbm,
    ) = refs[:14]
    out_hbm, g1_hbm, gs_hbm = refs[14:17], refs[17:20], refs[20:23]
    (
        dwg1_hbm, second_out,
        dw_in1, ddown1, ddownb1, dup1, dupb1, dw_out1, dw_short, dnorms1,
    ) = refs[23:33]
    weights2, grads2 = refs[33:41], refs[41:48]
    w_in2, bd2, down2, downb2, up2, upb2, w_out2, norms2 = weights2
    dw_in2, ddown2, ddownb2, dup2, dupb2, dw_out2, dnorms2 = grads2
    (
        acts, acts_sem, tall, shares, pool, x0, x1, x2, x3, h2, mid, acc, vec, se1, sq1, se2, sq2,
        pay, slots, send_sem, recv_sem, sems,
        near_send, near_recv, near_core_send, core_land, far_core, far_chip_send, far_chip_recv, far_line_send, far_line_recv,
    ) = refs[48:]
    places = Places(groups, inner)
    loads = [pltpu.make_async_copy(acts_hbm.at[k], acts.at[k], acts_sem.at[k]) for k in range(4)]
    for load in loads:
        load.start()
    sides, bases, rows_of, total = geo.sides, geo.bases, geo.rows, geo.total
    buckets = range(len(sides))
    devices = groups * inner

    outer_index, inner_index = lax.axis_index("dp"), lax.axis_index("fsdp")

    def any_partner(step):
        other = lax.rem(outer_index * inner + inner_index + step, devices)
        return (other // inner, lax.rem(other, inner))

    def inner_partner(step):
        return (outer_index, lax.rem(inner_index + step, inner))

    def outer_partner(step):
        return (lax.rem(outer_index + step, groups), inner_index)

    barrier = pltpu.get_barrier_semaphore()
    stages = exchange_stages(groups, inner)
    if len(stages) == 1:
        partners = [any_partner]
    else:
        partners = [inner_partner, outer_partner]
    for count_in_stage, partner in zip(stages, partners):

        def greet(step, carry, partner=partner):
            pl.semaphore_signal(barrier, inc=1, device_id=partner(step), device_id_type=MESH)
            return carry

        lax.fori_loop(1, count_in_stage, greet, 0)

    calls = []

    def put_rows(at, sums):
        for c in range(4):
            for r, row in enumerate(sums):
                pay[at, 4 * r + c : 4 * r + c + 1, :] = row[:, c * 128 : (c + 1) * 128]

    def send_stage(stage, at):
        def send(step, carry):
            pltpu.make_async_remote_copy(
                src_ref=pay.at[at],
                dst_ref=slots.at[at, step - 1],
                send_sem=send_sem.at[at],
                recv_sem=recv_sem.at[at],
                device_id=partners[stage](step),
                device_id_type=MESH,
            ).start()
            return carry

        lax.fori_loop(1, stages[stage], send, 0)

    def land_stage(stage, at):
        landed = slots.at[at, pl.ds(0, stages[stage] - 1)]
        pltpu.make_async_copy(landed, landed, recv_sem.at[at]).wait()
        sums = pay[at] + jnp.sum(slots[at, 0 : stages[stage] - 1], axis=0)
        pltpu.make_async_copy(landed, landed, send_sem.at[at]).wait()
        return sums

    def begin_sum(rows, place=None):
        if not calls:
            pl.semaphore_wait(barrier, sum(stages) - len(stages))
        if place is None:
            place = sum(p < 2 for p in calls) % 2
        calls.append(place)
        put_rows(place * len(stages), rows)
        send_stage(0, place * len(stages))
        return place, len(rows)

    def finish_sum(begun):
        place, number = begun
        for stage in range(len(stages)):
            at = place * len(stages) + stage
            if stage:
                pay[at] = sums
                send_stage(stage, at)
            sums = land_stage(stage, at)
        return [
            jnp.concatenate([sums[4 * r + c : 4 * r + c + 1, :] for c in range(4)], axis=1) for r in range(number)
        ]

    def all_sum(rows):
        return finish_sum(begin_sum(rows))

    def each(step, carry):
        for b in buckets:
            def line(i, kept, b=b):
                size = sides[b] * 16
                return step(b, aligned(bases[b] + i * size, size), i, kept)
            carry = lax.fori_loop(0, sides[b], line, carry)
        return carry

    zero8 = jnp.zeros((8, WIDTH), F32)

    def masked(values, b):
        return (values.reshape(-1, 16, WIDTH) * mask[b][None]).reshape(values.shape)

    def set_norm(k, sums, squares, norms, index, live):
        mean = sums / live
        inv_std = lax.rsqrt(squares / live - mean * mean + EPSILON)
        scale = inv_std * norms[2 * index : 2 * index + 1, :]
        offset = norms[2 * index + 1 : 2 * index + 2, :] - mean * scale
        for r, row in enumerate((mean, inv_std, scale, offset, 0.5 * scale, 0.5 * offset)):
            vec[6 * k + r : 6 * k + r + 1, :] = row

    def row(k, r):
        return vec[6 * k + r : 6 * k + r + 1, :]

    def half(k, u):
        return u * row(k, 4) + row(k, 5)

    def set_grad(k, sum_g, sum_d, live, at=48):
        scale, inv_std = row(k, 2), row(k, 1)
        on_u = -scale * inv_std * inv_std * sum_d / live
        vec[at : at + 1, :] = scale
        vec[at + 1 : at + 2, :] = on_u
        vec[at + 2 : at + 3, :] = -scale * sum_g / live - row(k, 0) * on_u

    def grad_u(g, u, b, at=48):
        inner_grad = g * vec[at : at + 1, :] + (u * vec[at + 1 : at + 2, :] + vec[at + 2 : at + 3, :])
        return masked(inner_grad, b).astype(BF16)

    def stats(x):
        def step(b, rows, i, carry):
            u = x[rows, :]
            return carry[0] + fold(u), carry[1] + fold(u * u)
        sums, squares = each(step, (zero8, zero8))
        return down_to_row(sums), down_to_row(squares)

    def window(base, width, b, r0, c0, lanes, lines=None):
        side = sides[b]
        return jnp.concatenate(
            [
                pool[base + ((r0 + i) * width + c0) * 16 : base + ((r0 + i) * width + c0 + side) * 16, lanes]
                for i in lines or range(side)
            ],
            axis=0,
        )

    lane_halves = [slice(0, HALF), slice(HALF, WIDTH)]

    def pattern(size, bit, value):
        index = lax.broadcasted_iota(jnp.int32, (size, WIDTH), 0)
        return ((index // bit) % 2 == value).astype(F32)

    def fill_halo(base, b, low_r, high_r, low_c, high_c):
        side = sides[b]
        width = side + low_c + high_c
        def cell(r, c, n=1):
            return slice(base + (r * width + c) * 16, base + (r * width + c + n) * 16)
        for i in range(side):
            r = i + low_r
            if low_c:
                value = pool[cell(r, side), :].astype(F32)
                pool[cell(r, 0), :] = (pltpu.roll(value, 4, 0) * pattern(16, 4, 1)).astype(BF16)
            if high_c:
                value = pool[cell(r, low_c), :].astype(F32)
                pool[cell(r, width - 1), :] = (pltpu.roll(value, 12, 0) * pattern(16, 4, 0)).astype(BF16)
        size = width * 16
        if low_r:
            value = pool[cell(side, 0, width), :].astype(F32)
            pool[cell(0, 0, width), :] = (pltpu.roll(value, 8, 0) * pattern(size, 8, 1)).astype(BF16)
        if high_r:
            value = pool[cell(low_r, 0, width), :].astype(F32)
            pool[cell(low_r + side, 0, width), :] = (
                pltpu.roll(value, size - 8, 0) * pattern(size, 8, 0)
            ).astype(BF16)

    first_of_image = (lax.broadcasted_iota(jnp.int32, (48, WIDTH), 0) % 16 < 4).astype(F32)

    def over_quadrants(v):
        return v + pltpu.roll(v, 4, 0) + pltpu.roll(v, 8, 0) + pltpu.roll(v, 12, 0)

    def squeeze_excite(x, k, down, downb, up, upb, se, sq):
        def step(b, rows, i, carry):
            v = half_silu(half(k, x[rows, :])).reshape(-1, 16, WIDTH)
            return tuple(c + jnp.sum(v, axis=0) if d == b else c for d, c in enumerate(carry))
        zero16 = jnp.zeros((16, WIDTH), F32)
        sums = each(step, tuple(zero16 for _ in buckets))
        pooled = jnp.concatenate(
            [over_quadrants(s) * (1.0 / (4 * side * side)) for s, side in zip(sums, sides)], axis=0
        )
        squeeze_pre = by_parts(dot, pooled, down[...]) + downb[...]
        squeezed = squeeze_pre * jax.nn.sigmoid(squeeze_pre)
        excite = jax.nn.sigmoid(by_parts(dot, squeezed, up[...]) + upb[...])
        se[0] = pooled
        sq[...] = squeeze_pre
        for b in buckets:
            se[1, 16 * b : 16 * b + 16, :] = excite[16 * b : 16 * b + 16, :] * mask[b]

    def gate(x, k, se, store):
        def step(b, rows, i, carry):
            v = half_silu(half(k, x[rows, :])).reshape(-1, 16, WIDTH)
            v = v * se[1, 16 * b : 16 * b + 16, :][None]
            store(rows, v.reshape(-1, WIDTH).astype(BF16))
            return carry
        each(step, 0)

    def squeeze_excite_back(g, u, k, down, up, se, sq, ddown, ddownb, dup, dupb):
        def step(b, rows, i, carry):
            v = half_silu(half(k, u[rows, :])) * g[rows, :]
            return tuple(
                c + jnp.sum(v.reshape(-1, 16, WIDTH), axis=0) if d == b else c
                for d, c in enumerate(carry)
            )
        zero16 = jnp.zeros((16, WIDTH), F32)
        sums = each(step, tuple(zero16 for _ in buckets))
        grad_excite = jnp.concatenate([over_quadrants(s) for s in sums], axis=0)
        excite = se[1]
        grad_up = grad_excite * excite * (1.0 - excite)
        squeeze_pre = sq[...]
        sig = jax.nn.sigmoid(squeeze_pre)
        once = first_of_image
        dup[...] = exact(squeeze_pre * sig, grad_up * once, ((0,), (0,)))
        dupb[...] = down_to_row(grad_up * once)
        grad_pre = by_parts(dot_nt, grad_up, up[...]) * (sig * (1.0 + squeeze_pre * (1.0 - sig)))
        ddown[...] = exact(se[0] * once, grad_pre, ((0,), (0,)))
        ddownb[...] = down_to_row(grad_pre * once[:, : grad_pre.shape[1]])
        pooled_grad = by_parts(dot_nt, grad_pre, down[...])
        for b in buckets:
            pixels = 4 * sides[b] * sides[b]
            vec[56 + 16 * b : 72 + 16 * b, :] = pooled_grad[16 * b : 16 * b + 16, :] * (1.0 / pixels)

        def apply(b, rows, i, carry):
            u_now = u[rows, :]
            y = half(k, u_now)
            slope = half_silu_grad(y, jnp.tanh(y))
            gv = g[rows, :].reshape(-1, 16, WIDTH) * se[1, 16 * b : 16 * b + 16, :][None]
            gv = (gv + vec[56 + 16 * b : 72 + 16 * b, :][None]).reshape(-1, WIDTH) * slope
            g[rows, :] = gv
            return carry[0] + fold(gv), carry[1] + fold(gv * (u_now - row(k, 0)))

        sum_g, sum_d = each(apply, (zero8, zero8))
        return down_to_row(sum_g), down_to_row(sum_d)

    def put_norm_grads(out, index, k, sum_g, sum_d):
        out[2 * index : 2 * index + 1, :] = row(k, 1) * sum_d
        out[2 * index + 1 : 2 * index + 2, :] = sum_g

    planes = [(0, 0), (0, 1), (1, 0), (1, 1)]

    chunk = total // 5
    wide = [x0, x1, x2, x3]

    def stat_dot(plane, weight, out, carry):
        def step(i, kept):
            rows = aligned(i * chunk, chunk)
            u = dot(acts[plane, rows, :], weight[...])
            if out is not None:
                out[rows, :] = u
            return kept[0] + fold(u), kept[1] + fold(u * u)
        return lax.fori_loop(0, 5, step, carry)

    carry = (zero8, zero8)
    for plane in range(4):
        loads[plane].wait()
        carry = stat_dot(plane, w_in1, wide[plane], carry)
    one = begin_sum([down_to_row(v) for v in carry])
    short = begin_sum([down_to_row(v) for v in stat_dot(0, w_short, None, (zero8, zero8))], 2)
    live = count[...]
    vec[54:55, :] = live
    sums = finish_sum(one)
    set_norm(0, sums[0], sums[1], norms1, 0, 4.0 * live)

    end = 0
    h1_bases = []
    for pr, pc in planes:
        grid_bases, end = geo.grid(pr, pc, end)
        h1_bases.append(grid_bases)
    second = SecondGather(
        info, places, line2, pool, end, (near_send, near_recv, near_core_send, core_land)
    )
    second.begin()
    for plane, (pr, pc) in enumerate(planes):
        def step(b, rows, i, carry, plane=plane, pr=pr, pc=pc):
            width = sides[b] + pc
            start = h1_bases[plane][b] + ((i + pr) * width + pc) * 16
            pool[aligned(start, sides[b] * 16), :] = masked(half_silu(half(0, wide[plane][rows, :])), b).astype(BF16)
            return carry
        each(step, 0)
        for b in buckets:
            fill_halo(h1_bases[plane][b], b, pr, 0, pc, 0)
    for b in buckets:
        for h, lanes in enumerate(lane_halves):
            parts = []
            for tap in range(TAPS):
                dy, dx = tap // 3, tap % 3
                pr, pc = int(dy != 1), int(dx != 1)
                parts.append(
                    window(h1_bases[2 * pr + pc][b], sides[b] + pc, b, int(dy == 2), int(dx == 2), lanes)
                )
            x0[bases[b] : bases[b] + rows_of[b], lanes] = dot(
                jnp.concatenate(parts, axis=1), bd1[h].reshape(TAPS * HALF, HALF)
            )
    h1b_bases, end = geo.grid(2, 2, 0)
    g2b_bases, end = geo.grid(2, 2, end)
    h2b, cot_at = end, end + total
    g3b = cot_at
    second.pass_on()
    live = vec[54:55, :]
    sums = all_sum(stats(x0))
    set_norm(1, sums[0], sums[1], norms1, 1, live)
    squeeze_excite(x0, 1, down1, downb1, up1, upb1, se1, sq1)
    def keep_h2(rows, value):
        h2[rows, :] = value
    gate(x0, 1, se1, keep_h2)
    x1[...] = dot(h2[...], w_out1[...])
    begun = begin_sum(stats(x1))
    x2[...] = dot(acts[0], w_short[...])
    second.finish(x3, shares, tall, weights2)
    fetch = pltpu.make_async_copy(cot_hbm, pool.at[pl.ds(cot_at, total)], sems.at[0])
    fetch.start()
    sums = finish_sum(short)
    set_norm(3, sums[0], sums[1], norms1, 3, live)
    sums = finish_sum(begun)
    set_norm(2, sums[0], sums[1], norms1, 2, live)
    def middle(b, rows, i, carry):
        y = half(2, x1[rows, :]) + half(3, x2[rows, :])
        mid[rows, :] = masked(half_silu(y), b).astype(BF16)
        return carry
    each(middle, 0)

    x2[...] = dot(mid[...], w_in2[...])
    sums = all_sum(stats(x2))
    set_norm(4, sums[0], sums[1], norms2, 0, live)
    def hidden(b, rows, i, carry):
        start = h1b_bases[b] + ((i + 1) * (sides[b] + 2) + 1) * 16
        pool[aligned(start, sides[b] * 16), :] = masked(half_silu(half(4, x2[rows, :])), b).astype(BF16)
        return carry
    each(hidden, 0)
    for b in buckets:
        fill_halo(h1b_bases[b], b, 1, 1, 1, 1)
        for h, lanes in enumerate(lane_halves):
            parts = [
                window(h1b_bases[b], sides[b] + 2, b, tap // 3, tap % 3, lanes) for tap in range(TAPS)
            ]
            x3[bases[b] : bases[b] + rows_of[b], lanes] = dot(
                jnp.concatenate(parts, axis=1), bd2[h].reshape(TAPS * HALF, HALF)
            )
    sums = all_sum(stats(x3))
    set_norm(5, sums[0], sums[1], norms2, 1, live)
    squeeze_excite(x3, 5, down2, downb2, up2, upb2, se2, sq2)
    def keep_h2b(rows, value):
        pool[aligned(rows.start + h2b, rows.size), :] = value
    gate(x3, 5, se2, keep_h2b)
    x1[...] = dot(pool[h2b : h2b + total, :], w_out2[...])
    sums = all_sum(stats(x1))
    set_norm(6, sums[0], sums[1], norms2, 2, live)
    fetch.wait()
    out_at = g2b_bases[0]
    def finish(b, rows, i, carry):
        u = x1[rows, :]
        y = half(6, u) + 0.5 * mid[rows, :].astype(F32)
        tan = jnp.tanh(y)
        pool[aligned(rows.start + out_at, rows.size), :] = masked(y + y * tan, b).astype(BF16)
        g = pool[aligned(rows.start + cot_at, rows.size), :].astype(F32) * half_silu_grad(y, tan)
        x2[rows, :] = g
        return carry[0] + fold(g), carry[1] + fold(g * (u - row(6, 0)))
    local = [down_to_row(v) for v in each(finish, (zero8, zero8))]
    puts = [
        pltpu.make_async_copy(pool.at[pl.ds(out_at + bases[b], rows_of[b])], out_hbm[b], sems.at[2 + b])
        for b in buckets
    ]
    for put in puts:
        put.start()

    put_norm_grads(dnorms2, 2, 6, *local)
    set_grad(6, *all_sum(local), live)
    def third(b, rows, i, carry):
        pool[aligned(rows.start + g3b, rows.size), :] = grad_u(x2[rows, :], x1[rows, :], b)
        return carry
    each(third, 0)
    x1[...] = dot_nt(pool[g3b : g3b + total, :], w_out2[...])
    local = squeeze_excite_back(x1, x3, 5, down2, up2, se2, sq2, ddown2, ddownb2, dup2, dupb2)
    put_norm_grads(dnorms2, 1, 5, *local)
    begun = begin_sum(local)
    dw_out2[...] = dot_tn(pool[h2b : h2b + total, :], pool[g3b : g3b + total, :])
    set_grad(5, *finish_sum(begun), live)
    for put in puts:
        put.wait()
    def second_u(b, rows, i, carry):
        start = g2b_bases[b] + ((i + 1) * (sides[b] + 2) + 1) * 16
        pool[aligned(start, sides[b] * 16), :] = grad_u(x1[rows, :], x3[rows, :], b)
        return carry
    each(second_u, 0)
    for b in buckets:
        fill_halo(g2b_bases[b], b, 1, 1, 1, 1)
        for h, lanes in enumerate(lane_halves):
            parts = [
                window(g2b_bases[b], sides[b] + 2, b, 2 - tap // 3, 2 - tap % 3, lanes) for tap in range(TAPS)
            ]
            x1[bases[b] : bases[b] + rows_of[b], lanes] = dot_nt(
                jnp.concatenate(parts, axis=1),
                jnp.concatenate([bd2[h, tap] for tap in range(TAPS)], axis=1),
            )
    x3[...] = dot(mid[...], w_in2[...])
    def first(b, rows, i, carry):
        u = x3[rows, :]
        y = half(4, u)
        g = x1[rows, :] * half_silu_grad(y, jnp.tanh(y))
        x1[rows, :] = g
        return carry[0] + fold(g), carry[1] + fold(g * (u - row(4, 0)))
    local = [down_to_row(v) for v in each(first, (zero8, zero8))]
    put_norm_grads(dnorms2, 0, 4, *local)
    begun = begin_sum(local)
    for h, lanes in enumerate(lane_halves):
        source = jnp.concatenate(
            [window(h1b_bases[b], sides[b] + 2, b, 1, 1, lanes) for b in buckets], axis=0
        )
        for tap in range(TAPS):
            target = jnp.concatenate(
                [window(g2b_bases[b], sides[b] + 2, b, 2 - tap // 3, 2 - tap % 3, lanes) for b in buckets],
                axis=0,
            )
            acc[tap, h] = diagonal(dot_tn(source, target))
    set_grad(4, *finish_sum(begun), live)
    def first_u(b, rows, i, carry):
        pool[aligned(rows.start + g3b, rows.size), :] = grad_u(x1[rows, :], x3[rows, :], b)
        return carry
    each(first_u, 0)
    x2[...] = x2[...] + dot_nt(pool[g3b : g3b + total, :], w_in2[...])

    x3[...] = dot(h2[...], w_out1[...])
    x1[...] = dot(acts[0], w_short[...])
    def joined(b, rows, i, carry):
        u, s = x3[rows, :], x1[rows, :]
        y = half(2, u) + half(3, s)
        g = x2[rows, :] * half_silu_grad(y, jnp.tanh(y))
        x2[rows, :] = g
        return (
            carry[0] + fold(g),
            carry[1] + fold(g * (u - row(2, 0))),
            carry[2] + fold(g * (s - row(3, 0))),
        )
    local = [down_to_row(v) for v in each(joined, (zero8, zero8, zero8))]
    put_norm_grads(dnorms1, 2, 2, local[0], local[1])
    put_norm_grads(dnorms1, 3, 3, local[0], local[2])
    begun = begin_sum(local[:2])
    short = begin_sum(local[2:], 3)
    dw_in2[...] = dot_tn(mid[...], pool[g3b : g3b + total, :])
    g2_bases, g1_at = geo.grid(1, 1, 0)
    back = SecondScatter(
        info, places, pool, g1_at, h2b, (far_core, far_chip_send, far_chip_recv, far_line_send, far_line_recv)
    )
    back.begin(shares, acc, grads2)
    sums = finish_sum(begun)
    set_grad(2, *sums, live)
    sum_g = sums[0]
    def third_one(b, rows, i, carry):
        pool[rows, :] = grad_u(x2[rows, :], x3[rows, :], b)
        return carry
    each(third_one, 0)
    x3[...] = dot_nt(pool[0:total, :], w_out1[...])
    local = squeeze_excite_back(x3, x0, 1, down1, up1, se1, sq1, ddown1, ddownb1, dup1, dupb1)
    put_norm_grads(dnorms1, 1, 1, *local)
    begun = begin_sum(local)
    set_grad(3, sum_g, *finish_sum(short), live, 51)
    def shortcut(b, rows, i, carry):
        mid[rows, :] = grad_u(x2[rows, :], x1[rows, :], b, 51)
        return carry
    each(shortcut, 0)
    puts = [
        pltpu.make_async_copy(mid.at[pl.ds(bases[b], rows_of[b])], gs_hbm[b], sems.at[2 + b]) for b in buckets
    ]
    for put in puts:
        put.start()
    dw_short[...] = dot_tn(acts[0], mid[...])
    dw_out1[...] = dot_tn(h2[...], pool[0:total, :])
    set_grad(1, *finish_sum(begun), live)
    def second_one(b, rows, i, carry):
        start = g2_bases[b] + (i * (sides[b] + 1)) * 16
        pool[aligned(start, sides[b] * 16), :] = grad_u(x3[rows, :], x0[rows, :], b)
        return carry
    each(second_one, 0)
    for b in buckets:
        fill_halo(g2_bases[b], b, 0, 1, 0, 1)

    def group_grads(taps, b, h2_at):
        for h, lanes in enumerate(lane_halves):
            source = h2[h2_at : h2_at + rows_of[b], lanes]
            for tap in taps:
                target = window(g2_bases[b], sides[b] + 1, b, int(tap // 3 == 0), int(tap % 3 == 0), lanes)
                if b == 0:
                    acc[tap, h] = diagonal(dot_tn(source, target))
                else:
                    acc[tap, h] += diagonal(dot_tn(source, target))

    back.across_chips()
    carry = (zero8, zero8)
    kept = [x1, x2, x3]
    apart = max(rows_of[:-1])
    for plane, (pr, pc) in enumerate(planes):
        taps = [
            tap for tap in range(TAPS) if int(tap // 3 != 1) == pr and int(tap % 3 != 1) == pc
        ]
        for b in buckets:
            side = sides[b]
            pieces = [(0, side)]
            if plane == 3 and rows_of[b] > apart:
                pieces = [(0, side // 2), (side // 2, side)]
            h2_at = bases[b] if plane == 3 else 0
            for first_line, end_line in pieces:
                at, size = first_line * side * 16, (end_line - first_line) * side * 16
                x0[0:size, :] = dot(acts[plane, bases[b] + at : bases[b] + at + size, :], w_in1[...])
                grads_at, grads = (bases[b], kept[plane]) if plane < 3 else (apart, x0)
                for h, lanes in enumerate(lane_halves):
                    parts = [
                        window(
                            g2_bases[b], side + 1, b, int(tap // 3 == 0), int(tap % 3 == 0), lanes,
                            range(first_line, end_line),
                        )
                        for tap in taps
                    ]
                    grads[grads_at : grads_at + size, lanes] = dot_nt(
                        jnp.concatenate(parts, axis=1), jnp.concatenate([bd1[h, tap] for tap in taps], axis=1)
                    )
                def line(i, sums, b=b, plane=plane, at=at, h2_at=h2_at, grads=grads, grads_at=grads_at):
                    size = sides[b] * 16
                    u = x0[aligned(i * size, size), :]
                    y = half(0, u)
                    tan = jnp.tanh(y)
                    h2[aligned(h2_at + at + i * size, size), :] = masked(y + y * tan, b).astype(BF16)
                    here = aligned(grads_at + i * size, size)
                    g = grads[here, :] * half_silu_grad(y, tan)
                    if plane < 3:
                        grads[here, :] = g
                    else:
                        start = g1_at + plane * total + bases[b] + at + i * size
                        pool[aligned(start, size), :] = g.astype(BF16)
                    return sums[0] + fold(g), sums[1] + fold(g * (u - row(0, 0)))
                carry = lax.fori_loop(0, end_line - first_line, line, carry)
            if plane < 3:
                group_grads(taps, b, 0)
        if plane == 1:
            back.along_line()
    local = [down_to_row(v) for v in carry]
    put_norm_grads(dnorms1, 0, 0, *local)
    begun = begin_sum(local)
    for b in buckets:
        group_grads(taps, b, bases[b])
    back.finish(second_out)
    put_group1 = pltpu.make_async_copy(acc, dwg1_hbm, sems.at[1])
    put_group1.start()
    set_grad(0, *finish_sum(begun), 4.0 * live)
    for plane in range(4):
        x0[...] = dot(acts[plane], w_in1[...])
        at = g1_at + plane * total
        def first_one(b, rows, i, carry, at=at, plane=plane):
            here = aligned(rows.start + at, rows.size)
            g = kept[plane][rows, :] if plane < 3 else pool[here, :].astype(F32)
            pool[here, :] = grad_u(g, x0[rows, :], b)
            return carry
        each(first_one, 0)
        part = dot_tn(acts[plane], pool[at : at + total, :])
        if plane == 0:
            dw_in1[...] = part
        else:
            dw_in1[...] += part
        for b in buckets:
            put = pltpu.make_async_copy(
                pool.at[pl.ds(at + bases[b], rows_of[b])], g1_hbm[b].at[plane], sems.at[5 + 3 * plane + b]
            )
            put.start()
            puts.append(put)
    for put in puts:
        put.wait()
    put_group1.wait()


def whole():
    return pl.BlockSpec(memory_space=pltpu.VMEM)


def anywhere():
    return pl.BlockSpec(memory_space=pl.ANY)


def shape(dims, dtype=F32):
    return jax.ShapeDtypeStruct(dims, dtype)


def blocks(geo, infos, acts, mask, count, first, line2, cot):
    groups, inner = lax.axis_size("dp"), lax.axis_size("fsdp")
    total = geo.total
    ins = [acts, mask, count, *first, line2, cot]
    info = infos[1]
    hbm_outs = [
        *[shape((rows, WIDTH), BF16) for rows in geo.rows],
        *[shape((4, rows, WIDTH), BF16) for rows in geo.rows],
        *[shape((rows, WIDTH), BF16) for rows in geo.rows],
        shape((TAPS, 2, HALF, 128)),
    ]
    vmem_outs = [shape((info.share, 128))]
    vmem_outs += [shape(d) for j, d in enumerate(shapes_of(True)) if j != 1]
    second = shapes_of(False)
    pool_rows = 0
    for pr, pc in ((0, 0), (0, 1), (1, 0), (1, 1)):
        pool_rows = geo.grid(pr, pc, pool_rows)[1]
    pool_rows = pool_rows + groups * info.block
    pool_rows = max(
        pool_rows, geo.grid(2, 2, geo.grid(2, 2, 0)[1])[1] + 2 * total, geo.grid(1, 1, 0)[1] + 4 * total
    )
    stages = exchange_stages(groups, inner)
    big = pltpu.VMEM((total, WIDTH), F32)
    scratch = [pltpu.VMEM(second[0], BF16), pltpu.VMEM((2, TAPS, HALF, HALF), BF16)]
    scratch += [pltpu.VMEM(d, F32 if d[0] == 1 else BF16) for d in second[2:-1]] + [pltpu.VMEM(second[-1], F32)]
    scratch += [pltpu.VMEM(d, F32) for j, d in enumerate(second) if j != 1]
    chips = groups // 2
    scratch += [
        pltpu.VMEM(acts.shape, BF16), pltpu.SemaphoreType.DMA((4,)),
        pltpu.VMEM((WIDTH, 128), F32), pltpu.VMEM((2, info.padded, 128), F32),
        pltpu.VMEM((pool_rows, WIDTH), BF16), big, big, big, big,
        pltpu.VMEM((total, WIDTH), BF16), pltpu.VMEM((total, WIDTH), BF16),
        pltpu.VMEM((TAPS, 2, HALF, 128), F32), pltpu.VMEM((104, WIDTH), F32),
        pltpu.VMEM((2, 48, WIDTH), F32), pltpu.VMEM((48, SQUEEZE_A), F32),
        pltpu.VMEM((2, 48, WIDTH), F32), pltpu.VMEM((48, SQUEEZE_B), F32),
        pltpu.VMEM((4 * len(stages), 8, 128), F32),
        pltpu.VMEM((4 * len(stages), max(stages) - 1, 8, 128), F32),
        pltpu.SemaphoreType.DMA((4 * len(stages),)), pltpu.SemaphoreType.DMA((4 * len(stages),)),
        pltpu.SemaphoreType.DMA((17,)),
    ]
    scratch += [
        pltpu.SemaphoreType.DMA(dims)
        for dims in (
            (chips - 1,), (chips - 1,), (chips,), (), (2,), (chips - 1,), (chips - 1,), (inner - 1,), (inner - 1,)
        )
    ]
    outs = pl.pallas_call(
        functools.partial(body, geo, info, groups, inner),
        out_shape=hbm_outs + vmem_outs,
        in_specs=[anywhere()] + [whole()] * 12 + [anywhere()],
        out_specs=[anywhere()] * len(hbm_outs) + [whole()] * len(vmem_outs),
        scratch_shapes=scratch,
        compiler_params=pltpu.CompilerParams(
            collective_id=0, has_side_effects=True, vmem_limit_bytes=LIMIT
        ),
    )(*ins)
    first_grads = [outs[11], outs[9], *outs[12:]]
    return outs[0:3], outs[3:6], outs[6:9], first_grads, outs[10].reshape(-1)


class Flat:
    def __init__(self, is_first, full_length, devices, inner):
        self.shapes = shapes_of(is_first)
        self.starts = []
        offset = 0
        for dims in self.shapes:
            self.starts.append(offset // 128)
            offset = offset + math.prod(dims)
        self.skew = offset % 128
        self.used = offset
        self.rows = full_length // 128
        self.share = self.rows // devices
        self.padded = -(-(self.share + 3) // 16) * 16
        self.layers = -(-inner // 4)
        self.block = self.layers * self.padded


def first_lanes(limit, dims):
    return lax.broadcasted_iota(jnp.int32, dims, 1) < limit


def column_pick(b):
    row = lax.broadcasted_iota(jnp.int32, (384, SQUEEZE_A), 0)
    column = lax.broadcasted_iota(jnp.int32, (384, SQUEEZE_A), 1)
    return (row == column + SQUEEZE_A * b).astype(F32)


def unskew(info, flat):
    row = info.starts[4]
    while row < info.rows:
        size = min(256, info.rows - row)
        here = pltpu.roll(flat[row : row + size, :], 128 - info.skew, 1)
        after = pltpu.roll(flat[row + 1 : row + size + 1, :], 128 - info.skew, 1)
        flat[row : row + size, :] = jnp.where(first_lanes(128 - info.skew, (size, 128)), here, after)
        row = row + size


def reskew(info, flat):
    row = info.rows
    first = info.starts[4]
    while row > first:
        size = min(256, row - first)
        start = row - size
        here = pltpu.roll(flat[start:row, :], info.skew, 1)
        if start == first:
            ahead = pltpu.roll(flat[start : row, :], info.skew, 1)
            ahead = pltpu.roll(ahead, 1, 0)
            keep = flat[info.rows + 8 : info.rows + 9, :]
            is_top = lax.broadcasted_iota(jnp.int32, (size, 128), 0) == 0
            ahead = jnp.where(is_top, jnp.broadcast_to(keep, (size, 128)), ahead)
        else:
            ahead = pltpu.roll(flat[start - 1 : row - 1, :], info.skew, 1)
        flat[start:row, :] = jnp.where(first_lanes(info.skew, (size, 128)), ahead, here)
        row = start


def unpack(info, flat, block_pad, outs):
    def wide(out, start):
        rows = out.shape[0]
        for c in range(4):
            out[:, c * 128 : (c + 1) * 128] = flat[pl.ds(start + c, rows, stride=4), :].astype(out.dtype)

    starts = info.starts
    w_in, bd, down, downb, up, upb, w_out = outs[:7]
    wide(w_in, starts[0])
    row = lax.broadcasted_iota(jnp.int32, (128, HALF), 0) // 32
    lane = lax.broadcasted_iota(jnp.int32, (128, HALF), 1) // GROUP_WIDTH
    on_diagonal = (row == lane).astype(F32)

    def spread(index, carry):
        rows = flat[pl.ds(pl.multiple_of(starts[1] + index * 128, 8), 128), :]
        turned = pltpu.roll(rows, GROUP_WIDTH, 1)
        left = first_lanes(GROUP_WIDTH, (128, 128))
        for parity, pair in enumerate((jnp.where(left, rows, turned), jnp.where(left, turned, rows))):
            tiled = jnp.concatenate([pair, pair], axis=1) * on_diagonal
            block_pad[pl.ds(parity, 128, stride=2), :] = tiled[:, :128]
            block_pad[pl.ds(HALF + parity, 128, stride=2), :] = tiled[:, 128:]
        bd[index % 2, index // 2, :, 0:128] = block_pad[0:HALF, :].astype(BF16)
        bd[index % 2, index // 2, :, 128:HALF] = block_pad[HALF : 2 * HALF, :].astype(BF16)
        return carry

    lax.fori_loop(0, 2 * TAPS, spread, 0)
    if down.shape[1] == 128:
        down[...] = flat[starts[2] : starts[2] + WIDTH, :].astype(BF16)
    else:
        joined = jnp.concatenate([flat[pl.ds(starts[2] + q, 64, stride=3), :] for q in range(3)], axis=1)
        for b in range(8):
            block_pad[pl.ds(b, 64, stride=8), 0:SQUEEZE_A] = dot(joined, column_pick(b))
        down[...] = block_pad[:, 0:SQUEEZE_A].astype(BF16)
    downb[...] = flat[starts[3] : starts[3] + 1, 0 : downb.shape[1]]
    if info.skew:
        unskew(info, flat)
    wide(up, starts[4])
    upb[...] = jnp.concatenate([flat[starts[5] + c : starts[5] + c + 1, :] for c in range(4)], axis=1)
    wide(w_out, starts[6])
    if len(outs) == 9:
        wide(outs[7], starts[7])
    wide(outs[-1], starts[-1])


def pack(info, flat, grads):
    def wide(value, start):
        rows = value.shape[0]
        for c in range(4):
            flat[pl.ds(start + c, rows, stride=4), :] = value[:, c * 128 : (c + 1) * 128]

    starts = info.starts
    d_in, dwg, ddown, ddownb, dup, dupb, d_out = grads[:7]
    flat[info.used // 128 // 8 * 8 : info.rows, :] = jnp.zeros_like(flat[info.used // 128 // 8 * 8 : info.rows, :])
    wide(d_in, starts[0])
    group_odd = lax.broadcasted_iota(jnp.int32, (128, 128), 0) // 32 % 2 == 1
    left = first_lanes(GROUP_WIDTH, (128, 128))

    def collect(index, carry):
        even = dwg[index // 2, index % 2, pl.ds(0, 128, stride=2), :]
        odd = dwg[index // 2, index % 2, pl.ds(1, 128, stride=2), :]
        even_turned, odd_turned = pltpu.roll(even, GROUP_WIDTH, 1), pltpu.roll(odd, GROUP_WIDTH, 1)
        rows = jnp.where(
            group_odd, jnp.where(left, even_turned, odd), jnp.where(left, even, odd_turned)
        )
        flat[pl.ds(pl.multiple_of(starts[1] + index * 128, 8), 128), :] = rows
        return carry

    lax.fori_loop(0, 2 * TAPS, collect, 0)
    if ddown.shape[1] == 128:
        flat[starts[2] : starts[2] + WIDTH, :] = ddown[...]
    else:
        joined = sum(
            exact(ddown[pl.ds(b, 64, stride=8), :], column_pick(b), ((1,), (1,))) for b in range(8)
        )
        for q in range(3):
            flat[pl.ds(starts[2] + q, 64, stride=3), :] = joined[:, q * 128 : (q + 1) * 128]
    wide(dup, starts[4])
    for c in range(4):
        flat[starts[5] + c : starts[5] + c + 1, :] = dupb[:, c * 128 : (c + 1) * 128]
    wide(d_out, starts[6])
    if len(grads) == 9:
        wide(grads[7], starts[7])
    wide(grads[-1], starts[-1])
    if info.skew:
        flat[info.rows + 8 : info.rows + 9, 0 : ddownb.shape[1]] = ddownb[...]
        reskew(info, flat)
    else:
        flat[starts[3] : starts[3] + 1, :] = ddownb[...]


class Places:
    def __init__(self, groups, inner):
        self.outer, self.inner = lax.axis_index("dp"), lax.axis_index("fsdp")
        self.chips, self.lines = groups // 2, inner
        self.chip, self.core = self.outer // 2, lax.rem(self.outer, 2)

    def along(self, step):
        return lax.rem(self.inner + step, self.lines)

    def across(self, step):
        return lax.rem(self.chip + step, self.chips)

    def line(self, step):
        return (self.outer, self.along(step))

    def other_chip(self, step):
        return (2 * self.across(step) + self.core, self.inner)

    def sibling(self):
        return (2 * self.chip + 1 - self.core, self.inner)

    def greet(self, barrier):
        for step in range(1, self.lines):
            pl.semaphore_signal(barrier, inc=1, device_id=self.line(step), device_id_type=MESH)
        for step in range(1, self.chips):
            pl.semaphore_signal(barrier, inc=1, device_id=self.other_chip(step), device_id_type=MESH)
        pl.semaphore_signal(barrier, inc=1, device_id=self.sibling(), device_id_type=MESH)

    def greeted(self, barrier):
        pl.semaphore_wait(barrier, self.lines + self.chips - 1)


def remote(source, target, send_sem, recv_sem, device):
    return pltpu.make_async_remote_copy(
        src_ref=source, dst_ref=target, send_sem=send_sem, recv_sem=recv_sem, device_id=device, device_id_type=MESH
    )


def lane_tile(c):
    return slice(128 * c, 128 * c + 128)


def quarters(info, d):
    start = info.share * d
    for c in range(4):
        first = (c - start) % 4
        yield c, first, (start + first) // 4, -(-(info.share - first) // 4)


class SecondGather:
    def __init__(self, info, places, line, pool, start, semaphores):
        self.info, self.places, self.line, self.pool, self.start = info, places, line, pool, start
        self.chip_send, self.chip_recv, self.core_send, self.core_land = semaphores
        self.started = []

    def block(self, core, chip):
        row = self.start + (core * self.places.chips + chip) * self.info.block
        return self.pool.at[aligned(row, self.info.block)]

    def begin(self):
        places = self.places
        mine = self.block(places.core, places.chip)
        mine[...] = self.line[...]
        for step in range(1, places.chips):
            self.started.append(
                remote(
                    self.line, mine, self.chip_send.at[step - 1], self.chip_recv.at[step - 1], places.other_chip(step)
                )
            )
        self.started.append(remote(self.line, mine, self.core_send.at[0], self.core_land, places.sibling()))
        for copy in self.started:
            copy.start()

    def pass_on(self):
        places = self.places
        for step in range(1, places.chips):
            self.started[step - 1].wait_recv()
            landed = self.block(places.core, places.across(places.chips - step))
            copy = remote(landed, landed, self.core_send.at[step], self.core_land, places.sibling())
            copy.start()
            self.started.append(copy)

    def finish(self, flat, shares, tall, weights):
        info, places = self.info, self.places
        half_rows = places.chips * info.block
        half = self.pool.at[pl.ds(self.start, half_rows)]
        pltpu.make_async_copy(half, half, self.core_land).wait()
        for copy in self.started:
            copy.wait_send()
        for d in range(2 * places.chips * places.lines):
            z, outer = d % places.lines, d // places.lines
            row = self.start + (outer % 2 * places.chips + outer // 2) * info.block + z // 4 * info.padded
            share = shares.at[d % 2]
            share[...] = self.pool[row : row + info.padded, lane_tile(z % 4)].astype(F32)
            for c, first, at, rows in quarters(info, d):
                flat[at : at + rows, lane_tile(c)] = share[pl.ds(first, rows, stride=4), :]
        w_in, bd, down, downb, up, upb, w_out, norms = weights
        w_in[...] = flat[0:WIDTH, :].astype(BF16)
        at = WIDTH
        row = lax.broadcasted_iota(jnp.int32, (32, HALF), 0) // 8
        lane = lax.broadcasted_iota(jnp.int32, (32, HALF), 1) // GROUP_WIDTH
        on_diagonal = (row == lane).astype(F32)

        def spread(index, carry):
            for c in range(4):
                rows = flat[pl.ds(pl.multiple_of(at + index * 32, 8), 32), lane_tile(c)]
                turned = pltpu.roll(rows, GROUP_WIDTH, 1)
                left = first_lanes(GROUP_WIDTH, (32, 128))
                for parity, pair in enumerate((jnp.where(left, rows, turned), jnp.where(left, turned, rows))):
                    tiled = jnp.concatenate([pair, pair], axis=1) * on_diagonal
                    tall[pl.ds(2 * c + parity, 32, stride=8), :] = tiled[:, :128]
                    tall[pl.ds(HALF + 2 * c + parity, 32, stride=8), :] = tiled[:, 128:]
            bd[index % 2, index // 2, :, 0:128] = tall[0:HALF, :].astype(BF16)
            bd[index % 2, index // 2, :, 128:HALF] = tall[HALF : 2 * HALF, :].astype(BF16)
            return carry

        lax.fori_loop(0, 2 * TAPS, spread, 0)
        at = at + TAPS * 64
        for c in range(4):
            tall[pl.ds(c, 128, stride=4), :] = flat[at : at + 128, lane_tile(c)]
        down[...] = tall[...].astype(BF16)
        at = at + 128
        downb[...] = flat[at : at + 1, lane_tile(0)]
        for out in (up, upb, w_out, norms):
            rows = out.shape[0]
            for c in range(4):
                begin = at + (c + 1) // 4
                out[:, lane_tile(c)] = flat[begin : begin + rows, lane_tile((c + 1) % 4)].astype(out.dtype)
            at = at + rows


class SecondScatter:
    def __init__(self, info, places, pool, start, landing, semaphores):
        self.info, self.places, self.pool = info, places, pool
        self.core_sem, self.chip_send, self.chip_recv, self.line_send, self.line_recv = semaphores
        block, chips = info.block, places.chips
        self.core_in = landing
        self.chip_in = self.core_in + chips * block
        self.line_in = self.chip_in + (chips - 1) * block
        self.line_sum = self.line_in + block
        self.parts = start

    def rows(self, start, size):
        return self.pool.at[aligned(start, size)]

    def part(self, core, chip):
        return self.parts + (core * self.places.chips + chip) * self.info.block

    def begin(self, shares, acc, grads):
        info, places = self.info, self.places
        d_in, ddown, ddownb, dup, dupb, d_out, dnorms = grads
        group_odd = lax.broadcasted_iota(jnp.int32, (128, 128), 0) // 32 % 2 == 1
        left = first_lanes(GROUP_WIDTH, (128, 128))

        def collect(index, carry):
            tap, h = index // 2, index % 2
            even, odd = acc[tap, h, pl.ds(0, 128, stride=2), :], acc[tap, h, pl.ds(1, 128, stride=2), :]
            even_turned, odd_turned = pltpu.roll(even, GROUP_WIDTH, 1), pltpu.roll(odd, GROUP_WIDTH, 1)
            acc[tap, h, 0:128, :] = jnp.where(
                group_odd, jnp.where(left, even_turned, odd), jnp.where(left, even, odd_turned)
            )
            return carry

        lax.fori_loop(0, 2 * TAPS, collect, 0)
        pieces = [(0, 4 * WIDTH, d_in, 4)]
        at = 4 * WIDTH
        for index in range(2 * TAPS):
            pieces.append((at, 128, acc.at[index // 2, index % 2], 1))
            at = at + 128
        for value, tiles in ((ddown, 1), (ddownb, 1), (dup, 4), (dupb, 4), (d_out, 4), (dnorms, 4)):
            pieces.append((at, value.shape[0] * tiles, value, tiles))
            at = at + value.shape[0] * tiles
        for d in range(2 * places.chips * places.lines):
            z, outer = d % places.lines, d // places.lines
            share = shares.at[d % 2]
            begin, end = info.share * d, info.share * (d + 1)
            if end > at:
                share[...] = jnp.zeros_like(share)
            for start, rows, value, tiles in pieces:
                low, high = max(begin, start), min(end, start + rows)
                for c in range(tiles):
                    first = low + (c - (low - start)) % tiles
                    number = -(-(high - first) // tiles)
                    if number > 0:
                        row = (first - start) // tiles
                        piece = value[row : row + number, lane_tile(c)]
                        if tiles == 1:
                            share[first - begin : first - begin + number, :] = piece
                        else:
                            share[pl.ds(first - begin, number, stride=tiles), :] = piece
            row = self.part(outer % 2, outer // 2) + z // 4 * info.padded
            self.pool[row : row + info.padded, lane_tile(z % 4)] = share[...].astype(BF16)
        size = places.chips * info.block
        self.core_copy = remote(
            self.rows(self.part(1 - places.core, 0), size),
            self.rows(self.core_in, size),
            self.core_sem.at[0],
            self.core_sem.at[1],
            places.sibling(),
        )
        self.core_copy.start()

    def across_chips(self):
        info, places = self.info, self.places
        self.core_copy.wait_recv()

        def add(index, carry):
            mine = aligned(self.part(places.core, 0) + index * info.padded, info.padded)
            theirs = aligned(self.core_in + index * info.padded, info.padded)
            self.pool[mine, :] = (self.pool[mine, :].astype(F32) + self.pool[theirs, :].astype(F32)).astype(BF16)
            return carry

        lax.fori_loop(0, places.chips * info.layers, add, 0)
        self.copies = []
        for step in range(1, places.chips):
            self.copies.append(
                remote(
                    self.rows(self.part(places.core, places.across(step)), info.block),
                    self.rows(self.chip_in + (step - 1) * info.block, info.block),
                    self.chip_send.at[step - 1],
                    self.chip_recv.at[step - 1],
                    places.other_chip(step),
                )
            )
            self.copies[-1].start()

    def along_line(self):
        info, places = self.info, self.places
        for copy in self.copies:
            copy.wait_recv()
        for layer in range(info.layers):
            at = layer * info.padded
            value = self.pool[aligned(self.part(places.core, places.chip) + at, info.padded), :].astype(F32)
            for step in range(places.chips - 1):
                begin = self.chip_in + step * info.block + at
                value = value + self.pool[begin : begin + info.padded, :].astype(F32)
            self.pool[self.line_sum + at : self.line_sum + at + info.padded, :] = value.astype(BF16)
        self.lines = []
        for step in range(1, places.lines):
            z = places.along(step)
            self.lines.append(
                remote(
                    self.pool.at[
                        aligned(self.line_sum + z // 4 * info.padded, info.padded),
                        pl.ds(pl.multiple_of(lax.rem(z, 4) * 128, 128), 128),
                    ],
                    self.pool.at[
                        pl.ds(self.line_in + (step - 1) // 4 * info.padded, info.padded),
                        lane_tile((step - 1) % 4),
                    ],
                    self.line_send.at[step - 1],
                    self.line_recv.at[step - 1],
                    places.line(step),
                )
            )
            self.lines[-1].start()

    def finish(self, out):
        info, places = self.info, self.places
        z = places.inner
        value = self.pool[
            aligned(self.line_sum + z // 4 * info.padded, info.padded),
            pl.ds(pl.multiple_of(lax.rem(z, 4) * 128, 128), 128),
        ].astype(F32)
        for step in range(1, places.lines):
            self.lines[step - 1].wait_recv()
            begin = self.line_in + (step - 1) // 4 * info.padded
            value = value + self.pool[begin : begin + info.padded, lane_tile((step - 1) % 4)].astype(F32)
        out[...] = value[0 : info.share]
        for copy in [self.core_copy] + self.copies + self.lines:
            copy.wait_send()


def gather_body(geo, infos, groups, inner, *refs):
    images_hbm, cots_hbm, counts = refs[0:3], refs[3:6], refs[6]
    shards = refs[7:9]
    acts_hbm, cot_hbm, mask, live = refs[9:13]
    weights, line_out = refs[13:22], refs[22]
    (
        wide_cell, cot_cell, block_pad, gathered, line_in, flat, stage2,
        line_send, line_recv, chip_send, chip_recv, core_send, core_recv,
        *images_and_cots, acts, cot, load_sem, store_sem,
    ) = refs[23:]
    images, cots = images_and_cots[:3], images_and_cots[3:]
    loads = [
        pltpu.make_async_copy(source, target, load_sem.at[k])
        for k, (source, target) in enumerate(zip([*images_hbm, *cots_hbm], images_and_cots))
    ]
    for load in loads:
        load.start()
    stores = []
    places = Places(groups, inner)
    barrier = pltpu.get_barrier_semaphore()
    places.greet(barrier)
    z = places.inner
    mine = [
        gathered.at[places.chip, places.core, z],
        line_in.at[
            aligned(z // 4 * infos[1].padded, infos[1].padded), pl.ds(pl.multiple_of(lax.rem(z, 4) * 128, 128), 128)
        ],
    ]
    slot = lax.broadcasted_iota(jnp.int32, (16, WIDTH), 0) % 4
    for b in range(3):
        mask[b] = jnp.where(slot < counts[0, b], 1.0, 0.0)
    for k, info in enumerate(infos):
        stage = flat.at[pl.ds(0, info.padded)] if k == 0 else stage2
        stage[info.padded - 16 : info.padded, :] = jnp.zeros((16, 128), F32)
        stage[0 : info.share, :] = shards[k][...]
        for b in range(3):
            value = jnp.broadcast_to(counts[0, b].astype(F32), (1, 128))
            stage[info.share + b : info.share + b + 1, :] = value
        mine[k][...] = stage[...].astype(BF16)
    places.greeted(barrier)
    started = []

    def begin(copy):
        copy.start()
        started.append(copy)
        return copy

    lines = [
        [
            begin(remote(mine[k], mine[k], line_send.at[k, step - 1], line_recv.at[k, step - 1], places.line(step)))
            for step in range(1, inner)
        ]
        for k in range(2)
    ]
    chip_copies = []

    def forward(step):
        if step:
            lines[0][step - 1].wait_recv()
        share = gathered.at[places.chip, places.core, places.along(inner - step)]
        for over in range(1, places.chips):
            at = (over - 1) * inner + step
            chip_copies.append(
                begin(remote(share, share, chip_send.at[at], chip_recv.at[at], places.other_chip(over)))
            )
        begin(remote(share, share, core_send.at[step], core_recv, places.sibling()))

    def pass_on(step):
        for over in range(1, places.chips):
            chip_copies[step * (places.chips - 1) + over - 1].wait_recv()
            share = gathered.at[places.across(places.chips - over), places.core, places.along(inner - step)]
            begin(remote(share, share, core_send.at[over * inner + step], core_recv, places.sibling()))

    def complete():
        half = gathered.at[:, 0]
        pltpu.make_async_copy(half, half, core_recv).wait()
        info = infos[0]
        found = jnp.zeros((3, 128), F32)
        for d in range(groups * inner):
            at = info.share * d
            piece = gathered[d // inner // 2, d // inner % 2, d % inner].astype(F32)
            flat[at : at + info.share, :] = piece[0 : info.share]
            found = found + piece[info.share : info.share + 3]
        total = sum(found[b : b + 1, :] * (4.0 * side * side) for b, side in enumerate(geo.sides))
        live[...] = jnp.concatenate([total] * 4, axis=1)
        unpack(info, flat, block_pad, weights)
        for copy in lines[1]:
            copy.wait_recv()
        line_out[...] = line_in[...]

    def arrange(b):
        side = geo.sides[b]
        size = side * 16

        def line(i, carry):
            rows = aligned(geo.bases[b] + i * size, size)
            for pr in range(2):
                for pc in range(2):
                    for q in range(4):
                        wide_cell[0:side, 4 * q : 4 * q + 4, :] = images[b][q // 2, i, pr, q % 2, :, pc].astype(F32)
                    value = wide_cell[0:side] * mask[b][None, :, :WIDTH_IN]
                    acts[2 * pr + pc, rows, :] = value.reshape(size, WIDTH_IN).astype(BF16)
            for q in range(4):
                cot_cell[0:side, 4 * q : 4 * q + 4, :] = cots[b][q // 2, i, q % 2].astype(F32)
            value = cot_cell[0:side] * mask[b][None]
            cot[rows, :] = value.reshape(size, WIDTH).astype(BF16)
            return carry

        loads[b].wait()
        loads[3 + b].wait()
        lax.fori_loop(0, side, line, 0)
        some = pl.ds(geo.bases[b], geo.rows[b])
        stores.append(pltpu.make_async_copy(acts.at[:, some], acts_hbm.at[:, some], store_sem.at[2 * b]))
        stores.append(pltpu.make_async_copy(cot.at[some], cot_hbm.at[some], store_sem.at[2 * b + 1]))
        for store in stores[-2:]:
            store.start()

    forward(0)
    arrange(0)
    for step in range(1, inner):
        forward(step)
    arrange(1)
    pass_on(0)
    arrange(2)
    for step in range(1, inner):
        pass_on(step)
    complete()
    for store in stores:
        store.wait()
    for copy in started:
        copy.wait_send()


def gather(geo, infos, images, cots, counts, shards):
    groups, inner = lax.axis_size("dp"), lax.axis_size("fsdp")
    ins = [*images, *cots, counts, *[shard.reshape(-1, 128) for shard in shards]]
    outs = [shape((4, geo.total, WIDTH_IN), BF16), shape((geo.total, WIDTH), BF16)]
    outs += [shape((3, 16, WIDTH)), shape((1, WIDTH))]
    for is_first in (True,):
        dims = shapes_of(is_first)
        outs += [shape(dims[0], BF16), shape((2, TAPS, HALF, HALF), BF16)]
        outs += [shape(d, F32 if d[0] == 1 else BF16) for d in dims[2:-1]] + [shape(dims[-1])]
    outs += [shape((infos[1].block, WIDTH), BF16)]
    side = max(geo.sides)
    scratch = [
        pltpu.VMEM((side, 16, WIDTH_IN), F32), pltpu.VMEM((side, 16, WIDTH), F32), pltpu.VMEM((2 * HALF, 128), F32),
    ]
    scratch += [
        pltpu.VMEM((groups // 2, 2, inner, infos[0].padded, 128), BF16), pltpu.VMEM((infos[1].block, WIDTH), BF16),
        pltpu.VMEM((infos[0].rows + 16, 128), F32), pltpu.VMEM((infos[1].padded, 128), F32),
    ]
    chips = groups // 2
    scratch += [
        pltpu.SemaphoreType.DMA(dims)
        for dims in (
            (2, inner - 1), (2, inner - 1), ((chips - 1) * inner,), ((chips - 1) * inner,), (chips * inner,), ()
        )
    ]
    scratch += [pltpu.VMEM(value.shape, BF16) for value in ins[:6]]
    scratch += [pltpu.VMEM(value.shape, BF16) for value in outs[:2]]
    scratch += [pltpu.SemaphoreType.DMA((6,)), pltpu.SemaphoreType.DMA((6,))]
    results = pl.pallas_call(
        functools.partial(gather_body, geo, infos, groups, inner),
        out_shape=outs,
        in_specs=[anywhere()] * 6 + [pl.BlockSpec(memory_space=pltpu.SMEM)] + [whole()] * 2,
        out_specs=[anywhere()] * 2 + [whole()] * (len(outs) - 2),
        scratch_shapes=scratch,
        compiler_params=pltpu.CompilerParams(
            collective_id=1, has_side_effects=True, vmem_limit_bytes=LIMIT
        ),
    )(*ins)
    return results[:4], results[4:13], results[13]


def scatter_body(info, groups, inner, *refs):
    grads, out = refs[0:9], refs[9]
    flat, parts, core_in, chip_sum, chip_in, line_sum, line_in = refs[10:17]
    core_send, core_recv, chip_send, chip_recv, line_send, line_recv = refs[17:]
    places = Places(groups, inner)
    barrier = pltpu.get_barrier_semaphore()
    places.greet(barrier)
    devices = groups * inner
    pack(info, flat, grads)
    for d in range(devices):
        place = parts.at[d // inner % 2, d // inner // 2, d % inner]
        place[0 : info.padded, :] = flat[info.share * d : info.share * d + info.padded, :].astype(BF16)
    places.greeted(barrier)
    core = remote(parts.at[1 - places.core], core_in, core_send, core_recv, places.sibling())
    core.start()
    core.wait_recv()

    def add(index, carry):
        chip, z = index // inner, index % inner
        chip_sum[chip, z] = (parts[places.core, chip, z].astype(F32) + core_in[chip, z].astype(F32)).astype(BF16)
        return carry

    lax.fori_loop(0, places.chips * inner, add, 0)
    copies = []
    for step in range(1, places.chips):
        copies.append(
            remote(chip_sum.at[places.across(step)], chip_in.at[step - 1], chip_send.at[step - 1], chip_recv.at[step - 1], places.other_chip(step))
        )
        copies[-1].start()
    for copy in copies:
        copy.wait_recv()

    def add_chips(z, carry):
        value = chip_sum[places.chip, z].astype(F32)
        for step in range(places.chips - 1):
            value = value + chip_in[step, z].astype(F32)
        line_sum[z] = value.astype(BF16)
        return carry

    lax.fori_loop(0, inner, add_chips, 0)
    lines = []
    for step in range(1, inner):
        lines.append(
            remote(line_sum.at[places.along(step)], line_in.at[step - 1], line_send.at[step - 1], line_recv.at[step - 1], places.line(step))
        )
        lines[-1].start()
    for copy in lines:
        copy.wait_recv()
    value = line_sum[places.inner].astype(F32)
    for step in range(inner - 1):
        value = value + line_in[step].astype(F32)
    out[...] = value[0 : info.share, :]
    core.wait_send()
    for copy in copies + lines:
        copy.wait_send()


def scatter(info, ins):
    groups, inner = lax.axis_size("dp"), lax.axis_size("fsdp")
    chips = groups // 2
    size = info.padded
    def part(*lead):
        return pltpu.VMEM((*lead, size, 128), BF16)
    out = pl.pallas_call(
        functools.partial(scatter_body, info, groups, inner),
        out_shape=shape((info.share, 128)),
        in_specs=[whole()] * len(ins),
        out_specs=whole(),
        scratch_shapes=[
            pltpu.VMEM((info.rows + 16, 128), F32),
            part(2, chips, inner), part(chips, inner), part(chips, inner), part(chips - 1, inner), part(inner),
            part(inner - 1),
        ]
        + [pltpu.SemaphoreType.DMA(dims) for dims in ((), (), (chips - 1,), (chips - 1,), (inner - 1,), (inner - 1,))],
        compiler_params=pltpu.CompilerParams(
            collective_id=2, has_side_effects=True, vmem_limit_bytes=LIMIT
        ),
    )(*ins)
    return out.reshape(-1)


def restore_body(geo, *refs):
    number = len(geo.sides)
    g1, gs, out = (refs[k * number : (k + 1) * number] for k in range(3))
    w_in, w_short = refs[3 * number : 3 * number + 2]
    rest = refs[3 * number + 2 :]
    output_hbm, grad_hbm = rest[:number], rest[number : 2 * number]
    g1_in, gs_in, out_in, outputs, image_grads = (rest[(k + 2) * number : (k + 3) * number] for k in range(5))
    grad_cell, out_cell, in_sems, out_sems = rest[7 * number :]
    order = list(range(number))[::-1]
    loads, stores = {}, []
    for b in order:
        loads[b] = [
            pltpu.make_async_copy(source, target, in_sems.at[b, k])
            for k, (source, target) in enumerate(((g1[b], g1_in[b]), (gs[b], gs_in[b]), (out[b], out_in[b])))
        ]
        for load in loads[b]:
            load.start()
    for b in order:
        side = geo.sides[b]
        size = side * 16
        for load in loads[b]:
            load.wait()

        def line(i, carry, b=b, side=side, size=size):
            rows = aligned(i * size, size)
            out_cell[0:side] = out_in[b][rows, :].astype(F32).reshape(side, 16, WIDTH)
            for q in range(4):
                outputs[b][q // 2, i, q % 2] = out_cell[0:side, 4 * q : 4 * q + 4, :].astype(BF16)
            value = dot_nt(g1_in[b][:, rows, :].reshape(4 * size, WIDTH), w_in[...])
            grad_cell[:, 0:side] = value.reshape(4, side, 16, WIDTH_IN)
            grad_cell[0, 0:side] += dot_nt(gs_in[b][rows, :], w_short[...]).reshape(side, 16, WIDTH_IN)
            for plane in range(4):
                for q in range(4):
                    image_grads[b][q // 2, i, plane // 2, q % 2, :, plane % 2] = grad_cell[
                        plane, 0:side, 4 * q : 4 * q + 4, :
                    ]
            return carry

        cuts = [0, side // 2, side]
        for k in range(2):
            lax.fori_loop(cuts[k], cuts[k + 1], line, 0)
            some = pl.ds(cuts[k], cuts[k + 1] - cuts[k])
            for j, (source, target) in enumerate(((outputs[b], output_hbm[b]), (image_grads[b], grad_hbm[b]))):
                stores.append(pltpu.make_async_copy(source.at[:, some], target.at[:, some], out_sems.at[b, 2 * k + j]))
                stores[-1].start()
    for store in stores:
        store.wait()


def restore(geo, g1, gs, out, w_in, w_short):
    ins = [*g1, *gs, *out, w_in, w_short]
    sides = geo.sides
    out_dims = [(2, side, 2, side, 4, WIDTH) for side in sides]
    grad_dims = [(2, side, 2, 2, side, 2, 4, WIDTH_IN) for side in sides]
    most = max(sides)
    results = pl.pallas_call(
        functools.partial(restore_body, geo),
        out_shape=[shape(dims, BF16) for dims in out_dims] + [shape(dims) for dims in grad_dims],
        in_specs=[anywhere()] * 9 + [whole()] * 2,
        out_specs=[anywhere()] * 6,
        scratch_shapes=[pltpu.VMEM(value.shape, BF16) for value in ins[:9]]
        + [pltpu.VMEM(dims, BF16) for dims in out_dims]
        + [pltpu.VMEM(dims, F32) for dims in grad_dims]
        + [pltpu.VMEM((4, most, 16, WIDTH_IN), F32), pltpu.VMEM((most, 16, WIDTH), F32)]
        + [pltpu.SemaphoreType.DMA((3, 3)), pltpu.SemaphoreType.DMA((3, 4))],
        compiler_params=pltpu.CompilerParams(vmem_limit_bytes=LIMIT),
    )(*ins)
    grids = [
        result.reshape(scale * side, scale * side, 4, -1).transpose(2, 0, 1, 3)
        for result, side, scale in zip(results, sides * 2, [2] * 3 + [4] * 3)
    ]
    return grids


def per_device(*args):
    images, counts = args[0:3], args[3]
    cots = args[6:9]
    geo = Geometry([image.shape[1] // 4 for image in images])
    inner = lax.axis_size("fsdp")
    devices = lax.axis_size("dp") * inner
    infos = [Flat(k == 0, args[4 + k].shape[0] * devices, devices, inner) for k in range(2)]
    split_images = [
        image.transpose(1, 2, 0, 3).reshape(2, side, 2, 2, side, 2, 4, WIDTH_IN)
        for image, side in zip(images, geo.sides)
    ]
    split_cots = [
        value.transpose(1, 2, 0, 3).reshape(2, side, 2, side, 4, WIDTH) for value, side in zip(cots, geo.sides)
    ]
    (acts, cot, mask, live), first, line2 = gather(geo, infos, split_images, split_cots, counts, args[4:6])
    out, g1, gs, first_grads, second_out = blocks(geo, infos, acts, mask, live, first, line2, cot)
    return (
        *restore(geo, g1, gs, out, first[0], first[7]),
        scatter(infos[0], first_grads),
        second_out,
    )


def solution(mesh):
    images = P(("dp", "fsdp"), None, None, None)
    flat = P(("dp", "fsdp"))
    in_specs = (images, images, images, P(("dp", "fsdp"), None), flat, flat, images, images, images)
    out_specs = (images,) * 6 + (flat, flat)
    return jax.shard_map(per_device, mesh=mesh, in_specs=in_specs, out_specs=out_specs, check_vma=False)
```

```python
import functools
import math

import jax
import jax.numpy as jnp
from jax import lax
from jax.experimental import pallas as pl
from jax.experimental.pallas import tpu as pltpu
from jax.sharding import PartitionSpec as P

WIDTH_IN = 192
GROUPS = 8
GROUP_WIDTH = 64
SQUEEZE_A = 48
SQUEEZE_B = 128
WIDTH = 512
HALF = 256
ALL = slice(0, WIDTH)
HALVES = (slice(0, HALF), slice(HALF, WIDTH))
TAPS = 9
EPSILON = 1e-05
HIGHEST = lax.Precision.HIGHEST
MESH = pl.DeviceIdType.MESH
F32 = jnp.float32
BF16 = jnp.bfloat16
LIMIT = 127 * 2**19


def shapes_of(is_first):
    width_in, squeeze = (WIDTH_IN, SQUEEZE_A) if is_first else (WIDTH, SQUEEZE_B)
    shapes = [
        (width_in, WIDTH),
        (TAPS, GROUPS, GROUP_WIDTH, GROUP_WIDTH),
        (WIDTH, squeeze),
        (1, squeeze),
        (squeeze, WIDTH),
        (1, WIDTH),
        (WIDTH, WIDTH),
    ]
    if is_first:
        shapes.append((WIDTH_IN, WIDTH))
    shapes.append((8 if is_first else 6, WIDTH))
    return shapes


def diagonal(product):
    parts = []
    for g in range(4):
        lanes = slice(128 * (g // 2), 128 * (g // 2) + 128)
        parts.append(product[g * GROUP_WIDTH : (g + 1) * GROUP_WIDTH, lanes])
    return jnp.concatenate(parts, axis=0)


def dot(left, right):
    return jnp.dot(left, right, preferred_element_type=F32)


def dot_nt(left, right):
    return lax.dot_general(left, right, (((1,), (1,)), ((), ())), preferred_element_type=F32)


def dot_tn(left, right):
    return lax.dot_general(left, right, (((0,), (0,)), ((), ())), preferred_element_type=F32)


def exact(left, right, dims):
    return lax.dot_general(
        left, right, (dims, ((), ())), precision=HIGHEST, preferred_element_type=F32
    )


def by_parts(product, left, right):
    high = left.astype(BF16)
    rest = left - high.astype(F32)
    middle = rest.astype(BF16)
    low = (rest - middle.astype(F32)).astype(BF16)
    rows = left.shape[0]
    full = product(jnp.concatenate([high, middle, low], axis=0), right)
    return full[:rows] + full[rows : 2 * rows] + full[2 * rows :]


def half_silu(half):
    return half + half * jnp.tanh(half)


def half_silu_grad(half, tan):
    return (0.5 + 0.5 * tan) * (1.0 + half * (1.0 - tan))


def fold(values):
    return jnp.sum(values.reshape(-1, 8, values.shape[-1]), axis=0)


def down_to_row(values):
    return jnp.sum(values, axis=0, keepdims=True)


class Geometry:
    def __init__(self, sides):
        self.sides = sides
        self.rows = [side * side * 16 for side in sides]
        self.bases = [sum(self.rows[:b]) for b in range(len(sides))]
        self.total = sum(self.rows)

    def grid(self, extra_rows, extra_cols, start):
        bases = []
        for side in self.sides:
            bases.append(start)
            start = start + (side + extra_rows) * (side + extra_cols) * 16
        return bases, start


def exchange_stages(groups, inner):
    return [groups * inner] if groups * inner <= 64 else [inner, groups]


def aligned(start, size):
    if isinstance(start, int):
        return pl.ds(start, size)
    return pl.ds(pl.multiple_of(start, 16), size)


def body(geo, info, groups, inner, *refs):
    (
        acts_hbm, mask, count, w_in1, bd1, down1, downb1, up1, upb1, w_out1, w_short, norms1, line2, cot_hbm,
    ) = refs[:14]
    out_hbm, g1_hbm, gs_hbm = refs[14:17], refs[17:20], refs[20:23]
    (
        dwg1_hbm, second_out,
        dw_in1, ddown1, ddownb1, dup1, dupb1, dw_out1, dw_short, dnorms1,
    ) = refs[23:33]
    weights2, grads2 = refs[33:41], refs[41:48]
    w_in2, bd2, down2, downb2, up2, upb2, w_out2, norms2 = weights2
    dw_in2, ddown2, ddownb2, dup2, dupb2, dw_out2, dnorms2 = grads2
    (
        acts, acts_sem, tall, shares, pool, x0, x1, x2, x3, h2, mid, acc, vec, se1, sq1, se2, sq2,
        pay, slots, send_sem, recv_sem, half_pay, half_slots, half_send, half_recv, sems,
        near_send, near_recv, near_core_send, core_land, far_core, far_chip_send, far_chip_recv, far_line_send, far_line_recv,
    ) = refs[48:]
    exchange = ((pay, slots, send_sem, recv_sem), (half_pay, half_slots, half_send, half_recv))
    places = Places(groups, inner)
    loads = [pltpu.make_async_copy(acts_hbm.at[k], acts.at[k], acts_sem.at[k]) for k in range(4)]
    for load in loads:
        load.start()
    sides, bases, rows_of, total = geo.sides, geo.bases, geo.rows, geo.total
    buckets = range(len(sides))
    devices = groups * inner

    outer_index, inner_index = lax.axis_index("dp"), lax.axis_index("fsdp")

    def any_partner(step):
        other = lax.rem(outer_index * inner + inner_index + step, devices)
        return (other // inner, lax.rem(other, inner))

    def inner_partner(step):
        return (outer_index, lax.rem(inner_index + step, inner))

    def outer_partner(step):
        return (lax.rem(outer_index + step, groups), inner_index)

    barrier = pltpu.get_barrier_semaphore()
    stages = exchange_stages(groups, inner)
    if len(stages) == 1:
        partners = [any_partner]
    else:
        partners = [inner_partner, outer_partner]
    for count_in_stage, partner in zip(stages, partners):

        def greet(step, carry, partner=partner):
            pl.semaphore_signal(barrier, inc=1, device_id=partner(step), device_id_type=MESH)
            return carry

        lax.fori_loop(1, count_in_stage, greet, 0)

    calls = []

    def begin_sum(rows, place=None):
        if not calls:
            pl.semaphore_wait(barrier, sum(stages) - len(stages))
        kind = int(rows[0].shape[1] == HALF)
        if place is None:
            place = calls.count(kind) % (4 if kind else 2)
            calls.append(kind)
        buffers = exchange[kind]
        pay = buffers[0]
        for r, value in enumerate(rows):
            for c in range(value.shape[1] // 128):
                at = r * (value.shape[1] // 128) + c
                pay[place * len(stages), at : at + 1, :] = value[:, lane_tile(c)]
        send_stage(buffers, 0, place * len(stages))
        return kind, place, len(rows)

    def send_stage(buffers, stage, at):
        pay, slots, send_sem, recv_sem = buffers

        def send(step, carry):
            pltpu.make_async_remote_copy(
                src_ref=pay.at[at],
                dst_ref=slots.at[at, step - 1],
                send_sem=send_sem.at[at],
                recv_sem=recv_sem.at[at],
                device_id=partners[stage](step),
                device_id_type=MESH,
            ).start()
            return carry

        lax.fori_loop(1, stages[stage], send, 0)

    def finish_sum(begun):
        kind, place, number = begun
        buffers = exchange[kind]
        pay, slots, send_sem, recv_sem = buffers
        for stage in range(len(stages)):
            at = place * len(stages) + stage
            if stage:
                pay[at] = sums
                send_stage(buffers, stage, at)
            landed = slots.at[at, pl.ds(0, stages[stage] - 1)]
            pltpu.make_async_copy(landed, landed, recv_sem.at[at]).wait()
            sums = pay[at] + jnp.sum(slots[at, 0 : stages[stage] - 1], axis=0)
            pltpu.make_async_copy(landed, landed, send_sem.at[at]).wait()
        tiles = 2 if kind else 4
        return [
            jnp.concatenate([sums[tiles * r + c : tiles * r + c + 1, :] for c in range(tiles)], axis=1)
            for r in range(number)
        ]

    def each(step, carry):
        for b in buckets:
            def line(i, kept, b=b):
                size = sides[b] * 16
                return step(b, aligned(bases[b] + i * size, size), i, kept)
            def pair(j, kept, line=line):
                return line(2 * j + 1, line(2 * j, kept))
            carry = lax.fori_loop(0, sides[b] // 2, pair, carry)
            if sides[b] % 2:
                carry = line(sides[b] - 1, carry)
        return carry

    zero8 = jnp.zeros((8, WIDTH), F32)

    zero_half = jnp.zeros((8, HALF), F32)

    def masked(values, b):
        width = values.shape[-1]
        return (values.reshape(-1, 16, width) * mask[b, :, 0:width][None]).reshape(values.shape)

    def set_norm(k, sums, squares, norms, index, live, lanes=ALL):
        live = live[:, lanes]
        mean = sums / live
        inv_std = lax.rsqrt(squares / live - mean * mean + EPSILON)
        scale = inv_std * norms[2 * index : 2 * index + 1, lanes]
        offset = norms[2 * index + 1 : 2 * index + 2, lanes] - mean * scale
        for r, value in enumerate((mean, inv_std, scale, offset, 0.5 * scale, 0.5 * offset)):
            vec[6 * k + r : 6 * k + r + 1, lanes] = value

    def row(k, r, lanes=ALL):
        return vec[6 * k + r : 6 * k + r + 1, lanes]

    def half(k, u, lanes=ALL):
        return u * row(k, 4, lanes) + row(k, 5, lanes)

    def set_grad(k, sum_g, sum_d, live, at=48, lanes=ALL):
        live = live[:, lanes]
        scale, inv_std = row(k, 2, lanes), row(k, 1, lanes)
        on_u = -scale * inv_std * inv_std * sum_d / live
        vec[at : at + 1, lanes] = scale
        vec[at + 1 : at + 2, lanes] = on_u
        vec[at + 2 : at + 3, lanes] = -scale * sum_g / live - row(k, 0, lanes) * on_u

    def grad_u(g, u, b, at=48, lanes=ALL):
        inner_grad = g * vec[at : at + 1, lanes] + (u * vec[at + 1 : at + 2, lanes] + vec[at + 2 : at + 3, lanes])
        return masked(inner_grad, b).astype(BF16)

    def keep_and_fold(x, rows, lanes, u, carry):
        x[rows, lanes] = u
        return carry[0] + fold(u), carry[1] + fold(u * u)

    def begin_stats(carry):
        return begin_sum([down_to_row(v) for v in carry])

    def begin_dot_stats(x, left, weight):
        begun = []
        for lanes in HALVES:
            carry = (zero_half, zero_half)
            for rows in (slice(0, bases[-1]), slice(bases[-1], total)):
                carry = keep_and_fold(x, rows, lanes, dot(left[rows, :], weight[:, lanes]), carry)
            begun.append(begin_stats(carry))
        return begun

    def window(base, width, b, r0, c0, lanes, lines=None):
        side = sides[b]
        return jnp.concatenate(
            [
                pool[base + ((r0 + i) * width + c0) * 16 : base + ((r0 + i) * width + c0 + side) * 16, lanes]
                for i in lines or range(side)
            ],
            axis=0,
        )

    def pattern(size, bit, value):
        index = lax.broadcasted_iota(jnp.int32, (size, HALF), 0)
        return ((index // bit) % 2 == value).astype(F32)

    def fill_halo(base, b, low_r, high_r, low_c, high_c, lanes):
        side = sides[b]
        width = side + low_c + high_c
        def cell(r, c, n=1):
            return slice(base + (r * width + c) * 16, base + (r * width + c + n) * 16)
        def shifted(source, target, shift, keep):
            value = pool[source, lanes].astype(F32)
            pool[target, lanes] = (pltpu.roll(value, shift, 0) * keep).astype(BF16)
        for i in range(side):
            r = i + low_r
            if low_c:
                shifted(cell(r, side), cell(r, 0), 4, pattern(16, 4, 1))
            if high_c:
                shifted(cell(r, low_c), cell(r, width - 1), 12, pattern(16, 4, 0))
        size = width * 16
        if low_r:
            shifted(cell(side, 0, width), cell(0, 0, width), 8, pattern(size, 8, 1))
        if high_r:
            shifted(cell(low_r, 0, width), cell(low_r + side, 0, width), size - 8, pattern(size, 8, 0))

    first_of_image = (lax.broadcasted_iota(jnp.int32, (48, WIDTH), 0) % 16 < 4).astype(F32)

    def over_quadrants(v):
        return v + pltpu.roll(v, 4, 0) + pltpu.roll(v, 8, 0) + pltpu.roll(v, 12, 0)

    def squeeze_excite(x, k, begun, norms, down, downb, up, upb, se, sq):
        zero16 = jnp.zeros((16, HALF), F32)
        found = []
        for lanes, part in zip(HALVES, begun):
            set_norm(k, *finish_sum(part), norms, 1, live, lanes)
            def step(b, rows, i, carry, lanes=lanes):
                v = half_silu(half(k, x[rows, lanes], lanes)).reshape(-1, 16, HALF)
                return tuple(c + jnp.sum(v, axis=0) if d == b else c for d, c in enumerate(carry))
            found.append(each(step, tuple(zero16 for _ in buckets)))
        sums = [jnp.concatenate([left, right], axis=1) for left, right in zip(*found)]
        pooled = jnp.concatenate(
            [over_quadrants(s) * (1.0 / (4 * side * side)) for s, side in zip(sums, sides)], axis=0
        )
        squeeze_pre = by_parts(dot, pooled, down[...]) + downb[...]
        squeezed = squeeze_pre * jax.nn.sigmoid(squeeze_pre)
        excite = jax.nn.sigmoid(by_parts(dot, squeezed, up[...]) + upb[...])
        se[0] = pooled
        sq[...] = squeeze_pre
        for b in buckets:
            se[1, 16 * b : 16 * b + 16, :] = excite[16 * b : 16 * b + 16, :] * mask[b]

    def gate(x, k, se, store):
        def step(b, rows, i, carry):
            v = half_silu(half(k, x[rows, :])).reshape(-1, 16, WIDTH)
            v = v * se[1, 16 * b : 16 * b + 16, :][None]
            store(rows, v.reshape(-1, WIDTH).astype(BF16))
            return carry
        each(step, 0)

    def squeeze_excite_back(g, u, k, down, up, se, sq, ddown, ddownb, dup, dupb, norm_grads):
        def step(b, rows, i, carry):
            v = half_silu(half(k, u[rows, :])) * g[rows, :]
            return tuple(
                c + jnp.sum(v.reshape(-1, 16, WIDTH), axis=0) if d == b else c
                for d, c in enumerate(carry)
            )
        zero16 = jnp.zeros((16, WIDTH), F32)
        sums = each(step, tuple(zero16 for _ in buckets))
        grad_excite = jnp.concatenate([over_quadrants(s) for s in sums], axis=0)
        excite = se[1]
        grad_up = grad_excite * excite * (1.0 - excite)
        squeeze_pre = sq[...]
        sig = jax.nn.sigmoid(squeeze_pre)
        once = first_of_image
        dup[...] = exact(squeeze_pre * sig, grad_up * once, ((0,), (0,)))
        dupb[...] = down_to_row(grad_up * once)
        grad_pre = by_parts(dot_nt, grad_up, up[...]) * (sig * (1.0 + squeeze_pre * (1.0 - sig)))
        ddown[...] = exact(se[0] * once, grad_pre, ((0,), (0,)))
        ddownb[...] = down_to_row(grad_pre * once[:, : grad_pre.shape[1]])
        pooled_grad = by_parts(dot_nt, grad_pre, down[...])
        for b in buckets:
            pixels = 4 * sides[b] * sides[b]
            vec[56 + 16 * b : 72 + 16 * b, :] = pooled_grad[16 * b : 16 * b + 16, :] * (1.0 / pixels)

        begun = []
        for lanes in HALVES:
            def apply(b, rows, i, carry, lanes=lanes):
                u_now = u[rows, lanes]
                y = half(k, u_now, lanes)
                slope = half_silu_grad(y, jnp.tanh(y))
                gv = g[rows, lanes].reshape(-1, 16, HALF) * se[1, 16 * b : 16 * b + 16, lanes][None]
                gv = (gv + vec[56 + 16 * b : 72 + 16 * b, lanes][None]).reshape(-1, HALF) * slope
                g[rows, lanes] = gv
                return carry[0] + fold(gv), carry[1] + fold(gv * (u_now - row(k, 0, lanes)))

            local = [down_to_row(v) for v in each(apply, (zero_half, zero_half))]
            put_norm_grads(norm_grads, 1, k, *local, lanes)
            begun.append(begin_sum(local))
        return begun

    def put_norm_grads(out, index, k, sum_g, sum_d, lanes=ALL):
        out[2 * index : 2 * index + 1, lanes] = row(k, 1, lanes) * sum_d
        out[2 * index + 1 : 2 * index + 2, lanes] = sum_g

    planes = [(0, 0), (0, 1), (1, 0), (1, 1)]

    chunk = total // 5
    wide = [x0, x1, x2, x3]

    def stat_dot(plane, weight, out, lanes, carry):
        def step(i, kept):
            rows = aligned(i * chunk, chunk)
            u = dot(acts[plane, rows, :], weight[:, lanes])
            if out is not None:
                out[rows, lanes] = u
            return kept[0] + fold(u), kept[1] + fold(u * u)
        return lax.fori_loop(0, 5, step, carry, unroll=True)

    one = []
    for lanes in HALVES:
        carry = (zero_half, zero_half)
        for plane in range(4):
            if len(one) == 0:
                loads[plane].wait()
            carry = stat_dot(plane, w_in1, wide[plane], lanes, carry)
        one.append(begin_sum([down_to_row(v) for v in carry]))
    short = begin_sum([down_to_row(v) for v in stat_dot(0, w_short, None, ALL, (zero8, zero8))], 2)
    live = count[...]
    vec[54:55, :] = live

    end = 0
    h1_bases = []
    for pr, pc in planes:
        grid_bases, end = geo.grid(pr, pc, end)
        h1_bases.append(grid_bases)
    second = SecondGather(
        info, places, line2, pool, end, (near_send, near_recv, near_core_send, core_land)
    )
    two = []
    for h, lanes in enumerate(HALVES):
        set_norm(0, *finish_sum(one[h]), norms1, 0, 4.0 * live, lanes)
        if h == 0:
            second.begin()
        for plane, (pr, pc) in enumerate(planes):
            def step(b, rows, i, carry, plane=plane, pr=pr, pc=pc, lanes=lanes):
                width = sides[b] + pc
                start = h1_bases[plane][b] + ((i + pr) * width + pc) * 16
                value = half_silu(half(0, wide[plane][rows, lanes], lanes))
                pool[aligned(start, sides[b] * 16), lanes] = masked(value, b).astype(BF16)
                return carry
            each(step, 0)
            for b in buckets:
                fill_halo(h1_bases[plane][b], b, pr, 0, pc, 0, lanes)
        carry = (zero_half, zero_half)
        for b in buckets:
            parts = []
            for tap in range(TAPS):
                dy, dx = tap // 3, tap % 3
                pr, pc = int(dy != 1), int(dx != 1)
                parts.append(
                    window(h1_bases[2 * pr + pc][b], sides[b] + pc, b, int(dy == 2), int(dx == 2), lanes)
                )
            u = dot(jnp.concatenate(parts, axis=1), bd1[h].reshape(TAPS * HALF, HALF))
            carry = keep_and_fold(x0, slice(bases[b], bases[b] + rows_of[b]), lanes, u, carry)
        two.append(begin_stats(carry))
    h1b_bases, end = geo.grid(2, 2, 0)
    g2b_bases, end = geo.grid(2, 2, end)
    h2b, cot_at = end, end + total
    g3b = cot_at
    second.pass_on()
    live = vec[54:55, :]
    squeeze_excite(x0, 1, two, norms1, down1, downb1, up1, upb1, se1, sq1)
    def keep_h2(rows, value):
        h2[rows, :] = value
    gate(x0, 1, se1, keep_h2)
    begun = begin_dot_stats(x1, h2, w_out1)
    x2[...] = dot(acts[0], w_short[...])
    second.finish(x3, shares, tall, weights2)
    fetch = pltpu.make_async_copy(cot_hbm, pool.at[pl.ds(cot_at, total)], sems.at[0])
    fetch.start()
    sums = finish_sum(short)
    set_norm(3, sums[0], sums[1], norms1, 3, live)
    for lanes, part in zip(HALVES, begun):
        set_norm(2, *finish_sum(part), norms1, 2, live, lanes)
    def middle(b, rows, i, carry):
        y = half(2, x1[rows, :]) + half(3, x2[rows, :])
        mid[rows, :] = masked(half_silu(y), b).astype(BF16)
        return carry
    each(middle, 0)

    one = begin_dot_stats(x2, mid, w_in2)
    two = []
    for h, lanes in enumerate(HALVES):
        set_norm(4, *finish_sum(one[h]), norms2, 0, live, lanes)
        def hidden(b, rows, i, carry, lanes=lanes):
            start = h1b_bases[b] + ((i + 1) * (sides[b] + 2) + 1) * 16
            value = half_silu(half(4, x2[rows, lanes], lanes))
            pool[aligned(start, sides[b] * 16), lanes] = masked(value, b).astype(BF16)
            return carry
        each(hidden, 0)
        carry = (zero_half, zero_half)
        for b in buckets:
            fill_halo(h1b_bases[b], b, 1, 1, 1, 1, lanes)
            parts = [
                window(h1b_bases[b], sides[b] + 2, b, tap // 3, tap % 3, lanes) for tap in range(TAPS)
            ]
            u = dot(jnp.concatenate(parts, axis=1), bd2[h].reshape(TAPS * HALF, HALF))
            carry = keep_and_fold(x3, slice(bases[b], bases[b] + rows_of[b]), lanes, u, carry)
        two.append(begin_stats(carry))
    squeeze_excite(x3, 5, two, norms2, down2, downb2, up2, upb2, se2, sq2)
    def keep_h2b(rows, value):
        pool[aligned(rows.start + h2b, rows.size), :] = value
    gate(x3, 5, se2, keep_h2b)
    begun = begin_dot_stats(x1, pool.at[pl.ds(h2b, total)], w_out2)
    fetch.wait()
    out_at = g2b_bases[0]
    three = []
    for lanes, part in zip(HALVES, begun):
        set_norm(6, *finish_sum(part), norms2, 2, live, lanes)
        def finish(b, rows, i, carry, lanes=lanes):
            u = x1[rows, lanes]
            y = half(6, u, lanes) + 0.5 * mid[rows, lanes].astype(F32)
            tan = jnp.tanh(y)
            pool[aligned(rows.start + out_at, rows.size), lanes] = masked(y + y * tan, b).astype(BF16)
            g = pool[aligned(rows.start + cot_at, rows.size), lanes].astype(F32) * half_silu_grad(y, tan)
            x2[rows, lanes] = g
            return carry[0] + fold(g), carry[1] + fold(g * (u - row(6, 0, lanes)))
        local = [down_to_row(v) for v in each(finish, (zero_half, zero_half))]
        put_norm_grads(dnorms2, 2, 6, *local, lanes)
        three.append(begin_sum(local))
    puts = [
        pltpu.make_async_copy(pool.at[pl.ds(out_at + bases[b], rows_of[b])], out_hbm[b], sems.at[2 + b])
        for b in buckets
    ]
    for put in puts:
        put.start()

    for lanes, part in zip(HALVES, three):
        set_grad(6, *finish_sum(part), live, lanes=lanes)
        def third(b, rows, i, carry, lanes=lanes):
            value = grad_u(x2[rows, lanes], x1[rows, lanes], b, lanes=lanes)
            pool[aligned(rows.start + g3b, rows.size), lanes] = value
            return carry
        each(third, 0)
    x1[...] = dot_nt(pool[g3b : g3b + total, :], w_out2[...])
    two = squeeze_excite_back(x1, x3, 5, down2, up2, se2, sq2, ddown2, ddownb2, dup2, dupb2, dnorms2)
    dw_out2[...] = dot_tn(pool[h2b : h2b + total, :], pool[g3b : g3b + total, :])
    for put in puts:
        put.wait()
    for h, lanes in enumerate(HALVES):
        set_grad(5, *finish_sum(two[h]), live, lanes=lanes)
        def second_u(b, rows, i, carry, lanes=lanes):
            start = g2b_bases[b] + ((i + 1) * (sides[b] + 2) + 1) * 16
            pool[aligned(start, sides[b] * 16), lanes] = grad_u(x1[rows, lanes], x3[rows, lanes], b, lanes=lanes)
            return carry
        each(second_u, 0)
        for b in buckets:
            fill_halo(g2b_bases[b], b, 1, 1, 1, 1, lanes)
            parts = [
                window(g2b_bases[b], sides[b] + 2, b, 2 - tap // 3, 2 - tap % 3, lanes) for tap in range(TAPS)
            ]
            x1[bases[b] : bases[b] + rows_of[b], lanes] = dot_nt(
                jnp.concatenate(parts, axis=1),
                jnp.concatenate([bd2[h, tap] for tap in range(TAPS)], axis=1),
            )
    x3[...] = dot(mid[...], w_in2[...])
    def first(b, rows, i, carry):
        u = x3[rows, :]
        y = half(4, u)
        g = x1[rows, :] * half_silu_grad(y, jnp.tanh(y))
        x1[rows, :] = g
        return carry[0] + fold(g), carry[1] + fold(g * (u - row(4, 0)))
    local = [down_to_row(v) for v in each(first, (zero8, zero8))]
    put_norm_grads(dnorms2, 0, 4, *local)
    begun = begin_sum(local)
    for h, lanes in enumerate(HALVES):
        source = jnp.concatenate(
            [window(h1b_bases[b], sides[b] + 2, b, 1, 1, lanes) for b in buckets], axis=0
        )
        for tap in range(TAPS):
            target = jnp.concatenate(
                [window(g2b_bases[b], sides[b] + 2, b, 2 - tap // 3, 2 - tap % 3, lanes) for b in buckets],
                axis=0,
            )
            acc[tap, h] = diagonal(dot_tn(source, target))
    set_grad(4, *finish_sum(begun), live)
    def first_u(b, rows, i, carry):
        pool[aligned(rows.start + g3b, rows.size), :] = grad_u(x1[rows, :], x3[rows, :], b)
        return carry
    each(first_u, 0)
    x2[...] = x2[...] + dot_nt(pool[g3b : g3b + total, :], w_in2[...])

    x3[...] = dot(h2[...], w_out1[...])
    x1[...] = dot(acts[0], w_short[...])
    def joined(b, rows, i, carry):
        u, s = x3[rows, :], x1[rows, :]
        y = half(2, u) + half(3, s)
        g = x2[rows, :] * half_silu_grad(y, jnp.tanh(y))
        x2[rows, :] = g
        return (
            carry[0] + fold(g),
            carry[1] + fold(g * (u - row(2, 0))),
            carry[2] + fold(g * (s - row(3, 0))),
        )
    local = [down_to_row(v) for v in each(joined, (zero8, zero8, zero8))]
    put_norm_grads(dnorms1, 2, 2, local[0], local[1])
    put_norm_grads(dnorms1, 3, 3, local[0], local[2])
    begun = begin_sum(local[:2])
    short = begin_sum(local[2:], 2)
    dw_in2[...] = dot_tn(mid[...], pool[g3b : g3b + total, :])
    g2_bases, g1_at = geo.grid(1, 1, 0)
    back = SecondScatter(
        info, places, pool, g1_at, h2b, (far_core, far_chip_send, far_chip_recv, far_line_send, far_line_recv)
    )
    back.begin(shares, acc, grads2)
    sums = finish_sum(begun)
    set_grad(2, *sums, live)
    sum_g = sums[0]
    def third_one(b, rows, i, carry):
        pool[rows, :] = grad_u(x2[rows, :], x3[rows, :], b)
        return carry
    each(third_one, 0)
    x3[...] = dot_nt(pool[0:total, :], w_out1[...])
    two = squeeze_excite_back(x3, x0, 1, down1, up1, se1, sq1, ddown1, ddownb1, dup1, dupb1, dnorms1)
    set_grad(3, sum_g, *finish_sum(short), live, 51)
    def shortcut(b, rows, i, carry):
        mid[rows, :] = grad_u(x2[rows, :], x1[rows, :], b, 51)
        return carry
    each(shortcut, 0)
    puts = [
        pltpu.make_async_copy(mid.at[pl.ds(bases[b], rows_of[b])], gs_hbm[b], sems.at[2 + b]) for b in buckets
    ]
    for put in puts:
        put.start()
    dw_short[...] = dot_tn(acts[0], mid[...])
    dw_out1[...] = dot_tn(h2[...], pool[0:total, :])
    for lanes, part in zip(HALVES, two):
        set_grad(1, *finish_sum(part), live, lanes=lanes)
    def second_one(b, rows, i, carry):
        start = g2_bases[b] + (i * (sides[b] + 1)) * 16
        pool[aligned(start, sides[b] * 16), :] = grad_u(x3[rows, :], x0[rows, :], b)
        return carry
    each(second_one, 0)
    for b in buckets:
        for lanes in HALVES:
            fill_halo(g2_bases[b], b, 0, 1, 0, 1, lanes)

    def group_grads(taps, b, h2_at):
        for h, lanes in enumerate(HALVES):
            source = h2[h2_at : h2_at + rows_of[b], lanes]
            for tap in taps:
                target = window(g2_bases[b], sides[b] + 1, b, int(tap // 3 == 0), int(tap % 3 == 0), lanes)
                if b == 0:
                    acc[tap, h] = diagonal(dot_tn(source, target))
                else:
                    acc[tap, h] += diagonal(dot_tn(source, target))

    back.across_chips()
    carry = (zero8, zero8)
    kept = [x1, x2, x3]
    apart = max(rows_of[:-1])
    for plane, (pr, pc) in enumerate(planes):
        taps = [
            tap for tap in range(TAPS) if int(tap // 3 != 1) == pr and int(tap % 3 != 1) == pc
        ]
        for b in buckets:
            side = sides[b]
            pieces = [(0, side)]
            if plane == 3 and rows_of[b] > apart:
                pieces = [(0, side // 2), (side // 2, side)]
            h2_at = bases[b] if plane == 3 else 0
            for first_line, end_line in pieces:
                at, size = first_line * side * 16, (end_line - first_line) * side * 16
                x0[0:size, :] = dot(acts[plane, bases[b] + at : bases[b] + at + size, :], w_in1[...])
                grads_at, grads = (bases[b], kept[plane]) if plane < 3 else (apart, x0)
                for h, lanes in enumerate(HALVES):
                    parts = [
                        window(
                            g2_bases[b], side + 1, b, int(tap // 3 == 0), int(tap % 3 == 0), lanes,
                            range(first_line, end_line),
                        )
                        for tap in taps
                    ]
                    grads[grads_at : grads_at + size, lanes] = dot_nt(
                        jnp.concatenate(parts, axis=1), jnp.concatenate([bd1[h, tap] for tap in taps], axis=1)
                    )
                def line(i, sums, b=b, plane=plane, at=at, h2_at=h2_at, grads=grads, grads_at=grads_at):
                    size = sides[b] * 16
                    u = x0[aligned(i * size, size), :]
                    y = half(0, u)
                    tan = jnp.tanh(y)
                    h2[aligned(h2_at + at + i * size, size), :] = masked(y + y * tan, b).astype(BF16)
                    here = aligned(grads_at + i * size, size)
                    g = grads[here, :] * half_silu_grad(y, tan)
                    if plane < 3:
                        grads[here, :] = g
                    else:
                        start = g1_at + plane * total + bases[b] + at + i * size
                        pool[aligned(start, size), :] = g.astype(BF16)
                    return sums[0] + fold(g), sums[1] + fold(g * (u - row(0, 0)))
                carry = lax.fori_loop(0, end_line - first_line, line, carry)
            if plane < 3:
                group_grads(taps, b, 0)
        if plane == 1:
            back.along_line()
    local = [down_to_row(v) for v in carry]
    put_norm_grads(dnorms1, 0, 0, *local)
    begun = begin_sum(local)
    for b in buckets:
        group_grads(taps, b, bases[b])
    back.finish(second_out)
    put_group1 = pltpu.make_async_copy(acc, dwg1_hbm, sems.at[1])
    put_group1.start()
    set_grad(0, *finish_sum(begun), 4.0 * live)
    for plane in range(4):
        x0[...] = dot(acts[plane], w_in1[...])
        at = g1_at + plane * total
        def first_one(b, rows, i, carry, at=at, plane=plane):
            here = aligned(rows.start + at, rows.size)
            g = kept[plane][rows, :] if plane < 3 else pool[here, :].astype(F32)
            pool[here, :] = grad_u(g, x0[rows, :], b)
            return carry
        each(first_one, 0)
        part = dot_tn(acts[plane], pool[at : at + total, :])
        if plane == 0:
            dw_in1[...] = part
        else:
            dw_in1[...] += part
        for b in buckets:
            put = pltpu.make_async_copy(
                pool.at[pl.ds(at + bases[b], rows_of[b])], g1_hbm[b].at[plane], sems.at[5 + 3 * plane + b]
            )
            put.start()
            puts.append(put)
    for put in puts:
        put.wait()
    put_group1.wait()


def whole():
    return pl.BlockSpec(memory_space=pltpu.VMEM)


def anywhere():
    return pl.BlockSpec(memory_space=pl.ANY)


def shape(dims, dtype=F32):
    return jax.ShapeDtypeStruct(dims, dtype)


def blocks(geo, infos, acts, mask, count, first, line2, cot):
    groups, inner = lax.axis_size("dp"), lax.axis_size("fsdp")
    total = geo.total
    ins = [acts, mask, count, *first, line2, cot]
    info = infos[1]
    hbm_outs = [
        *[shape((rows, WIDTH), BF16) for rows in geo.rows],
        *[shape((4, rows, WIDTH), BF16) for rows in geo.rows],
        *[shape((rows, WIDTH), BF16) for rows in geo.rows],
        shape((TAPS, 2, HALF, 128)),
    ]
    vmem_outs = [shape((info.share, 128))]
    vmem_outs += [shape(d) for j, d in enumerate(shapes_of(True)) if j != 1]
    second = shapes_of(False)
    pool_rows = 0
    for pr, pc in ((0, 0), (0, 1), (1, 0), (1, 1)):
        pool_rows = geo.grid(pr, pc, pool_rows)[1]
    pool_rows = pool_rows + groups * info.block
    pool_rows = max(
        pool_rows, geo.grid(2, 2, geo.grid(2, 2, 0)[1])[1] + 2 * total, geo.grid(1, 1, 0)[1] + 4 * total
    )
    stages = exchange_stages(groups, inner)
    big = pltpu.VMEM((total, WIDTH), F32)
    scratch = [pltpu.VMEM(second[0], BF16), pltpu.VMEM((2, TAPS, HALF, HALF), BF16)]
    scratch += [pltpu.VMEM(d, F32 if d[0] == 1 else BF16) for d in second[2:-1]] + [pltpu.VMEM(second[-1], F32)]
    scratch += [pltpu.VMEM(d, F32) for j, d in enumerate(second) if j != 1]
    chips = groups // 2
    scratch += [
        pltpu.VMEM(acts.shape, BF16), pltpu.SemaphoreType.DMA((4,)),
        pltpu.VMEM((WIDTH, 128), F32), pltpu.VMEM((2, info.padded, 128), F32),
        pltpu.VMEM((pool_rows, WIDTH), BF16), big, big, big, big,
        pltpu.VMEM((total, WIDTH), BF16), pltpu.VMEM((total, WIDTH), BF16),
        pltpu.VMEM((TAPS, 2, HALF, 128), F32), pltpu.VMEM((104, WIDTH), F32),
        pltpu.VMEM((2, 48, WIDTH), F32), pltpu.VMEM((48, SQUEEZE_A), F32),
        pltpu.VMEM((2, 48, WIDTH), F32), pltpu.VMEM((48, SQUEEZE_B), F32),
        pltpu.VMEM((3 * len(stages), 8, 128), F32),
        pltpu.VMEM((3 * len(stages), max(stages) - 1, 8, 128), F32),
        pltpu.SemaphoreType.DMA((3 * len(stages),)), pltpu.SemaphoreType.DMA((3 * len(stages),)),
        pltpu.VMEM((4 * len(stages), 4, 128), F32),
        pltpu.VMEM((4 * len(stages), max(stages) - 1, 4, 128), F32),
        pltpu.SemaphoreType.DMA((4 * len(stages),)), pltpu.SemaphoreType.DMA((4 * len(stages),)),
        pltpu.SemaphoreType.DMA((17,)),
    ]
    scratch += [
        pltpu.SemaphoreType.DMA(dims)
        for dims in (
            (chips - 1,), (chips - 1,), (chips,), (), (2,), (chips - 1,), (chips - 1,), (inner - 1,), (inner - 1,)
        )
    ]
    outs = pl.pallas_call(
        functools.partial(body, geo, info, groups, inner),
        out_shape=hbm_outs + vmem_outs,
        in_specs=[anywhere()] + [whole()] * 12 + [anywhere()],
        out_specs=[anywhere()] * len(hbm_outs) + [whole()] * len(vmem_outs),
        scratch_shapes=scratch,
        compiler_params=pltpu.CompilerParams(
            collective_id=0, has_side_effects=True, vmem_limit_bytes=LIMIT
        ),
    )(*ins)
    first_grads = [outs[11], outs[9], *outs[12:]]
    return outs[0:3], outs[3:6], outs[6:9], first_grads, outs[10].reshape(-1)


class Flat:
    def __init__(self, is_first, full_length, devices, inner):
        self.shapes = shapes_of(is_first)
        self.starts = []
        offset = 0
        for dims in self.shapes:
            self.starts.append(offset // 128)
            offset = offset + math.prod(dims)
        self.skew = offset % 128
        self.used = offset
        self.rows = full_length // 128
        self.share = self.rows // devices
        self.padded = -(-(self.share + 3) // 16) * 16
        self.layers = -(-inner // 4)
        self.block = self.layers * self.padded


def first_lanes(limit, dims):
    return lax.broadcasted_iota(jnp.int32, dims, 1) < limit


def column_pick(b):
    row = lax.broadcasted_iota(jnp.int32, (384, SQUEEZE_A), 0)
    column = lax.broadcasted_iota(jnp.int32, (384, SQUEEZE_A), 1)
    return (row == column + SQUEEZE_A * b).astype(F32)


def unskew(info, flat):
    row = info.starts[4]
    while row < info.rows:
        size = min(256, info.rows - row)
        here = pltpu.roll(flat[row : row + size, :], 128 - info.skew, 1)
        after = pltpu.roll(flat[row + 1 : row + size + 1, :], 128 - info.skew, 1)
        flat[row : row + size, :] = jnp.where(first_lanes(128 - info.skew, (size, 128)), here, after)
        row = row + size


def reskew(info, flat):
    row = info.rows
    first = info.starts[4]
    while row > first:
        size = min(256, row - first)
        start = row - size
        here = pltpu.roll(flat[start:row, :], info.skew, 1)
        if start == first:
            ahead = pltpu.roll(flat[start : row, :], info.skew, 1)
            ahead = pltpu.roll(ahead, 1, 0)
            keep = flat[info.rows + 8 : info.rows + 9, :]
            is_top = lax.broadcasted_iota(jnp.int32, (size, 128), 0) == 0
            ahead = jnp.where(is_top, jnp.broadcast_to(keep, (size, 128)), ahead)
        else:
            ahead = pltpu.roll(flat[start - 1 : row - 1, :], info.skew, 1)
        flat[start:row, :] = jnp.where(first_lanes(info.skew, (size, 128)), ahead, here)
        row = start


def unpack(info, flat, block_pad, outs):
    def wide(out, start):
        rows = out.shape[0]
        for c in range(4):
            out[:, c * 128 : (c + 1) * 128] = flat[pl.ds(start + c, rows, stride=4), :].astype(out.dtype)

    starts = info.starts
    w_in, bd, down, downb, up, upb, w_out = outs[:7]
    wide(w_in, starts[0])
    row = lax.broadcasted_iota(jnp.int32, (128, HALF), 0) // 32
    lane = lax.broadcasted_iota(jnp.int32, (128, HALF), 1) // GROUP_WIDTH
    on_diagonal = (row == lane).astype(F32)

    def spread(index, carry):
        rows = flat[pl.ds(pl.multiple_of(starts[1] + index * 128, 8), 128), :]
        turned = pltpu.roll(rows, GROUP_WIDTH, 1)
        left = first_lanes(GROUP_WIDTH, (128, 128))
        for parity, pair in enumerate((jnp.where(left, rows, turned), jnp.where(left, turned, rows))):
            tiled = jnp.concatenate([pair, pair], axis=1) * on_diagonal
            block_pad[pl.ds(parity, 128, stride=2), :] = tiled[:, :128]
            block_pad[pl.ds(HALF + parity, 128, stride=2), :] = tiled[:, 128:]
        bd[index % 2, index // 2, :, 0:128] = block_pad[0:HALF, :].astype(BF16)
        bd[index % 2, index // 2, :, 128:HALF] = block_pad[HALF : 2 * HALF, :].astype(BF16)
        return carry

    lax.fori_loop(0, 2 * TAPS, spread, 0)
    if down.shape[1] == 128:
        down[...] = flat[starts[2] : starts[2] + WIDTH, :].astype(BF16)
    else:
        joined = jnp.concatenate([flat[pl.ds(starts[2] + q, 64, stride=3), :] for q in range(3)], axis=1)
        for b in range(8):
            block_pad[pl.ds(b, 64, stride=8), 0:SQUEEZE_A] = dot(joined, column_pick(b))
        down[...] = block_pad[:, 0:SQUEEZE_A].astype(BF16)
    downb[...] = flat[starts[3] : starts[3] + 1, 0 : downb.shape[1]]
    if info.skew:
        unskew(info, flat)
    wide(up, starts[4])
    upb[...] = jnp.concatenate([flat[starts[5] + c : starts[5] + c + 1, :] for c in range(4)], axis=1)
    wide(w_out, starts[6])
    if len(outs) == 9:
        wide(outs[7], starts[7])
    wide(outs[-1], starts[-1])


def pack(info, flat, grads):
    def wide(value, start):
        rows = value.shape[0]
        for c in range(4):
            flat[pl.ds(start + c, rows, stride=4), :] = value[:, c * 128 : (c + 1) * 128]

    starts = info.starts
    d_in, dwg, ddown, ddownb, dup, dupb, d_out = grads[:7]
    flat[info.used // 128 // 8 * 8 : info.rows, :] = jnp.zeros_like(flat[info.used // 128 // 8 * 8 : info.rows, :])
    wide(d_in, starts[0])
    group_odd = lax.broadcasted_iota(jnp.int32, (128, 128), 0) // 32 % 2 == 1
    left = first_lanes(GROUP_WIDTH, (128, 128))

    def collect(index, carry):
        even = dwg[index // 2, index % 2, pl.ds(0, 128, stride=2), :]
        odd = dwg[index // 2, index % 2, pl.ds(1, 128, stride=2), :]
        even_turned, odd_turned = pltpu.roll(even, GROUP_WIDTH, 1), pltpu.roll(odd, GROUP_WIDTH, 1)
        rows = jnp.where(
            group_odd, jnp.where(left, even_turned, odd), jnp.where(left, even, odd_turned)
        )
        flat[pl.ds(pl.multiple_of(starts[1] + index * 128, 8), 128), :] = rows
        return carry

    lax.fori_loop(0, 2 * TAPS, collect, 0)
    if ddown.shape[1] == 128:
        flat[starts[2] : starts[2] + WIDTH, :] = ddown[...]
    else:
        joined = sum(
            exact(ddown[pl.ds(b, 64, stride=8), :], column_pick(b), ((1,), (1,))) for b in range(8)
        )
        for q in range(3):
            flat[pl.ds(starts[2] + q, 64, stride=3), :] = joined[:, q * 128 : (q + 1) * 128]
    wide(dup, starts[4])
    for c in range(4):
        flat[starts[5] + c : starts[5] + c + 1, :] = dupb[:, c * 128 : (c + 1) * 128]
    wide(d_out, starts[6])
    if len(grads) == 9:
        wide(grads[7], starts[7])
    wide(grads[-1], starts[-1])
    if info.skew:
        flat[info.rows + 8 : info.rows + 9, 0 : ddownb.shape[1]] = ddownb[...]
        reskew(info, flat)
    else:
        flat[starts[3] : starts[3] + 1, :] = ddownb[...]


class Places:
    def __init__(self, groups, inner):
        self.outer, self.inner = lax.axis_index("dp"), lax.axis_index("fsdp")
        self.chips, self.lines = groups // 2, inner
        self.chip, self.core = self.outer // 2, lax.rem(self.outer, 2)

    def along(self, step):
        return lax.rem(self.inner + step, self.lines)

    def across(self, step):
        return lax.rem(self.chip + step, self.chips)

    def line(self, step):
        return (self.outer, self.along(step))

    def other_chip(self, step):
        return (2 * self.across(step) + self.core, self.inner)

    def sibling(self):
        return (2 * self.chip + 1 - self.core, self.inner)

    def greet(self, barrier):
        for step in range(1, self.lines):
            pl.semaphore_signal(barrier, inc=1, device_id=self.line(step), device_id_type=MESH)
        for step in range(1, self.chips):
            pl.semaphore_signal(barrier, inc=1, device_id=self.other_chip(step), device_id_type=MESH)
        pl.semaphore_signal(barrier, inc=1, device_id=self.sibling(), device_id_type=MESH)

    def greeted(self, barrier):
        pl.semaphore_wait(barrier, self.lines + self.chips - 1)


def remote(source, target, send_sem, recv_sem, device):
    return pltpu.make_async_remote_copy(
        src_ref=source, dst_ref=target, send_sem=send_sem, recv_sem=recv_sem, device_id=device, device_id_type=MESH
    )


def lane_tile(c):
    return slice(128 * c, 128 * c + 128)


def quarters(info, d):
    start = info.share * d
    for c in range(4):
        first = (c - start) % 4
        yield c, first, (start + first) // 4, -(-(info.share - first) // 4)


class SecondGather:
    def __init__(self, info, places, line, pool, start, semaphores):
        self.info, self.places, self.line, self.pool, self.start = info, places, line, pool, start
        self.chip_send, self.chip_recv, self.core_send, self.core_land = semaphores
        self.started = []

    def block(self, core, chip):
        row = self.start + (core * self.places.chips + chip) * self.info.block
        return self.pool.at[aligned(row, self.info.block)]

    def begin(self):
        places = self.places
        mine = self.block(places.core, places.chip)
        mine[...] = self.line[...]
        for step in range(1, places.chips):
            self.started.append(
                remote(
                    self.line, mine, self.chip_send.at[step - 1], self.chip_recv.at[step - 1], places.other_chip(step)
                )
            )
        self.started.append(remote(self.line, mine, self.core_send.at[0], self.core_land, places.sibling()))
        for copy in self.started:
            copy.start()

    def pass_on(self):
        places = self.places
        for step in range(1, places.chips):
            self.started[step - 1].wait_recv()
            landed = self.block(places.core, places.across(places.chips - step))
            copy = remote(landed, landed, self.core_send.at[step], self.core_land, places.sibling())
            copy.start()
            self.started.append(copy)

    def finish(self, flat, shares, tall, weights):
        info, places = self.info, self.places
        half_rows = places.chips * info.block
        half = self.pool.at[pl.ds(self.start, half_rows)]
        pltpu.make_async_copy(half, half, self.core_land).wait()
        for copy in self.started:
            copy.wait_send()
        for d in range(2 * places.chips * places.lines):
            z, outer = d % places.lines, d // places.lines
            row = self.start + (outer % 2 * places.chips + outer // 2) * info.block + z // 4 * info.padded
            share = shares.at[d % 2]
            share[...] = self.pool[row : row + info.padded, lane_tile(z % 4)].astype(F32)
            for c, first, at, rows in quarters(info, d):
                flat[at : at + rows, lane_tile(c)] = share[pl.ds(first, rows, stride=4), :]
        w_in, bd, down, downb, up, upb, w_out, norms = weights
        w_in[...] = flat[0:WIDTH, :].astype(BF16)
        at = WIDTH
        row = lax.broadcasted_iota(jnp.int32, (32, HALF), 0) // 8
        lane = lax.broadcasted_iota(jnp.int32, (32, HALF), 1) // GROUP_WIDTH
        on_diagonal = (row == lane).astype(F32)

        def spread(index, carry):
            for c in range(4):
                rows = flat[pl.ds(pl.multiple_of(at + index * 32, 8), 32), lane_tile(c)]
                turned = pltpu.roll(rows, GROUP_WIDTH, 1)
                left = first_lanes(GROUP_WIDTH, (32, 128))
                for parity, pair in enumerate((jnp.where(left, rows, turned), jnp.where(left, turned, rows))):
                    tiled = jnp.concatenate([pair, pair], axis=1) * on_diagonal
                    tall[pl.ds(2 * c + parity, 32, stride=8), :] = tiled[:, :128]
                    tall[pl.ds(HALF + 2 * c + parity, 32, stride=8), :] = tiled[:, 128:]
            bd[index % 2, index // 2, :, 0:128] = tall[0:HALF, :].astype(BF16)
            bd[index % 2, index // 2, :, 128:HALF] = tall[HALF : 2 * HALF, :].astype(BF16)
            return carry

        lax.fori_loop(0, 2 * TAPS, spread, 0)
        at = at + TAPS * 64
        for c in range(4):
            tall[pl.ds(c, 128, stride=4), :] = flat[at : at + 128, lane_tile(c)]
        down[...] = tall[...].astype(BF16)
        at = at + 128
        downb[...] = flat[at : at + 1, lane_tile(0)]
        for out in (up, upb, w_out, norms):
            rows = out.shape[0]
            for c in range(4):
                begin = at + (c + 1) // 4
                out[:, lane_tile(c)] = flat[begin : begin + rows, lane_tile((c + 1) % 4)].astype(out.dtype)
            at = at + rows


class SecondScatter:
    def __init__(self, info, places, pool, start, landing, semaphores):
        self.info, self.places, self.pool = info, places, pool
        self.core_sem, self.chip_send, self.chip_recv, self.line_send, self.line_recv = semaphores
        block, chips = info.block, places.chips
        self.core_in = landing
        self.chip_in = self.core_in + chips * block
        self.line_in = self.chip_in + (chips - 1) * block
        self.line_sum = self.line_in + block
        self.parts = start

    def rows(self, start, size):
        return self.pool.at[aligned(start, size)]

    def part(self, core, chip):
        return self.parts + (core * self.places.chips + chip) * self.info.block

    def begin(self, shares, acc, grads):
        info, places = self.info, self.places
        d_in, ddown, ddownb, dup, dupb, d_out, dnorms = grads
        group_odd = lax.broadcasted_iota(jnp.int32, (128, 128), 0) // 32 % 2 == 1
        left = first_lanes(GROUP_WIDTH, (128, 128))

        def collect(index, carry):
            tap, h = index // 2, index % 2
            even, odd = acc[tap, h, pl.ds(0, 128, stride=2), :], acc[tap, h, pl.ds(1, 128, stride=2), :]
            even_turned, odd_turned = pltpu.roll(even, GROUP_WIDTH, 1), pltpu.roll(odd, GROUP_WIDTH, 1)
            acc[tap, h, 0:128, :] = jnp.where(
                group_odd, jnp.where(left, even_turned, odd), jnp.where(left, even, odd_turned)
            )
            return carry

        lax.fori_loop(0, 2 * TAPS, collect, 0)
        pieces = [(0, 4 * WIDTH, d_in, 4)]
        at = 4 * WIDTH
        for index in range(2 * TAPS):
            pieces.append((at, 128, acc.at[index // 2, index % 2], 1))
            at = at + 128
        for value, tiles in ((ddown, 1), (ddownb, 1), (dup, 4), (dupb, 4), (d_out, 4), (dnorms, 4)):
            pieces.append((at, value.shape[0] * tiles, value, tiles))
            at = at + value.shape[0] * tiles
        for d in range(2 * places.chips * places.lines):
            z, outer = d % places.lines, d // places.lines
            share = shares.at[d % 2]
            begin, end = info.share * d, info.share * (d + 1)
            if end > at:
                share[...] = jnp.zeros_like(share)
            for start, rows, value, tiles in pieces:
                low, high = max(begin, start), min(end, start + rows)
                for c in range(tiles):
                    first = low + (c - (low - start)) % tiles
                    number = -(-(high - first) // tiles)
                    if number > 0:
                        row = (first - start) // tiles
                        piece = value[row : row + number, lane_tile(c)]
                        if tiles == 1:
                            share[first - begin : first - begin + number, :] = piece
                        else:
                            share[pl.ds(first - begin, number, stride=tiles), :] = piece
            row = self.part(outer % 2, outer // 2) + z // 4 * info.padded
            self.pool[row : row + info.padded, lane_tile(z % 4)] = share[...].astype(BF16)
        size = places.chips * info.block
        self.core_copy = remote(
            self.rows(self.part(1 - places.core, 0), size),
            self.rows(self.core_in, size),
            self.core_sem.at[0],
            self.core_sem.at[1],
            places.sibling(),
        )
        self.core_copy.start()

    def across_chips(self):
        info, places = self.info, self.places
        self.core_copy.wait_recv()

        def add(index, carry):
            mine = aligned(self.part(places.core, 0) + index * info.padded, info.padded)
            theirs = aligned(self.core_in + index * info.padded, info.padded)
            self.pool[mine, :] = (self.pool[mine, :].astype(F32) + self.pool[theirs, :].astype(F32)).astype(BF16)
            return carry

        lax.fori_loop(0, places.chips * info.layers, add, 0)
        self.copies = []
        for step in range(1, places.chips):
            self.copies.append(
                remote(
                    self.rows(self.part(places.core, places.across(step)), info.block),
                    self.rows(self.chip_in + (step - 1) * info.block, info.block),
                    self.chip_send.at[step - 1],
                    self.chip_recv.at[step - 1],
                    places.other_chip(step),
                )
            )
            self.copies[-1].start()

    def along_line(self):
        info, places = self.info, self.places
        for copy in self.copies:
            copy.wait_recv()
        for layer in range(info.layers):
            at = layer * info.padded
            value = self.pool[aligned(self.part(places.core, places.chip) + at, info.padded), :].astype(F32)
            for step in range(places.chips - 1):
                begin = self.chip_in + step * info.block + at
                value = value + self.pool[begin : begin + info.padded, :].astype(F32)
            self.pool[self.line_sum + at : self.line_sum + at + info.padded, :] = value.astype(BF16)
        self.lines = []
        for step in range(1, places.lines):
            z = places.along(step)
            self.lines.append(
                remote(
                    self.pool.at[
                        aligned(self.line_sum + z // 4 * info.padded, info.padded),
                        pl.ds(pl.multiple_of(lax.rem(z, 4) * 128, 128), 128),
                    ],
                    self.pool.at[
                        pl.ds(self.line_in + (step - 1) // 4 * info.padded, info.padded),
                        lane_tile((step - 1) % 4),
                    ],
                    self.line_send.at[step - 1],
                    self.line_recv.at[step - 1],
                    places.line(step),
                )
            )
            self.lines[-1].start()

    def finish(self, out):
        info, places = self.info, self.places
        z = places.inner
        value = self.pool[
            aligned(self.line_sum + z // 4 * info.padded, info.padded),
            pl.ds(pl.multiple_of(lax.rem(z, 4) * 128, 128), 128),
        ].astype(F32)
        for step in range(1, places.lines):
            self.lines[step - 1].wait_recv()
            begin = self.line_in + (step - 1) // 4 * info.padded
            value = value + self.pool[begin : begin + info.padded, lane_tile((step - 1) % 4)].astype(F32)
        out[...] = value[0 : info.share]
        for copy in [self.core_copy] + self.copies + self.lines:
            copy.wait_send()


def gather_body(geo, infos, groups, inner, *refs):
    images_hbm, cots_hbm, counts = refs[0:3], refs[3:6], refs[6]
    shards = refs[7:9]
    acts_hbm, cot_hbm, mask, live = refs[9:13]
    weights, line_out = refs[13:22], refs[22]
    (
        wide_cell, cot_cell, block_pad, gathered, line_in, flat, stage2,
        line_send, line_recv, chip_send, chip_recv, core_send, core_recv,
        *images_and_cots, acts, cot, load_sem, store_sem,
    ) = refs[23:]
    images, cots = images_and_cots[:3], images_and_cots[3:]
    loads = [
        pltpu.make_async_copy(source, target, load_sem.at[k])
        for k, (source, target) in enumerate(zip([*images_hbm, *cots_hbm], images_and_cots))
    ]
    for load in loads:
        load.start()
    stores = []
    places = Places(groups, inner)
    barrier = pltpu.get_barrier_semaphore()
    places.greet(barrier)
    z = places.inner
    mine = [
        gathered.at[places.chip, places.core, z],
        line_in.at[
            aligned(z // 4 * infos[1].padded, infos[1].padded), pl.ds(pl.multiple_of(lax.rem(z, 4) * 128, 128), 128)
        ],
    ]
    slot = lax.broadcasted_iota(jnp.int32, (16, WIDTH), 0) % 4
    for b in range(3):
        mask[b] = jnp.where(slot < counts[0, b], 1.0, 0.0)
    for k, info in enumerate(infos):
        stage = flat.at[pl.ds(0, info.padded)] if k == 0 else stage2
        stage[info.padded - 16 : info.padded, :] = jnp.zeros((16, 128), F32)
        stage[0 : info.share, :] = shards[k][...]
        for b in range(3):
            value = jnp.broadcast_to(counts[0, b].astype(F32), (1, 128))
            stage[info.share + b : info.share + b + 1, :] = value
        mine[k][...] = stage[...].astype(BF16)
    places.greeted(barrier)
    started = []

    def begin(copy):
        copy.start()
        started.append(copy)
        return copy

    lines = [
        [
            begin(remote(mine[k], mine[k], line_send.at[k, step - 1], line_recv.at[k, step - 1], places.line(step)))
            for step in range(1, inner)
        ]
        for k in range(2)
    ]
    chip_copies = []

    def forward(step):
        if step:
            lines[0][step - 1].wait_recv()
        share = gathered.at[places.chip, places.core, places.along(inner - step)]
        for over in range(1, places.chips):
            at = (over - 1) * inner + step
            chip_copies.append(
                begin(remote(share, share, chip_send.at[at], chip_recv.at[at], places.other_chip(over)))
            )
        begin(remote(share, share, core_send.at[step], core_recv, places.sibling()))

    def pass_on(step):
        for over in range(1, places.chips):
            chip_copies[step * (places.chips - 1) + over - 1].wait_recv()
            share = gathered.at[places.across(places.chips - over), places.core, places.along(inner - step)]
            begin(remote(share, share, core_send.at[over * inner + step], core_recv, places.sibling()))

    def complete():
        half = gathered.at[:, 0]
        pltpu.make_async_copy(half, half, core_recv).wait()
        info = infos[0]
        found = jnp.zeros((3, 128), F32)
        for d in range(groups * inner):
            at = info.share * d
            piece = gathered[d // inner // 2, d // inner % 2, d % inner].astype(F32)
            flat[at : at + info.share, :] = piece[0 : info.share]
            found = found + piece[info.share : info.share + 3]
        total = sum(found[b : b + 1, :] * (4.0 * side * side) for b, side in enumerate(geo.sides))
        live[...] = jnp.concatenate([total] * 4, axis=1)
        unpack(info, flat, block_pad, weights)
        for copy in lines[1]:
            copy.wait_recv()
        line_out[...] = line_in[...]

    def arrange(b):
        side = geo.sides[b]
        size = side * 16

        def line(i, carry):
            rows = aligned(geo.bases[b] + i * size, size)
            for pr in range(2):
                for pc in range(2):
                    for q in range(4):
                        wide_cell[0:side, 4 * q : 4 * q + 4, :] = images[b][q // 2, i, pr, q % 2, :, pc].astype(F32)
                    value = wide_cell[0:side] * mask[b][None, :, :WIDTH_IN]
                    acts[2 * pr + pc, rows, :] = value.reshape(size, WIDTH_IN).astype(BF16)
            for q in range(4):
                cot_cell[0:side, 4 * q : 4 * q + 4, :] = cots[b][q // 2, i, q % 2].astype(F32)
            value = cot_cell[0:side] * mask[b][None]
            cot[rows, :] = value.reshape(size, WIDTH).astype(BF16)
            return carry

        loads[b].wait()
        loads[3 + b].wait()
        lax.fori_loop(0, side, line, 0)
        some = pl.ds(geo.bases[b], geo.rows[b])
        stores.append(pltpu.make_async_copy(acts.at[:, some], acts_hbm.at[:, some], store_sem.at[2 * b]))
        stores.append(pltpu.make_async_copy(cot.at[some], cot_hbm.at[some], store_sem.at[2 * b + 1]))
        for store in stores[-2:]:
            store.start()

    forward(0)
    arrange(0)
    for step in range(1, inner):
        forward(step)
    arrange(1)
    pass_on(0)
    arrange(2)
    for step in range(1, inner):
        pass_on(step)
    complete()
    for store in stores:
        store.wait()
    for copy in started:
        copy.wait_send()


def gather(geo, infos, images, cots, counts, shards):
    groups, inner = lax.axis_size("dp"), lax.axis_size("fsdp")
    ins = [*images, *cots, counts, *[shard.reshape(-1, 128) for shard in shards]]
    outs = [shape((4, geo.total, WIDTH_IN), BF16), shape((geo.total, WIDTH), BF16)]
    outs += [shape((3, 16, WIDTH)), shape((1, WIDTH))]
    for is_first in (True,):
        dims = shapes_of(is_first)
        outs += [shape(dims[0], BF16), shape((2, TAPS, HALF, HALF), BF16)]
        outs += [shape(d, F32 if d[0] == 1 else BF16) for d in dims[2:-1]] + [shape(dims[-1])]
    outs += [shape((infos[1].block, WIDTH), BF16)]
    side = max(geo.sides)
    scratch = [
        pltpu.VMEM((side, 16, WIDTH_IN), F32), pltpu.VMEM((side, 16, WIDTH), F32), pltpu.VMEM((2 * HALF, 128), F32),
    ]
    scratch += [
        pltpu.VMEM((groups // 2, 2, inner, infos[0].padded, 128), BF16), pltpu.VMEM((infos[1].block, WIDTH), BF16),
        pltpu.VMEM((infos[0].rows + 16, 128), F32), pltpu.VMEM((infos[1].padded, 128), F32),
    ]
    chips = groups // 2
    scratch += [
        pltpu.SemaphoreType.DMA(dims)
        for dims in (
            (2, inner - 1), (2, inner - 1), ((chips - 1) * inner,), ((chips - 1) * inner,), (chips * inner,), ()
        )
    ]
    scratch += [pltpu.VMEM(value.shape, BF16) for value in ins[:6]]
    scratch += [pltpu.VMEM(value.shape, BF16) for value in outs[:2]]
    scratch += [pltpu.SemaphoreType.DMA((6,)), pltpu.SemaphoreType.DMA((6,))]
    results = pl.pallas_call(
        functools.partial(gather_body, geo, infos, groups, inner),
        out_shape=outs,
        in_specs=[anywhere()] * 6 + [pl.BlockSpec(memory_space=pltpu.SMEM)] + [whole()] * 2,
        out_specs=[anywhere()] * 2 + [whole()] * (len(outs) - 2),
        scratch_shapes=scratch,
        compiler_params=pltpu.CompilerParams(
            collective_id=1, has_side_effects=True, vmem_limit_bytes=LIMIT
        ),
    )(*ins)
    return results[:4], results[4:13], results[13]


def scatter_body(info, groups, inner, *refs):
    grads, out = refs[0:9], refs[9]
    flat, parts, core_in, chip_sum, chip_in, line_sum, line_in = refs[10:17]
    core_send, core_recv, chip_send, chip_recv, line_send, line_recv = refs[17:]
    places = Places(groups, inner)
    barrier = pltpu.get_barrier_semaphore()
    places.greet(barrier)
    devices = groups * inner
    pack(info, flat, grads)
    for d in range(devices):
        place = parts.at[d // inner % 2, d // inner // 2, d % inner]
        place[0 : info.padded, :] = flat[info.share * d : info.share * d + info.padded, :].astype(BF16)
    places.greeted(barrier)
    order = [*range(1, inner), 0]
    copies = []

    def send(*args):
        copies.append(remote(*args))
        copies[-1].start()
        return copies[-1]

    core, chip, lines = {}, {}, []
    for step in order:
        z = places.along(step)
        core[step] = send(
            parts.at[1 - places.core, :, z], core_in.at[:, z], core_send.at[step], core_recv.at[step], places.sibling()
        )
    for step in order:
        z = places.along(step)
        core[step].wait_recv()
        for at in range(places.chips):
            value = parts[places.core, at, z].astype(F32) + core_in[at, z].astype(F32)
            chip_sum[at, z] = value.astype(BF16)
        chip[step] = []
        for over in range(1, places.chips):
            at = (over - 1) * inner + step
            chip[step].append(
                send(
                    chip_sum.at[places.across(over), z], chip_in.at[over - 1, z], chip_send.at[at], chip_recv.at[at],
                    places.other_chip(over),
                )
            )
    for step in order:
        z = places.along(step)
        value = chip_sum[places.chip, z].astype(F32)
        for over in range(1, places.chips):
            chip[step][over - 1].wait_recv()
            value = value + chip_in[over - 1, z].astype(F32)
        line_sum[z] = value.astype(BF16)
        if step:
            lines.append(
                send(
                    line_sum.at[z], line_in.at[step - 1], line_send.at[step - 1], line_recv.at[step - 1],
                    places.line(step),
                )
            )
    for copy in lines:
        copy.wait_recv()
    value = line_sum[places.inner].astype(F32)
    for step in range(inner - 1):
        value = value + line_in[step].astype(F32)
    out[...] = value[0 : info.share, :]
    for copy in copies:
        copy.wait_send()


def scatter(info, ins):
    groups, inner = lax.axis_size("dp"), lax.axis_size("fsdp")
    chips = groups // 2
    size = info.padded
    def part(*lead):
        return pltpu.VMEM((*lead, size, 128), BF16)
    out = pl.pallas_call(
        functools.partial(scatter_body, info, groups, inner),
        out_shape=shape((info.share, 128)),
        in_specs=[whole()] * len(ins),
        out_specs=whole(),
        scratch_shapes=[
            pltpu.VMEM((info.rows + 16, 128), F32),
            part(2, chips, inner), part(chips, inner), part(chips, inner), part(chips - 1, inner), part(inner),
            part(inner - 1),
        ]
        + [pltpu.SemaphoreType.DMA(dims) for dims in ((inner,), (inner,), *[((chips - 1) * inner,)] * 2, (inner - 1,), (inner - 1,))],
        compiler_params=pltpu.CompilerParams(
            collective_id=2, has_side_effects=True, vmem_limit_bytes=LIMIT
        ),
    )(*ins)
    return out.reshape(-1)


def restore_body(geo, *refs):
    number = len(geo.sides)
    g1, gs, out = (refs[k * number : (k + 1) * number] for k in range(3))
    w_in, w_short = refs[3 * number : 3 * number + 2]
    rest = refs[3 * number + 2 :]
    output_hbm, grad_hbm = rest[:number], rest[number : 2 * number]
    g1_in, gs_in, out_in, outputs, image_grads = (rest[(k + 2) * number : (k + 3) * number] for k in range(5))
    grad_cell, out_cell, in_sems, out_sems = rest[7 * number :]
    order = list(range(number))[::-1]
    loads, stores = {}, []
    for b in order:
        loads[b] = [
            pltpu.make_async_copy(source, target, in_sems.at[b, k])
            for k, (source, target) in enumerate(((g1[b], g1_in[b]), (gs[b], gs_in[b]), (out[b], out_in[b])))
        ]
        for load in loads[b]:
            load.start()
    for b in order:
        side = geo.sides[b]
        size = side * 16
        for load in loads[b]:
            load.wait()

        def line(i, carry, b=b, side=side, size=size):
            rows = aligned(i * size, size)
            out_cell[0:side] = out_in[b][rows, :].astype(F32).reshape(side, 16, WIDTH)
            for q in range(4):
                outputs[b][q // 2, i, q % 2] = out_cell[0:side, 4 * q : 4 * q + 4, :].astype(BF16)
            value = dot_nt(g1_in[b][:, rows, :].reshape(4 * size, WIDTH), w_in[...])
            grad_cell[:, 0:side] = value.reshape(4, side, 16, WIDTH_IN)
            grad_cell[0, 0:side] += dot_nt(gs_in[b][rows, :], w_short[...]).reshape(side, 16, WIDTH_IN)
            for plane in range(4):
                for q in range(4):
                    image_grads[b][q // 2, i, plane // 2, q % 2, :, plane % 2] = grad_cell[
                        plane, 0:side, 4 * q : 4 * q + 4, :
                    ]
            return carry

        cuts = [0, side // 2, side]
        for k in range(2):
            lax.fori_loop(cuts[k], cuts[k + 1], line, 0)
            some = pl.ds(cuts[k], cuts[k + 1] - cuts[k])
            for j, (source, target) in enumerate(((outputs[b], output_hbm[b]), (image_grads[b], grad_hbm[b]))):
                stores.append(pltpu.make_async_copy(source.at[:, some], target.at[:, some], out_sems.at[b, 2 * k + j]))
                stores[-1].start()
    for store in stores:
        store.wait()


def restore(geo, g1, gs, out, w_in, w_short):
    ins = [*g1, *gs, *out, w_in, w_short]
    sides = geo.sides
    out_dims = [(2, side, 2, side, 4, WIDTH) for side in sides]
    grad_dims = [(2, side, 2, 2, side, 2, 4, WIDTH_IN) for side in sides]
    most = max(sides)
    results = pl.pallas_call(
        functools.partial(restore_body, geo),
        out_shape=[shape(dims, BF16) for dims in out_dims] + [shape(dims) for dims in grad_dims],
        in_specs=[anywhere()] * 9 + [whole()] * 2,
        out_specs=[anywhere()] * 6,
        scratch_shapes=[pltpu.VMEM(value.shape, BF16) for value in ins[:9]]
        + [pltpu.VMEM(dims, BF16) for dims in out_dims]
        + [pltpu.VMEM(dims, F32) for dims in grad_dims]
        + [pltpu.VMEM((4, most, 16, WIDTH_IN), F32), pltpu.VMEM((most, 16, WIDTH), F32)]
        + [pltpu.SemaphoreType.DMA((3, 3)), pltpu.SemaphoreType.DMA((3, 4))],
        compiler_params=pltpu.CompilerParams(vmem_limit_bytes=LIMIT),
    )(*ins)
    grids = [
        result.reshape(scale * side, scale * side, 4, -1).transpose(2, 0, 1, 3)
        for result, side, scale in zip(results, sides * 2, [2] * 3 + [4] * 3)
    ]
    return grids


def per_device(*args):
    images, counts = args[0:3], args[3]
    cots = args[6:9]
    geo = Geometry([image.shape[1] // 4 for image in images])
    inner = lax.axis_size("fsdp")
    devices = lax.axis_size("dp") * inner
    infos = [Flat(k == 0, args[4 + k].shape[0] * devices, devices, inner) for k in range(2)]
    split_images = [
        image.transpose(1, 2, 0, 3).reshape(2, side, 2, 2, side, 2, 4, WIDTH_IN)
        for image, side in zip(images, geo.sides)
    ]
    split_cots = [
        value.transpose(1, 2, 0, 3).reshape(2, side, 2, side, 4, WIDTH) for value, side in zip(cots, geo.sides)
    ]
    (acts, cot, mask, live), first, line2 = gather(geo, infos, split_images, split_cots, counts, args[4:6])
    out, g1, gs, first_grads, second_out = blocks(geo, infos, acts, mask, live, first, line2, cot)
    return (
        *restore(geo, g1, gs, out, first[0], first[7]),
        scatter(infos[0], first_grads),
        second_out,
    )


def solution(mesh):
    images = P(("dp", "fsdp"), None, None, None)
    flat = P(("dp", "fsdp"))
    in_specs = (images, images, images, P(("dp", "fsdp"), None), flat, flat, images, images, images)
    out_specs = (images,) * 6 + (flat, flat)
    return jax.shard_map(per_device, mesh=mesh, in_specs=in_specs, out_specs=out_specs, check_vma=False)
```

```python
import functools
import math

import jax
import jax.numpy as jnp
from jax import lax
from jax.experimental import pallas as pl
from jax.experimental.pallas import tpu as pltpu
from jax.sharding import PartitionSpec as P

WIDTH_IN = 192
GROUPS = 8
GROUP_WIDTH = 64
SQUEEZE_A = 48
SQUEEZE_B = 128
WIDTH = 512
HALF = 256
ALL = slice(0, WIDTH)
HALVES = (slice(0, HALF), slice(HALF, WIDTH))
TAPS = 9
EPSILON = 1e-05
HIGHEST = lax.Precision.HIGHEST
MESH = pl.DeviceIdType.MESH
F32 = jnp.float32
BF16 = jnp.bfloat16
LIMIT = 127 * 2**19


def shapes_of(is_first):
    width_in, squeeze = (WIDTH_IN, SQUEEZE_A) if is_first else (WIDTH, SQUEEZE_B)
    shapes = [
        (width_in, WIDTH),
        (TAPS, GROUPS, GROUP_WIDTH, GROUP_WIDTH),
        (WIDTH, squeeze),
        (1, squeeze),
        (squeeze, WIDTH),
        (1, WIDTH),
        (WIDTH, WIDTH),
    ]
    if is_first:
        shapes.append((WIDTH_IN, WIDTH))
    shapes.append((8 if is_first else 6, WIDTH))
    return shapes


def diagonal(product):
    parts = []
    for g in range(4):
        lanes = slice(128 * (g // 2), 128 * (g // 2) + 128)
        parts.append(product[g * GROUP_WIDTH : (g + 1) * GROUP_WIDTH, lanes])
    return jnp.concatenate(parts, axis=0)


def dot(left, right):
    return jnp.dot(left, right, preferred_element_type=F32)


def dot_nt(left, right):
    return lax.dot_general(left, right, (((1,), (1,)), ((), ())), preferred_element_type=F32)


def dot_tn(left, right):
    return lax.dot_general(left, right, (((0,), (0,)), ((), ())), preferred_element_type=F32)


def exact(left, right, dims):
    return lax.dot_general(
        left, right, (dims, ((), ())), precision=HIGHEST, preferred_element_type=F32
    )


def by_parts(product, left, right):
    high = left.astype(BF16)
    rest = left - high.astype(F32)
    middle = rest.astype(BF16)
    low = (rest - middle.astype(F32)).astype(BF16)
    rows = left.shape[0]
    full = product(jnp.concatenate([high, middle, low], axis=0), right)
    return full[:rows] + full[rows : 2 * rows] + full[2 * rows :]


def half_silu(half):
    return half + half * jnp.tanh(half)


def half_silu_grad(half, tan):
    return (0.5 + 0.5 * tan) * (1.0 + half * (1.0 - tan))


def fold(values):
    return jnp.sum(values.reshape(-1, 8, values.shape[-1]), axis=0)


def down_to_row(values):
    return jnp.sum(values, axis=0, keepdims=True)


class Geometry:
    def __init__(self, sides):
        self.sides = sides
        self.rows = [side * side * 16 for side in sides]
        self.bases = [sum(self.rows[:b]) for b in range(len(sides))]
        self.total = sum(self.rows)

    def grid(self, extra_rows, extra_cols, start):
        bases = []
        for side in self.sides:
            bases.append(start)
            start = start + (side + extra_rows) * (side + extra_cols) * 16
        return bases, start


def exchange_stages(groups, inner):
    return [groups * inner] if groups * inner <= 64 else [inner, groups]


def aligned(start, size):
    if isinstance(start, int):
        return pl.ds(start, size)
    return pl.ds(pl.multiple_of(start, 16), size)


def body(geo, info, groups, inner, *refs):
    (
        acts_hbm, mask, count, w_in1, bd1, down1, downb1, up1, upb1, w_out1, w_short, norms1, line2, cot_hbm,
    ) = refs[:14]
    out_hbm, g1_hbm, gs_hbm = refs[14:17], refs[17:20], refs[20:23]
    (
        dwg1_hbm, second_out,
        dw_in1, ddown1, ddownb1, dup1, dupb1, dw_out1, dw_short, dnorms1,
    ) = refs[23:33]
    weights2, grads2 = refs[33:41], refs[41:48]
    w_in2, bd2, down2, downb2, up2, upb2, w_out2, norms2 = weights2
    dw_in2, ddown2, ddownb2, dup2, dupb2, dw_out2, dnorms2 = grads2
    (
        acts, acts_sem, tall, shares, pool, x0, x1, x2, x3, h2, mid, acc, vec, se1, sq1, se2, sq2,
        pay, slots, send_sem, recv_sem, half_pay, half_slots, half_send, half_recv, sems,
        near_send, near_recv, near_core_send, core_land, far_core, far_chip_send, far_chip_recv, far_line_send, far_line_recv,
    ) = refs[48:]
    exchange = ((pay, slots, send_sem, recv_sem), (half_pay, half_slots, half_send, half_recv))
    places = Places(groups, inner)
    loads = [pltpu.make_async_copy(acts_hbm.at[k], acts.at[k], acts_sem.at[k]) for k in range(4)]
    for load in loads:
        load.start()
    sides, bases, rows_of, total = geo.sides, geo.bases, geo.rows, geo.total
    buckets = range(len(sides))
    devices = groups * inner

    outer_index, inner_index = lax.axis_index("dp"), lax.axis_index("fsdp")

    def any_partner(step):
        other = lax.rem(outer_index * inner + inner_index + step, devices)
        return (other // inner, lax.rem(other, inner))

    def inner_partner(step):
        return (outer_index, lax.rem(inner_index + step, inner))

    def outer_partner(step):
        return (lax.rem(outer_index + step, groups), inner_index)

    barrier = pltpu.get_barrier_semaphore()
    stages = exchange_stages(groups, inner)
    if len(stages) == 1:
        partners = [any_partner]
    else:
        partners = [inner_partner, outer_partner]
    for count_in_stage, partner in zip(stages, partners):

        def greet(step, carry, partner=partner):
            pl.semaphore_signal(barrier, inc=1, device_id=partner(step), device_id_type=MESH)
            return carry

        lax.fori_loop(1, count_in_stage, greet, 0)

    calls = []

    def begin_sum(rows, place=None):
        if not calls:
            pl.semaphore_wait(barrier, sum(stages) - len(stages))
        kind = int(rows[0].shape[1] == HALF)
        if place is None:
            place = calls.count(kind) % (4 if kind else 2)
            calls.append(kind)
        buffers = exchange[kind]
        pay = buffers[0]
        for r, value in enumerate(rows):
            for c in range(value.shape[1] // 128):
                at = r * (value.shape[1] // 128) + c
                pay[place * len(stages), at : at + 1, :] = value[:, lane_tile(c)]
        send_stage(buffers, 0, place * len(stages))
        return kind, place, len(rows)

    def send_stage(buffers, stage, at):
        pay, slots, send_sem, recv_sem = buffers

        def send(step, carry):
            pltpu.make_async_remote_copy(
                src_ref=pay.at[at],
                dst_ref=slots.at[at, step - 1],
                send_sem=send_sem.at[at],
                recv_sem=recv_sem.at[at],
                device_id=partners[stage](step),
                device_id_type=MESH,
            ).start()
            return carry

        lax.fori_loop(1, stages[stage], send, 0)

    def finish_sum(begun):
        kind, place, number = begun
        buffers = exchange[kind]
        pay, slots, send_sem, recv_sem = buffers
        for stage in range(len(stages)):
            at = place * len(stages) + stage
            if stage:
                pay[at] = sums
                send_stage(buffers, stage, at)
            landed = slots.at[at, pl.ds(0, stages[stage] - 1)]
            pltpu.make_async_copy(landed, landed, recv_sem.at[at]).wait()
            sums = pay[at] + jnp.sum(slots[at, 0 : stages[stage] - 1], axis=0)
            pltpu.make_async_copy(landed, landed, send_sem.at[at]).wait()
        tiles = 2 if kind else 4
        return [
            jnp.concatenate([sums[tiles * r + c : tiles * r + c + 1, :] for c in range(tiles)], axis=1)
            for r in range(number)
        ]

    def each(step, carry):
        for b in buckets:
            def line(i, kept, b=b):
                size = sides[b] * 16
                return step(b, aligned(bases[b] + i * size, size), i, kept)
            def pair(j, kept, line=line):
                return line(2 * j + 1, line(2 * j, kept))
            carry = lax.fori_loop(0, sides[b] // 2, pair, carry)
            if sides[b] % 2:
                carry = line(sides[b] - 1, carry)
        return carry

    zero8 = jnp.zeros((8, WIDTH), F32)

    zero_half = jnp.zeros((8, HALF), F32)

    def masked(values, b):
        width = values.shape[-1]
        return (values.reshape(-1, 16, width) * mask[b, :, 0:width][None]).reshape(values.shape)

    def set_norm(k, sums, squares, norms, index, live, lanes=ALL):
        live = live[:, lanes]
        mean = sums / live
        inv_std = lax.rsqrt(squares / live - mean * mean + EPSILON)
        scale = inv_std * norms[2 * index : 2 * index + 1, lanes]
        offset = norms[2 * index + 1 : 2 * index + 2, lanes] - mean * scale
        for r, value in enumerate((mean, inv_std, scale, offset, 0.5 * scale, 0.5 * offset)):
            vec[6 * k + r : 6 * k + r + 1, lanes] = value

    def row(k, r, lanes=ALL):
        return vec[6 * k + r : 6 * k + r + 1, lanes]

    def half(k, u, lanes=ALL):
        return u * row(k, 4, lanes) + row(k, 5, lanes)

    def set_grad(k, sum_g, sum_d, live, at=48, lanes=ALL):
        live = live[:, lanes]
        scale, inv_std = row(k, 2, lanes), row(k, 1, lanes)
        on_u = -scale * inv_std * inv_std * sum_d / live
        vec[at : at + 1, lanes] = scale
        vec[at + 1 : at + 2, lanes] = on_u
        vec[at + 2 : at + 3, lanes] = -scale * sum_g / live - row(k, 0, lanes) * on_u

    def grad_u(g, u, b, at=48, lanes=ALL):
        inner_grad = g * vec[at : at + 1, lanes] + (u * vec[at + 1 : at + 2, lanes] + vec[at + 2 : at + 3, lanes])
        return masked(inner_grad, b).astype(BF16)

    def keep_and_fold(x, rows, lanes, u, carry):
        x[rows, lanes] = u
        return carry[0] + fold(u), carry[1] + fold(u * u)

    def begin_stats(carry):
        return begin_sum([down_to_row(v) for v in carry])

    def begin_dot_stats(x, left, weight):
        begun = []
        for lanes in HALVES:
            carry = (zero_half, zero_half)
            for rows in (slice(0, bases[-1]), slice(bases[-1], total)):
                carry = keep_and_fold(x, rows, lanes, dot(left[rows, :], weight[:, lanes]), carry)
            begun.append(begin_stats(carry))
        return begun

    def window(base, width, b, r0, c0, lanes, lines=None):
        side = sides[b]
        return jnp.concatenate(
            [
                pool[base + ((r0 + i) * width + c0) * 16 : base + ((r0 + i) * width + c0 + side) * 16, lanes]
                for i in lines or range(side)
            ],
            axis=0,
        )

    def pattern(size, bit, value):
        index = lax.broadcasted_iota(jnp.int32, (size, HALF), 0)
        return ((index // bit) % 2 == value).astype(F32)

    def fill_halo(base, b, low_r, high_r, low_c, high_c, lanes):
        side = sides[b]
        width = side + low_c + high_c
        def cell(r, c, n=1):
            return slice(base + (r * width + c) * 16, base + (r * width + c + n) * 16)
        def shifted(source, target, shift, keep):
            value = pool[source, lanes].astype(F32)
            pool[target, lanes] = (pltpu.roll(value, shift, 0) * keep).astype(BF16)
        for i in range(side):
            r = i + low_r
            if low_c:
                shifted(cell(r, side), cell(r, 0), 4, pattern(16, 4, 1))
            if high_c:
                shifted(cell(r, low_c), cell(r, width - 1), 12, pattern(16, 4, 0))
        size = width * 16
        if low_r:
            shifted(cell(side, 0, width), cell(0, 0, width), 8, pattern(size, 8, 1))
        if high_r:
            shifted(cell(low_r, 0, width), cell(low_r + side, 0, width), size - 8, pattern(size, 8, 0))

    first_of_image = (lax.broadcasted_iota(jnp.int32, (48, WIDTH), 0) % 16 < 4).astype(F32)

    def over_quadrants(v):
        return v + pltpu.roll(v, 4, 0) + pltpu.roll(v, 8, 0) + pltpu.roll(v, 12, 0)

    def squeeze_excite(x, k, begun, norms, down, downb, up, upb, se, sq):
        zero16 = jnp.zeros((16, HALF), F32)
        found = []
        for lanes, part in zip(HALVES, begun):
            set_norm(k, *finish_sum(part), norms, 1, live, lanes)
            def step(b, rows, i, carry, lanes=lanes):
                v = half_silu(half(k, x[rows, lanes], lanes)).reshape(-1, 16, HALF)
                return tuple(c + jnp.sum(v, axis=0) if d == b else c for d, c in enumerate(carry))
            found.append(each(step, tuple(zero16 for _ in buckets)))
        sums = [jnp.concatenate([left, right], axis=1) for left, right in zip(*found)]
        pooled = jnp.concatenate(
            [over_quadrants(s) * (1.0 / (4 * side * side)) for s, side in zip(sums, sides)], axis=0
        )
        squeeze_pre = by_parts(dot, pooled, down[...]) + downb[...]
        squeezed = squeeze_pre * jax.nn.sigmoid(squeeze_pre)
        excite = jax.nn.sigmoid(by_parts(dot, squeezed, up[...]) + upb[...])
        se[0] = pooled
        sq[...] = squeeze_pre
        for b in buckets:
            se[1, 16 * b : 16 * b + 16, :] = excite[16 * b : 16 * b + 16, :] * mask[b]

    def gate(x, k, se, store):
        def step(b, rows, i, carry):
            v = half_silu(half(k, x[rows, :])).reshape(-1, 16, WIDTH)
            v = v * se[1, 16 * b : 16 * b + 16, :][None]
            store(rows, v.reshape(-1, WIDTH).astype(BF16))
            return carry
        each(step, 0)

    def squeeze_excite_back(g, u, k, down, up, se, sq, ddown, ddownb, dup, dupb, norm_grads):
        def step(b, rows, i, carry):
            v = half_silu(half(k, u[rows, :])) * g[rows, :]
            return tuple(
                c + jnp.sum(v.reshape(-1, 16, WIDTH), axis=0) if d == b else c
                for d, c in enumerate(carry)
            )
        zero16 = jnp.zeros((16, WIDTH), F32)
        sums = each(step, tuple(zero16 for _ in buckets))
        grad_excite = jnp.concatenate([over_quadrants(s) for s in sums], axis=0)
        excite = se[1]
        grad_up = grad_excite * excite * (1.0 - excite)
        squeeze_pre = sq[...]
        sig = jax.nn.sigmoid(squeeze_pre)
        once = first_of_image
        dup[...] = exact(squeeze_pre * sig, grad_up * once, ((0,), (0,)))
        dupb[...] = down_to_row(grad_up * once)
        grad_pre = by_parts(dot_nt, grad_up, up[...]) * (sig * (1.0 + squeeze_pre * (1.0 - sig)))
        ddown[...] = exact(se[0] * once, grad_pre, ((0,), (0,)))
        ddownb[...] = down_to_row(grad_pre * once[:, : grad_pre.shape[1]])
        pooled_grad = by_parts(dot_nt, grad_pre, down[...])
        for b in buckets:
            pixels = 4 * sides[b] * sides[b]
            vec[56 + 16 * b : 72 + 16 * b, :] = pooled_grad[16 * b : 16 * b + 16, :] * (1.0 / pixels)

        begun = []
        for lanes in HALVES:
            def apply(b, rows, i, carry, lanes=lanes):
                u_now = u[rows, lanes]
                y = half(k, u_now, lanes)
                slope = half_silu_grad(y, jnp.tanh(y))
                gv = g[rows, lanes].reshape(-1, 16, HALF) * se[1, 16 * b : 16 * b + 16, lanes][None]
                gv = (gv + vec[56 + 16 * b : 72 + 16 * b, lanes][None]).reshape(-1, HALF) * slope
                g[rows, lanes] = gv
                return carry[0] + fold(gv), carry[1] + fold(gv * (u_now - row(k, 0, lanes)))

            local = [down_to_row(v) for v in each(apply, (zero_half, zero_half))]
            put_norm_grads(norm_grads, 1, k, *local, lanes)
            begun.append(begin_sum(local))
        return begun

    def put_norm_grads(out, index, k, sum_g, sum_d, lanes=ALL):
        out[2 * index : 2 * index + 1, lanes] = row(k, 1, lanes) * sum_d
        out[2 * index + 1 : 2 * index + 2, lanes] = sum_g

    planes = [(0, 0), (0, 1), (1, 0), (1, 1)]

    chunk = total // 5
    wide = [x0, x1, x2, x3]

    def stat_dot(plane, weight, out, lanes, carry):
        def step(i, kept):
            rows = aligned(i * chunk, chunk)
            u = dot(acts[plane, rows, :], weight[:, lanes])
            if out is not None:
                out[rows, lanes] = u
            return kept[0] + fold(u), kept[1] + fold(u * u)
        return lax.fori_loop(0, 5, step, carry, unroll=True)

    one = []
    for lanes in HALVES:
        carry = (zero_half, zero_half)
        for plane in range(4):
            if len(one) == 0:
                loads[plane].wait()
            carry = stat_dot(plane, w_in1, wide[plane], lanes, carry)
        one.append(begin_sum([down_to_row(v) for v in carry]))
    short = begin_sum([down_to_row(v) for v in stat_dot(0, w_short, None, ALL, (zero8, zero8))], 2)
    live = count[...]
    vec[54:55, :] = live

    end = 0
    h1_bases = []
    for pr, pc in planes:
        grid_bases, end = geo.grid(pr, pc, end)
        h1_bases.append(grid_bases)
    second = SecondGather(
        info, places, line2, pool, end, (near_send, near_recv, near_core_send, core_land)
    )
    two = []
    for h, lanes in enumerate(HALVES):
        set_norm(0, *finish_sum(one[h]), norms1, 0, 4.0 * live, lanes)
        if h == 0:
            second.begin()
        for plane, (pr, pc) in enumerate(planes):
            def step(b, rows, i, carry, plane=plane, pr=pr, pc=pc, lanes=lanes):
                width = sides[b] + pc
                start = h1_bases[plane][b] + ((i + pr) * width + pc) * 16
                value = half_silu(half(0, wide[plane][rows, lanes], lanes))
                pool[aligned(start, sides[b] * 16), lanes] = masked(value, b).astype(BF16)
                return carry
            each(step, 0)
            for b in buckets:
                fill_halo(h1_bases[plane][b], b, pr, 0, pc, 0, lanes)
        carry = (zero_half, zero_half)
        for b in buckets:
            parts = []
            for tap in range(TAPS):
                dy, dx = tap // 3, tap % 3
                pr, pc = int(dy != 1), int(dx != 1)
                parts.append(
                    window(h1_bases[2 * pr + pc][b], sides[b] + pc, b, int(dy == 2), int(dx == 2), lanes)
                )
            u = dot(jnp.concatenate(parts, axis=1), bd1[h].reshape(TAPS * HALF, HALF))
            carry = keep_and_fold(x0, slice(bases[b], bases[b] + rows_of[b]), lanes, u, carry)
        two.append(begin_stats(carry))
    h1b_bases, end = geo.grid(2, 2, 0)
    g2b_bases, end = geo.grid(2, 2, end)
    h2b, cot_at = end, end + total
    g3b = cot_at
    second.pass_on()
    live = vec[54:55, :]
    squeeze_excite(x0, 1, two, norms1, down1, downb1, up1, upb1, se1, sq1)
    def keep_h2(rows, value):
        h2[rows, :] = value
    gate(x0, 1, se1, keep_h2)
    begun = begin_dot_stats(x1, h2, w_out1)
    x2[...] = dot(acts[0], w_short[...])
    second.finish(x3, shares, tall, weights2)
    fetch = pltpu.make_async_copy(cot_hbm, pool.at[pl.ds(cot_at, total)], sems.at[0])
    fetch.start()
    sums = finish_sum(short)
    set_norm(3, sums[0], sums[1], norms1, 3, live)
    for lanes, part in zip(HALVES, begun):
        set_norm(2, *finish_sum(part), norms1, 2, live, lanes)
    def middle(b, rows, i, carry):
        y = half(2, x1[rows, :]) + half(3, x2[rows, :])
        mid[rows, :] = masked(half_silu(y), b).astype(BF16)
        return carry
    each(middle, 0)

    one = begin_dot_stats(x2, mid, w_in2)
    two = []
    for h, lanes in enumerate(HALVES):
        set_norm(4, *finish_sum(one[h]), norms2, 0, live, lanes)
        def hidden(b, rows, i, carry, lanes=lanes):
            start = h1b_bases[b] + ((i + 1) * (sides[b] + 2) + 1) * 16
            value = half_silu(half(4, x2[rows, lanes], lanes))
            pool[aligned(start, sides[b] * 16), lanes] = masked(value, b).astype(BF16)
            return carry
        each(hidden, 0)
        carry = (zero_half, zero_half)
        for b in buckets:
            fill_halo(h1b_bases[b], b, 1, 1, 1, 1, lanes)
            parts = [
                window(h1b_bases[b], sides[b] + 2, b, tap // 3, tap % 3, lanes) for tap in range(TAPS)
            ]
            u = dot(jnp.concatenate(parts, axis=1), bd2[h].reshape(TAPS * HALF, HALF))
            carry = keep_and_fold(x3, slice(bases[b], bases[b] + rows_of[b]), lanes, u, carry)
        two.append(begin_stats(carry))
    squeeze_excite(x3, 5, two, norms2, down2, downb2, up2, upb2, se2, sq2)
    def keep_h2b(rows, value):
        pool[aligned(rows.start + h2b, rows.size), :] = value
    gate(x3, 5, se2, keep_h2b)
    begun = begin_dot_stats(x1, pool.at[pl.ds(h2b, total)], w_out2)
    fetch.wait()
    out_at = g2b_bases[0]
    three = []
    for lanes, part in zip(HALVES, begun):
        set_norm(6, *finish_sum(part), norms2, 2, live, lanes)
        def finish(b, rows, i, carry, lanes=lanes):
            u = x1[rows, lanes]
            y = half(6, u, lanes) + 0.5 * mid[rows, lanes].astype(F32)
            tan = jnp.tanh(y)
            pool[aligned(rows.start + out_at, rows.size), lanes] = masked(y + y * tan, b).astype(BF16)
            g = pool[aligned(rows.start + cot_at, rows.size), lanes].astype(F32) * half_silu_grad(y, tan)
            x2[rows, lanes] = g
            return carry[0] + fold(g), carry[1] + fold(g * (u - row(6, 0, lanes)))
        local = [down_to_row(v) for v in each(finish, (zero_half, zero_half))]
        put_norm_grads(dnorms2, 2, 6, *local, lanes)
        three.append(begin_sum(local))
    puts = [
        pltpu.make_async_copy(pool.at[pl.ds(out_at + bases[b], rows_of[b])], out_hbm[b], sems.at[2 + b])
        for b in buckets
    ]
    for put in puts:
        put.start()

    for lanes, part in zip(HALVES, three):
        set_grad(6, *finish_sum(part), live, lanes=lanes)
        def third(b, rows, i, carry, lanes=lanes):
            value = grad_u(x2[rows, lanes], x1[rows, lanes], b, lanes=lanes)
            pool[aligned(rows.start + g3b, rows.size), lanes] = value
            return carry
        each(third, 0)
    x1[...] = dot_nt(pool[g3b : g3b + total, :], w_out2[...])
    two = squeeze_excite_back(x1, x3, 5, down2, up2, se2, sq2, ddown2, ddownb2, dup2, dupb2, dnorms2)
    dw_out2[...] = dot_tn(pool[h2b : h2b + total, :], pool[g3b : g3b + total, :])
    for put in puts:
        put.wait()
    for h, lanes in enumerate(HALVES):
        set_grad(5, *finish_sum(two[h]), live, lanes=lanes)
        def second_u(b, rows, i, carry, lanes=lanes):
            start = g2b_bases[b] + ((i + 1) * (sides[b] + 2) + 1) * 16
            pool[aligned(start, sides[b] * 16), lanes] = grad_u(x1[rows, lanes], x3[rows, lanes], b, lanes=lanes)
            return carry
        each(second_u, 0)
        for b in buckets:
            fill_halo(g2b_bases[b], b, 1, 1, 1, 1, lanes)
            parts = [
                window(g2b_bases[b], sides[b] + 2, b, 2 - tap // 3, 2 - tap % 3, lanes) for tap in range(TAPS)
            ]
            x1[bases[b] : bases[b] + rows_of[b], lanes] = dot_nt(
                jnp.concatenate(parts, axis=1),
                jnp.concatenate([bd2[h, tap] for tap in range(TAPS)], axis=1),
            )
    x3[...] = dot(mid[...], w_in2[...])
    def first(b, rows, i, carry):
        u = x3[rows, :]
        y = half(4, u)
        g = x1[rows, :] * half_silu_grad(y, jnp.tanh(y))
        x1[rows, :] = g
        return carry[0] + fold(g), carry[1] + fold(g * (u - row(4, 0)))
    local = [down_to_row(v) for v in each(first, (zero8, zero8))]
    put_norm_grads(dnorms2, 0, 4, *local)
    begun = begin_sum(local)
    for h, lanes in enumerate(HALVES):
        source = jnp.concatenate(
            [window(h1b_bases[b], sides[b] + 2, b, 1, 1, lanes) for b in buckets], axis=0
        )
        for tap in range(TAPS):
            target = jnp.concatenate(
                [window(g2b_bases[b], sides[b] + 2, b, 2 - tap // 3, 2 - tap % 3, lanes) for b in buckets],
                axis=0,
            )
            acc[tap, h] = diagonal(dot_tn(source, target))
    set_grad(4, *finish_sum(begun), live)
    def first_u(b, rows, i, carry):
        pool[aligned(rows.start + g3b, rows.size), :] = grad_u(x1[rows, :], x3[rows, :], b)
        return carry
    each(first_u, 0)
    x2[...] = x2[...] + dot_nt(pool[g3b : g3b + total, :], w_in2[...])

    x3[...] = dot(h2[...], w_out1[...])
    x1[...] = dot(acts[0], w_short[...])
    def joined(b, rows, i, carry):
        u, s = x3[rows, :], x1[rows, :]
        y = half(2, u) + half(3, s)
        g = x2[rows, :] * half_silu_grad(y, jnp.tanh(y))
        x2[rows, :] = g
        return (
            carry[0] + fold(g),
            carry[1] + fold(g * (u - row(2, 0))),
            carry[2] + fold(g * (s - row(3, 0))),
        )
    local = [down_to_row(v) for v in each(joined, (zero8, zero8, zero8))]
    put_norm_grads(dnorms1, 2, 2, local[0], local[1])
    put_norm_grads(dnorms1, 3, 3, local[0], local[2])
    begun = begin_sum(local[:2])
    short = begin_sum(local[2:], 2)
    dw_in2[...] = dot_tn(mid[...], pool[g3b : g3b + total, :])
    g2_bases, g1_at = geo.grid(1, 1, 0)
    back = SecondScatter(
        info, places, pool, g1_at, h2b, (far_core, far_chip_send, far_chip_recv, far_line_send, far_line_recv)
    )
    back.begin(shares, acc, grads2)
    sums = finish_sum(begun)
    set_grad(2, *sums, live)
    sum_g = sums[0]
    def third_one(b, rows, i, carry):
        pool[rows, :] = grad_u(x2[rows, :], x3[rows, :], b)
        return carry
    each(third_one, 0)
    x3[...] = dot_nt(pool[0:total, :], w_out1[...])
    two = squeeze_excite_back(x3, x0, 1, down1, up1, se1, sq1, ddown1, ddownb1, dup1, dupb1, dnorms1)
    set_grad(3, sum_g, *finish_sum(short), live, 51)
    def shortcut(b, rows, i, carry):
        mid[rows, :] = grad_u(x2[rows, :], x1[rows, :], b, 51)
        return carry
    each(shortcut, 0)
    puts = [
        pltpu.make_async_copy(mid.at[pl.ds(bases[b], rows_of[b])], gs_hbm[b], sems.at[2 + b]) for b in buckets
    ]
    for put in puts:
        put.start()
    dw_short[...] = dot_tn(acts[0], mid[...])
    dw_out1[...] = dot_tn(h2[...], pool[0:total, :])
    for lanes, part in zip(HALVES, two):
        set_grad(1, *finish_sum(part), live, lanes=lanes)
    def second_one(b, rows, i, carry):
        start = g2_bases[b] + (i * (sides[b] + 1)) * 16
        pool[aligned(start, sides[b] * 16), :] = grad_u(x3[rows, :], x0[rows, :], b)
        return carry
    each(second_one, 0)
    for b in buckets:
        for lanes in HALVES:
            fill_halo(g2_bases[b], b, 0, 1, 0, 1, lanes)

    def group_grads(taps, b, h2_at):
        for h, lanes in enumerate(HALVES):
            source = h2[h2_at : h2_at + rows_of[b], lanes]
            for tap in taps:
                target = window(g2_bases[b], sides[b] + 1, b, int(tap // 3 == 0), int(tap % 3 == 0), lanes)
                if b == 0:
                    acc[tap, h] = diagonal(dot_tn(source, target))
                else:
                    acc[tap, h] += diagonal(dot_tn(source, target))

    back.across_chips()
    carry = (zero8, zero8)
    kept = [x1, x2, x3]
    apart = max(rows_of[:-1])
    for plane, (pr, pc) in enumerate(planes):
        taps = [
            tap for tap in range(TAPS) if int(tap // 3 != 1) == pr and int(tap % 3 != 1) == pc
        ]
        for b in buckets:
            side = sides[b]
            pieces = [(0, side)]
            if plane == 3 and rows_of[b] > apart:
                pieces = [(0, side // 2), (side // 2, side)]
            h2_at = bases[b] if plane == 3 else 0
            for first_line, end_line in pieces:
                at, size = first_line * side * 16, (end_line - first_line) * side * 16
                x0[0:size, :] = dot(acts[plane, bases[b] + at : bases[b] + at + size, :], w_in1[...])
                grads_at, grads = (bases[b], kept[plane]) if plane < 3 else (apart, x0)
                for h, lanes in enumerate(HALVES):
                    parts = [
                        window(
                            g2_bases[b], side + 1, b, int(tap // 3 == 0), int(tap % 3 == 0), lanes,
                            range(first_line, end_line),
                        )
                        for tap in taps
                    ]
                    grads[grads_at : grads_at + size, lanes] = dot_nt(
                        jnp.concatenate(parts, axis=1), jnp.concatenate([bd1[h, tap] for tap in taps], axis=1)
                    )
                def line(i, sums, b=b, plane=plane, at=at, h2_at=h2_at, grads=grads, grads_at=grads_at):
                    size = sides[b] * 16
                    u = x0[aligned(i * size, size), :]
                    y = half(0, u)
                    tan = jnp.tanh(y)
                    h2[aligned(h2_at + at + i * size, size), :] = masked(y + y * tan, b).astype(BF16)
                    here = aligned(grads_at + i * size, size)
                    g = grads[here, :] * half_silu_grad(y, tan)
                    if plane < 3:
                        grads[here, :] = g
                    else:
                        start = g1_at + plane * total + bases[b] + at + i * size
                        pool[aligned(start, size), :] = g.astype(BF16)
                    return sums[0] + fold(g), sums[1] + fold(g * (u - row(0, 0)))
                carry = lax.fori_loop(0, end_line - first_line, line, carry)
            if plane < 3:
                group_grads(taps, b, 0)
        if plane == 1:
            back.along_line()
    local = [down_to_row(v) for v in carry]
    put_norm_grads(dnorms1, 0, 0, *local)
    begun = begin_sum(local)
    for b in buckets:
        group_grads(taps, b, bases[b])
    back.finish(second_out)
    put_group1 = pltpu.make_async_copy(acc, dwg1_hbm, sems.at[1])
    put_group1.start()
    set_grad(0, *finish_sum(begun), 4.0 * live)
    for plane in range(4):
        x0[...] = dot(acts[plane], w_in1[...])
        at = g1_at + plane * total
        def first_one(b, rows, i, carry, at=at, plane=plane):
            here = aligned(rows.start + at, rows.size)
            g = kept[plane][rows, :] if plane < 3 else pool[here, :].astype(F32)
            pool[here, :] = grad_u(g, x0[rows, :], b)
            return carry
        each(first_one, 0)
        part = dot_tn(acts[plane], pool[at : at + total, :])
        if plane == 0:
            dw_in1[...] = part
        else:
            dw_in1[...] += part
        for b in buckets:
            put = pltpu.make_async_copy(
                pool.at[pl.ds(at + bases[b], rows_of[b])], g1_hbm[b].at[plane], sems.at[5 + 3 * plane + b]
            )
            put.start()
            puts.append(put)
    for put in puts:
        put.wait()
    put_group1.wait()


def whole():
    return pl.BlockSpec(memory_space=pltpu.VMEM)


def anywhere():
    return pl.BlockSpec(memory_space=pl.ANY)


def shape(dims, dtype=F32):
    return jax.ShapeDtypeStruct(dims, dtype)


def blocks(geo, infos, acts, mask, count, first, line2, cot):
    groups, inner = lax.axis_size("dp"), lax.axis_size("fsdp")
    total = geo.total
    ins = [acts, mask, count, *first, line2, cot]
    info = infos[1]
    hbm_outs = [
        *[shape((rows, WIDTH), BF16) for rows in geo.rows],
        *[shape((4, rows, WIDTH), BF16) for rows in geo.rows],
        *[shape((rows, WIDTH), BF16) for rows in geo.rows],
        shape((TAPS, 2, HALF, 128)),
    ]
    vmem_outs = [shape((info.share, 128))]
    vmem_outs += [shape(d) for j, d in enumerate(shapes_of(True)) if j != 1]
    second = shapes_of(False)
    pool_rows = 0
    for pr, pc in ((0, 0), (0, 1), (1, 0), (1, 1)):
        pool_rows = geo.grid(pr, pc, pool_rows)[1]
    pool_rows = pool_rows + groups * info.block
    pool_rows = max(
        pool_rows, geo.grid(2, 2, geo.grid(2, 2, 0)[1])[1] + 2 * total, geo.grid(1, 1, 0)[1] + 4 * total
    )
    stages = exchange_stages(groups, inner)
    big = pltpu.VMEM((total, WIDTH), F32)
    scratch = [pltpu.VMEM(second[0], BF16), pltpu.VMEM((2, TAPS, HALF, HALF), BF16)]
    scratch += [pltpu.VMEM(d, F32 if d[0] == 1 else BF16) for d in second[2:-1]] + [pltpu.VMEM(second[-1], F32)]
    scratch += [pltpu.VMEM(d, F32) for j, d in enumerate(second) if j != 1]
    chips = groups // 2
    scratch += [
        pltpu.VMEM(acts.shape, BF16), pltpu.SemaphoreType.DMA((4,)),
        pltpu.VMEM((WIDTH, 128), F32), pltpu.VMEM((2, info.padded, 128), F32),
        pltpu.VMEM((pool_rows, WIDTH), BF16), big, big, big, big,
        pltpu.VMEM((total, WIDTH), BF16), pltpu.VMEM((total, WIDTH), BF16),
        pltpu.VMEM((TAPS, 2, HALF, 128), F32), pltpu.VMEM((104, WIDTH), F32),
        pltpu.VMEM((2, 48, WIDTH), F32), pltpu.VMEM((48, SQUEEZE_A), F32),
        pltpu.VMEM((2, 48, WIDTH), F32), pltpu.VMEM((48, SQUEEZE_B), F32),
        pltpu.VMEM((3 * len(stages), 8, 128), F32),
        pltpu.VMEM((3 * len(stages), max(stages) - 1, 8, 128), F32),
        pltpu.SemaphoreType.DMA((3 * len(stages),)), pltpu.SemaphoreType.DMA((3 * len(stages),)),
        pltpu.VMEM((4 * len(stages), 4, 128), F32),
        pltpu.VMEM((4 * len(stages), max(stages) - 1, 4, 128), F32),
        pltpu.SemaphoreType.DMA((4 * len(stages),)), pltpu.SemaphoreType.DMA((4 * len(stages),)),
        pltpu.SemaphoreType.DMA((17,)),
    ]
    scratch += [
        pltpu.SemaphoreType.DMA(dims)
        for dims in (
            (chips - 1,), (chips - 1,), (chips,), (), (2,), (chips - 1,), (chips - 1,), (inner - 1,), (inner - 1,)
        )
    ]
    outs = pl.pallas_call(
        functools.partial(body, geo, info, groups, inner),
        out_shape=hbm_outs + vmem_outs,
        in_specs=[anywhere()] + [whole()] * 12 + [anywhere()],
        out_specs=[anywhere()] * len(hbm_outs) + [whole()] * len(vmem_outs),
        scratch_shapes=scratch,
        compiler_params=pltpu.CompilerParams(
            collective_id=0, has_side_effects=True, vmem_limit_bytes=LIMIT
        ),
    )(*ins)
    first_grads = [outs[11], outs[9], *outs[12:]]
    return outs[0:3], outs[3:6], outs[6:9], first_grads, outs[10].reshape(-1)


class Flat:
    def __init__(self, is_first, full_length, devices, inner):
        self.shapes = shapes_of(is_first)
        self.starts = []
        offset = 0
        for dims in self.shapes:
            self.starts.append(offset // 128)
            offset = offset + math.prod(dims)
        self.skew = offset % 128
        self.used = offset
        self.rows = full_length // 128
        self.share = self.rows // devices
        self.padded = -(-(self.share + 3) // 16) * 16
        self.layers = -(-inner // 4)
        self.block = self.layers * self.padded


def first_lanes(limit, dims):
    return lax.broadcasted_iota(jnp.int32, dims, 1) < limit


def column_pick(b):
    row = lax.broadcasted_iota(jnp.int32, (384, SQUEEZE_A), 0)
    column = lax.broadcasted_iota(jnp.int32, (384, SQUEEZE_A), 1)
    return (row == column + SQUEEZE_A * b).astype(F32)


def unskew(info, flat):
    row = info.starts[4]
    while row < info.rows:
        size = min(256, info.rows - row)
        here = pltpu.roll(flat[row : row + size, :], 128 - info.skew, 1)
        after = pltpu.roll(flat[row + 1 : row + size + 1, :], 128 - info.skew, 1)
        flat[row : row + size, :] = jnp.where(first_lanes(128 - info.skew, (size, 128)), here, after)
        row = row + size


def reskew(info, flat):
    row = info.rows
    first = info.starts[4]
    while row > first:
        size = min(256, row - first)
        start = row - size
        here = pltpu.roll(flat[start:row, :], info.skew, 1)
        if start == first:
            ahead = pltpu.roll(flat[start : row, :], info.skew, 1)
            ahead = pltpu.roll(ahead, 1, 0)
            keep = flat[info.rows + 8 : info.rows + 9, :]
            is_top = lax.broadcasted_iota(jnp.int32, (size, 128), 0) == 0
            ahead = jnp.where(is_top, jnp.broadcast_to(keep, (size, 128)), ahead)
        else:
            ahead = pltpu.roll(flat[start - 1 : row - 1, :], info.skew, 1)
        flat[start:row, :] = jnp.where(first_lanes(info.skew, (size, 128)), ahead, here)
        row = start


def unpack(info, flat, block_pad, outs):
    def wide(out, start):
        rows = out.shape[0]
        for c in range(4):
            out[:, c * 128 : (c + 1) * 128] = flat[pl.ds(start + c, rows, stride=4), :].astype(out.dtype)

    starts = info.starts
    w_in, bd, down, downb, up, upb, w_out = outs[:7]
    wide(w_in, starts[0])
    row = lax.broadcasted_iota(jnp.int32, (128, HALF), 0) // 32
    lane = lax.broadcasted_iota(jnp.int32, (128, HALF), 1) // GROUP_WIDTH
    on_diagonal = (row == lane).astype(F32)

    def spread(index, carry):
        rows = flat[pl.ds(pl.multiple_of(starts[1] + index * 128, 8), 128), :]
        turned = pltpu.roll(rows, GROUP_WIDTH, 1)
        left = first_lanes(GROUP_WIDTH, (128, 128))
        for parity, pair in enumerate((jnp.where(left, rows, turned), jnp.where(left, turned, rows))):
            tiled = jnp.concatenate([pair, pair], axis=1) * on_diagonal
            block_pad[pl.ds(parity, 128, stride=2), :] = tiled[:, :128]
            block_pad[pl.ds(HALF + parity, 128, stride=2), :] = tiled[:, 128:]
        bd[index % 2, index // 2, :, 0:128] = block_pad[0:HALF, :].astype(BF16)
        bd[index % 2, index // 2, :, 128:HALF] = block_pad[HALF : 2 * HALF, :].astype(BF16)
        return carry

    lax.fori_loop(0, 2 * TAPS, spread, 0)
    if down.shape[1] == 128:
        down[...] = flat[starts[2] : starts[2] + WIDTH, :].astype(BF16)
    else:
        joined = jnp.concatenate([flat[pl.ds(starts[2] + q, 64, stride=3), :] for q in range(3)], axis=1)
        for b in range(8):
            block_pad[pl.ds(b, 64, stride=8), 0:SQUEEZE_A] = dot(joined, column_pick(b))
        down[...] = block_pad[:, 0:SQUEEZE_A].astype(BF16)
    downb[...] = flat[starts[3] : starts[3] + 1, 0 : downb.shape[1]]
    if info.skew:
        unskew(info, flat)
    wide(up, starts[4])
    upb[...] = jnp.concatenate([flat[starts[5] + c : starts[5] + c + 1, :] for c in range(4)], axis=1)
    wide(w_out, starts[6])
    if len(outs) == 9:
        wide(outs[7], starts[7])
    wide(outs[-1], starts[-1])


def pack(info, flat, grads):
    def wide(value, start):
        rows = value.shape[0]
        for c in range(4):
            flat[pl.ds(start + c, rows, stride=4), :] = value[:, c * 128 : (c + 1) * 128]

    starts = info.starts
    d_in, dwg, ddown, ddownb, dup, dupb, d_out = grads[:7]
    flat[info.used // 128 // 8 * 8 : info.rows, :] = jnp.zeros_like(flat[info.used // 128 // 8 * 8 : info.rows, :])
    wide(d_in, starts[0])
    group_odd = lax.broadcasted_iota(jnp.int32, (128, 128), 0) // 32 % 2 == 1
    left = first_lanes(GROUP_WIDTH, (128, 128))

    def collect(index, carry):
        even = dwg[index // 2, index % 2, pl.ds(0, 128, stride=2), :]
        odd = dwg[index // 2, index % 2, pl.ds(1, 128, stride=2), :]
        even_turned, odd_turned = pltpu.roll(even, GROUP_WIDTH, 1), pltpu.roll(odd, GROUP_WIDTH, 1)
        rows = jnp.where(
            group_odd, jnp.where(left, even_turned, odd), jnp.where(left, even, odd_turned)
        )
        flat[pl.ds(pl.multiple_of(starts[1] + index * 128, 8), 128), :] = rows
        return carry

    lax.fori_loop(0, 2 * TAPS, collect, 0)
    if ddown.shape[1] == 128:
        flat[starts[2] : starts[2] + WIDTH, :] = ddown[...]
    else:
        joined = sum(
            exact(ddown[pl.ds(b, 64, stride=8), :], column_pick(b), ((1,), (1,))) for b in range(8)
        )
        for q in range(3):
            flat[pl.ds(starts[2] + q, 64, stride=3), :] = joined[:, q * 128 : (q + 1) * 128]
    wide(dup, starts[4])
    for c in range(4):
        flat[starts[5] + c : starts[5] + c + 1, :] = dupb[:, c * 128 : (c + 1) * 128]
    wide(d_out, starts[6])
    if len(grads) == 9:
        wide(grads[7], starts[7])
    wide(grads[-1], starts[-1])
    if info.skew:
        flat[info.rows + 8 : info.rows + 9, 0 : ddownb.shape[1]] = ddownb[...]
        reskew(info, flat)
    else:
        flat[starts[3] : starts[3] + 1, :] = ddownb[...]


class Places:
    def __init__(self, groups, inner):
        self.outer, self.inner = lax.axis_index("dp"), lax.axis_index("fsdp")
        self.chips, self.lines = groups // 2, inner
        self.chip, self.core = self.outer // 2, lax.rem(self.outer, 2)

    def along(self, step):
        return lax.rem(self.inner + step, self.lines)

    def across(self, step):
        return lax.rem(self.chip + step, self.chips)

    def line(self, step):
        return (self.outer, self.along(step))

    def other_chip(self, step):
        return (2 * self.across(step) + self.core, self.inner)

    def sibling(self):
        return (2 * self.chip + 1 - self.core, self.inner)

    def greet(self, barrier):
        for step in range(1, self.lines):
            pl.semaphore_signal(barrier, inc=1, device_id=self.line(step), device_id_type=MESH)
        for step in range(1, self.chips):
            pl.semaphore_signal(barrier, inc=1, device_id=self.other_chip(step), device_id_type=MESH)
        pl.semaphore_signal(barrier, inc=1, device_id=self.sibling(), device_id_type=MESH)

    def greeted(self, barrier):
        pl.semaphore_wait(barrier, self.lines + self.chips - 1)


def remote(source, target, send_sem, recv_sem, device):
    return pltpu.make_async_remote_copy(
        src_ref=source, dst_ref=target, send_sem=send_sem, recv_sem=recv_sem, device_id=device, device_id_type=MESH
    )


def lane_tile(c):
    return slice(128 * c, 128 * c + 128)


def quarters(info, d):
    start = info.share * d
    for c in range(4):
        first = (c - start) % 4
        yield c, first, (start + first) // 4, -(-(info.share - first) // 4)


class SecondGather:
    def __init__(self, info, places, line, pool, start, semaphores):
        self.info, self.places, self.line, self.pool, self.start = info, places, line, pool, start
        self.chip_send, self.chip_recv, self.core_send, self.core_land = semaphores
        self.started = []

    def block(self, core, chip):
        row = self.start + (core * self.places.chips + chip) * self.info.block
        return self.pool.at[aligned(row, self.info.block)]

    def begin(self):
        places = self.places
        mine = self.block(places.core, places.chip)
        mine[...] = self.line[...]
        for step in range(1, places.chips):
            self.started.append(
                remote(
                    self.line, mine, self.chip_send.at[step - 1], self.chip_recv.at[step - 1], places.other_chip(step)
                )
            )
        self.started.append(remote(self.line, mine, self.core_send.at[0], self.core_land, places.sibling()))
        for copy in self.started:
            copy.start()

    def pass_on(self):
        places = self.places
        for step in range(1, places.chips):
            self.started[step - 1].wait_recv()
            landed = self.block(places.core, places.across(places.chips - step))
            copy = remote(landed, landed, self.core_send.at[step], self.core_land, places.sibling())
            copy.start()
            self.started.append(copy)

    def finish(self, flat, shares, tall, weights):
        info, places = self.info, self.places
        half_rows = places.chips * info.block
        half = self.pool.at[pl.ds(self.start, half_rows)]
        pltpu.make_async_copy(half, half, self.core_land).wait()
        for copy in self.started:
            copy.wait_send()
        for d in range(2 * places.chips * places.lines):
            z, outer = d % places.lines, d // places.lines
            row = self.start + (outer % 2 * places.chips + outer // 2) * info.block + z // 4 * info.padded
            share = shares.at[d % 2]
            share[...] = self.pool[row : row + info.padded, lane_tile(z % 4)].astype(F32)
            for c, first, at, rows in quarters(info, d):
                flat[at : at + rows, lane_tile(c)] = share[pl.ds(first, rows, stride=4), :]
        w_in, bd, down, downb, up, upb, w_out, norms = weights
        w_in[...] = flat[0:WIDTH, :].astype(BF16)
        at = WIDTH
        row = lax.broadcasted_iota(jnp.int32, (32, HALF), 0) // 8
        lane = lax.broadcasted_iota(jnp.int32, (32, HALF), 1) // GROUP_WIDTH
        on_diagonal = (row == lane).astype(F32)

        def spread(index, carry):
            for c in range(4):
                rows = flat[pl.ds(pl.multiple_of(at + index * 32, 8), 32), lane_tile(c)]
                turned = pltpu.roll(rows, GROUP_WIDTH, 1)
                left = first_lanes(GROUP_WIDTH, (32, 128))
                for parity, pair in enumerate((jnp.where(left, rows, turned), jnp.where(left, turned, rows))):
                    tiled = jnp.concatenate([pair, pair], axis=1) * on_diagonal
                    tall[pl.ds(2 * c + parity, 32, stride=8), :] = tiled[:, :128]
                    tall[pl.ds(HALF + 2 * c + parity, 32, stride=8), :] = tiled[:, 128:]
            bd[index % 2, index // 2, :, 0:128] = tall[0:HALF, :].astype(BF16)
            bd[index % 2, index // 2, :, 128:HALF] = tall[HALF : 2 * HALF, :].astype(BF16)
            return carry

        lax.fori_loop(0, 2 * TAPS, spread, 0)
        at = at + TAPS * 64
        for c in range(4):
            tall[pl.ds(c, 128, stride=4), :] = flat[at : at + 128, lane_tile(c)]
        down[...] = tall[...].astype(BF16)
        at = at + 128
        downb[...] = flat[at : at + 1, lane_tile(0)]
        for out in (up, upb, w_out, norms):
            rows = out.shape[0]
            for c in range(4):
                begin = at + (c + 1) // 4
                out[:, lane_tile(c)] = flat[begin : begin + rows, lane_tile((c + 1) % 4)].astype(out.dtype)
            at = at + rows


class SecondScatter:
    def __init__(self, info, places, pool, start, landing, semaphores):
        self.info, self.places, self.pool = info, places, pool
        self.core_sem, self.chip_send, self.chip_recv, self.line_send, self.line_recv = semaphores
        block, chips = info.block, places.chips
        self.core_in = landing
        self.chip_in = self.core_in + chips * block
        self.line_in = self.chip_in + (chips - 1) * block
        self.line_sum = self.line_in + block
        self.parts = start

    def rows(self, start, size):
        return self.pool.at[aligned(start, size)]

    def part(self, core, chip):
        return self.parts + (core * self.places.chips + chip) * self.info.block

    def begin(self, shares, acc, grads):
        info, places = self.info, self.places
        d_in, ddown, ddownb, dup, dupb, d_out, dnorms = grads
        group_odd = lax.broadcasted_iota(jnp.int32, (128, 128), 0) // 32 % 2 == 1
        left = first_lanes(GROUP_WIDTH, (128, 128))

        def collect(index, carry):
            tap, h = index // 2, index % 2
            even, odd = acc[tap, h, pl.ds(0, 128, stride=2), :], acc[tap, h, pl.ds(1, 128, stride=2), :]
            even_turned, odd_turned = pltpu.roll(even, GROUP_WIDTH, 1), pltpu.roll(odd, GROUP_WIDTH, 1)
            acc[tap, h, 0:128, :] = jnp.where(
                group_odd, jnp.where(left, even_turned, odd), jnp.where(left, even, odd_turned)
            )
            return carry

        lax.fori_loop(0, 2 * TAPS, collect, 0)
        pieces = [(0, 4 * WIDTH, d_in, 4)]
        at = 4 * WIDTH
        for index in range(2 * TAPS):
            pieces.append((at, 128, acc.at[index // 2, index % 2], 1))
            at = at + 128
        for value, tiles in ((ddown, 1), (ddownb, 1), (dup, 4), (dupb, 4), (d_out, 4), (dnorms, 4)):
            pieces.append((at, value.shape[0] * tiles, value, tiles))
            at = at + value.shape[0] * tiles
        for d in range(2 * places.chips * places.lines):
            z, outer = d % places.lines, d // places.lines
            share = shares.at[d % 2]
            begin, end = info.share * d, info.share * (d + 1)
            if end > at:
                share[...] = jnp.zeros_like(share)
            for start, rows, value, tiles in pieces:
                low, high = max(begin, start), min(end, start + rows)
                for c in range(tiles):
                    first = low + (c - (low - start)) % tiles
                    number = -(-(high - first) // tiles)
                    if number > 0:
                        row = (first - start) // tiles
                        piece = value[row : row + number, lane_tile(c)]
                        if tiles == 1:
                            share[first - begin : first - begin + number, :] = piece
                        else:
                            share[pl.ds(first - begin, number, stride=tiles), :] = piece
            row = self.part(outer % 2, outer // 2) + z // 4 * info.padded
            self.pool[row : row + info.padded, lane_tile(z % 4)] = share[...].astype(BF16)
        size = places.chips * info.block
        self.core_copy = remote(
            self.rows(self.part(1 - places.core, 0), size),
            self.rows(self.core_in, size),
            self.core_sem.at[0],
            self.core_sem.at[1],
            places.sibling(),
        )
        self.core_copy.start()

    def across_chips(self):
        info, places = self.info, self.places
        self.core_copy.wait_recv()

        def add(index, carry):
            mine = aligned(self.part(places.core, 0) + index * info.padded, info.padded)
            theirs = aligned(self.core_in + index * info.padded, info.padded)
            self.pool[mine, :] = (self.pool[mine, :].astype(F32) + self.pool[theirs, :].astype(F32)).astype(BF16)
            return carry

        lax.fori_loop(0, places.chips * info.layers, add, 0)
        self.copies = []
        for step in range(1, places.chips):
            self.copies.append(
                remote(
                    self.rows(self.part(places.core, places.across(step)), info.block),
                    self.rows(self.chip_in + (step - 1) * info.block, info.block),
                    self.chip_send.at[step - 1],
                    self.chip_recv.at[step - 1],
                    places.other_chip(step),
                )
            )
            self.copies[-1].start()

    def along_line(self):
        info, places = self.info, self.places
        for copy in self.copies:
            copy.wait_recv()
        for layer in range(info.layers):
            at = layer * info.padded
            value = self.pool[aligned(self.part(places.core, places.chip) + at, info.padded), :].astype(F32)
            for step in range(places.chips - 1):
                begin = self.chip_in + step * info.block + at
                value = value + self.pool[begin : begin + info.padded, :].astype(F32)
            self.pool[self.line_sum + at : self.line_sum + at + info.padded, :] = value.astype(BF16)
        self.lines = []
        for step in range(1, places.lines):
            z = places.along(step)
            self.lines.append(
                remote(
                    self.pool.at[
                        aligned(self.line_sum + z // 4 * info.padded, info.padded),
                        pl.ds(pl.multiple_of(lax.rem(z, 4) * 128, 128), 128),
                    ],
                    self.pool.at[
                        pl.ds(self.line_in + (step - 1) // 4 * info.padded, info.padded),
                        lane_tile((step - 1) % 4),
                    ],
                    self.line_send.at[step - 1],
                    self.line_recv.at[step - 1],
                    places.line(step),
                )
            )
            self.lines[-1].start()

    def finish(self, out):
        info, places = self.info, self.places
        z = places.inner
        value = self.pool[
            aligned(self.line_sum + z // 4 * info.padded, info.padded),
            pl.ds(pl.multiple_of(lax.rem(z, 4) * 128, 128), 128),
        ].astype(F32)
        for step in range(1, places.lines):
            self.lines[step - 1].wait_recv()
            begin = self.line_in + (step - 1) // 4 * info.padded
            value = value + self.pool[begin : begin + info.padded, lane_tile((step - 1) % 4)].astype(F32)
        out[...] = value[0 : info.share]
        for copy in [self.core_copy] + self.copies + self.lines:
            copy.wait_send()


def gather_body(geo, infos, groups, inner, *refs):
    images_hbm, cots_hbm, counts = refs[0:3], refs[3:6], refs[6]
    shards = refs[7:9]
    acts_hbm, cot_hbm, mask, live = refs[9:13]
    weights, line_out = refs[13:22], refs[22]
    (
        wide_cell, cot_cell, block_pad, gathered, line_in, flat, stage2,
        line_send, line_recv, chip_send, chip_recv, core_send, core_recv,
        *images_and_cots, acts, cot, load_sem, store_sem,
    ) = refs[23:]
    images, cots = images_and_cots[:3], images_and_cots[3:]
    loads = [
        pltpu.make_async_copy(source, target, load_sem.at[k])
        for k, (source, target) in enumerate(zip([*images_hbm, *cots_hbm], images_and_cots))
    ]
    for load in loads:
        load.start()
    stores = []
    places = Places(groups, inner)
    barrier = pltpu.get_barrier_semaphore()
    places.greet(barrier)
    z = places.inner
    mine = [
        gathered.at[places.chip, places.core, z],
        line_in.at[
            aligned(z // 4 * infos[1].padded, infos[1].padded), pl.ds(pl.multiple_of(lax.rem(z, 4) * 128, 128), 128)
        ],
    ]
    slot = lax.broadcasted_iota(jnp.int32, (16, WIDTH), 0) % 4
    for b in range(3):
        mask[b] = jnp.where(slot < counts[0, b], 1.0, 0.0)
    for k, info in enumerate(infos):
        stage = flat.at[pl.ds(0, info.padded)] if k == 0 else stage2
        stage[info.padded - 16 : info.padded, :] = jnp.zeros((16, 128), F32)
        stage[0 : info.share, :] = shards[k][...]
        for b in range(3):
            value = jnp.broadcast_to(counts[0, b].astype(F32), (1, 128))
            stage[info.share + b : info.share + b + 1, :] = value
        mine[k][...] = stage[...].astype(BF16)
    places.greeted(barrier)
    started = []

    def begin(copy):
        copy.start()
        started.append(copy)
        return copy

    lines = [
        [
            begin(remote(mine[k], mine[k], line_send.at[k, step - 1], line_recv.at[k, step - 1], places.line(step)))
            for step in range(1, inner)
        ]
        for k in range(2)
    ]
    chip_copies = []

    def forward(step):
        if step:
            lines[0][step - 1].wait_recv()
        share = gathered.at[places.chip, places.core, places.along(inner - step)]
        for over in range(1, places.chips):
            at = (over - 1) * inner + step
            chip_copies.append(
                begin(remote(share, share, chip_send.at[at], chip_recv.at[at], places.other_chip(over)))
            )
        begin(remote(share, share, core_send.at[step], core_recv, places.sibling()))

    def pass_on(step):
        for over in range(1, places.chips):
            chip_copies[step * (places.chips - 1) + over - 1].wait_recv()
            share = gathered.at[places.across(places.chips - over), places.core, places.along(inner - step)]
            begin(remote(share, share, core_send.at[over * inner + step], core_recv, places.sibling()))

    def complete():
        half = gathered.at[:, 0]
        pltpu.make_async_copy(half, half, core_recv).wait()
        info = infos[0]
        found = jnp.zeros((3, 128), F32)
        for d in range(groups * inner):
            at = info.share * d
            piece = gathered[d // inner // 2, d // inner % 2, d % inner].astype(F32)
            flat[at : at + info.share, :] = piece[0 : info.share]
            found = found + piece[info.share : info.share + 3]
        total = sum(found[b : b + 1, :] * (4.0 * side * side) for b, side in enumerate(geo.sides))
        live[...] = jnp.concatenate([total] * 4, axis=1)
        unpack(info, flat, block_pad, weights)
        for copy in lines[1]:
            copy.wait_recv()
        line_out[...] = line_in[...]

    def arrange(b):
        side = geo.sides[b]
        size = side * 16

        def line(i, carry):
            rows = aligned(geo.bases[b] + i * size, size)
            for pr in range(2):
                for pc in range(2):
                    for q in range(4):
                        wide_cell[0:side, 4 * q : 4 * q + 4, :] = images[b][q // 2, i, pr, q % 2, :, pc].astype(F32)
                    value = wide_cell[0:side] * mask[b][None, :, :WIDTH_IN]
                    acts[2 * pr + pc, rows, :] = value.reshape(size, WIDTH_IN).astype(BF16)
            for q in range(4):
                cot_cell[0:side, 4 * q : 4 * q + 4, :] = cots[b][q // 2, i, q % 2].astype(F32)
            value = cot_cell[0:side] * mask[b][None]
            cot[rows, :] = value.reshape(size, WIDTH).astype(BF16)
            return carry

        loads[b].wait()
        loads[3 + b].wait()
        lax.fori_loop(0, side, line, 0)
        some = pl.ds(geo.bases[b], geo.rows[b])
        stores.append(pltpu.make_async_copy(acts.at[:, some], acts_hbm.at[:, some], store_sem.at[2 * b]))
        stores.append(pltpu.make_async_copy(cot.at[some], cot_hbm.at[some], store_sem.at[2 * b + 1]))
        for store in stores[-2:]:
            store.start()

    forward(0)
    arrange(0)
    for step in range(1, inner):
        forward(step)
    arrange(1)
    pass_on(0)
    arrange(2)
    for step in range(1, inner):
        pass_on(step)
    complete()
    for store in stores:
        store.wait()
    for copy in started:
        copy.wait_send()


def gather(geo, infos, images, cots, counts, shards):
    groups, inner = lax.axis_size("dp"), lax.axis_size("fsdp")
    ins = [*images, *cots, counts, *[shard.reshape(-1, 128) for shard in shards]]
    outs = [shape((4, geo.total, WIDTH_IN), BF16), shape((geo.total, WIDTH), BF16)]
    outs += [shape((3, 16, WIDTH)), shape((1, WIDTH))]
    for is_first in (True,):
        dims = shapes_of(is_first)
        outs += [shape(dims[0], BF16), shape((2, TAPS, HALF, HALF), BF16)]
        outs += [shape(d, F32 if d[0] == 1 else BF16) for d in dims[2:-1]] + [shape(dims[-1])]
    outs += [shape((infos[1].block, WIDTH), BF16)]
    side = max(geo.sides)
    scratch = [
        pltpu.VMEM((side, 16, WIDTH_IN), F32), pltpu.VMEM((side, 16, WIDTH), F32), pltpu.VMEM((2 * HALF, 128), F32),
    ]
    scratch += [
        pltpu.VMEM((groups // 2, 2, inner, infos[0].padded, 128), BF16), pltpu.VMEM((infos[1].block, WIDTH), BF16),
        pltpu.VMEM((infos[0].rows + 16, 128), F32), pltpu.VMEM((infos[1].padded, 128), F32),
    ]
    chips = groups // 2
    scratch += [
        pltpu.SemaphoreType.DMA(dims)
        for dims in (
            (2, inner - 1), (2, inner - 1), ((chips - 1) * inner,), ((chips - 1) * inner,), (chips * inner,), ()
        )
    ]
    scratch += [pltpu.VMEM(value.shape, BF16) for value in ins[:6]]
    scratch += [pltpu.VMEM(value.shape, BF16) for value in outs[:2]]
    scratch += [pltpu.SemaphoreType.DMA((6,)), pltpu.SemaphoreType.DMA((6,))]
    results = pl.pallas_call(
        functools.partial(gather_body, geo, infos, groups, inner),
        out_shape=outs,
        in_specs=[anywhere()] * 6 + [pl.BlockSpec(memory_space=pltpu.SMEM)] + [whole()] * 2,
        out_specs=[anywhere()] * 2 + [whole()] * (len(outs) - 2),
        scratch_shapes=scratch,
        compiler_params=pltpu.CompilerParams(
            collective_id=1, has_side_effects=True, vmem_limit_bytes=LIMIT
        ),
    )(*ins)
    return results[:4], results[4:13], results[13]


def scatter_body(info, groups, inner, *refs):
    grads, out = refs[0:9], refs[9]
    flat, parts, core_in, chip_sum, chip_in, line_sum, line_in = refs[10:17]
    core_send, core_recv, chip_send, chip_recv, line_send, line_recv = refs[17:]
    places = Places(groups, inner)
    barrier = pltpu.get_barrier_semaphore()
    places.greet(barrier)
    devices = groups * inner
    pack(info, flat, grads)
    for d in range(devices):
        place = parts.at[d // inner % 2, d // inner // 2, d % inner]
        place[0 : info.padded, :] = flat[info.share * d : info.share * d + info.padded, :].astype(BF16)
    places.greeted(barrier)
    order = [*range(1, inner), 0]
    copies = []

    def send(*args):
        copies.append(remote(*args))
        copies[-1].start()
        return copies[-1]

    core, chip, lines = {}, {}, []
    for step in order:
        z = places.along(step)
        core[step] = send(
            parts.at[1 - places.core, :, z], core_in.at[:, z], core_send.at[step], core_recv.at[step], places.sibling()
        )
    for step in order:
        z = places.along(step)
        core[step].wait_recv()
        for at in range(places.chips):
            value = parts[places.core, at, z].astype(F32) + core_in[at, z].astype(F32)
            chip_sum[at, z] = value.astype(BF16)
        chip[step] = []
        for over in range(1, places.chips):
            at = (over - 1) * inner + step
            chip[step].append(
                send(
                    chip_sum.at[places.across(over), z], chip_in.at[over - 1, z], chip_send.at[at], chip_recv.at[at],
                    places.other_chip(over),
                )
            )
    for step in order:
        z = places.along(step)
        value = chip_sum[places.chip, z].astype(F32)
        for over in range(1, places.chips):
            chip[step][over - 1].wait_recv()
            value = value + chip_in[over - 1, z].astype(F32)
        line_sum[z] = value.astype(BF16)
        if step:
            lines.append(
                send(
                    line_sum.at[z], line_in.at[step - 1], line_send.at[step - 1], line_recv.at[step - 1],
                    places.line(step),
                )
            )
    for copy in lines:
        copy.wait_recv()
    value = line_sum[places.inner].astype(F32)
    for step in range(inner - 1):
        value = value + line_in[step].astype(F32)
    out[...] = value[0 : info.share, :]
    for copy in copies:
        copy.wait_send()


def scatter(info, ins):
    groups, inner = lax.axis_size("dp"), lax.axis_size("fsdp")
    chips = groups // 2
    size = info.padded
    def part(*lead):
        return pltpu.VMEM((*lead, size, 128), BF16)
    out = pl.pallas_call(
        functools.partial(scatter_body, info, groups, inner),
        out_shape=shape((info.share, 128)),
        in_specs=[whole()] * len(ins),
        out_specs=whole(),
        scratch_shapes=[
            pltpu.VMEM((info.rows + 16, 128), F32),
            part(2, chips, inner), part(chips, inner), part(chips, inner), part(chips - 1, inner), part(inner),
            part(inner - 1),
        ]
        + [pltpu.SemaphoreType.DMA(dims) for dims in ((inner,), (inner,), *[((chips - 1) * inner,)] * 2, (inner - 1,), (inner - 1,))],
        compiler_params=pltpu.CompilerParams(
            collective_id=2, has_side_effects=True, vmem_limit_bytes=LIMIT
        ),
    )(*ins)
    return out.reshape(-1)


def restore_body(geo, *refs):
    number = len(geo.sides)
    g1, gs, out = (refs[k * number : (k + 1) * number] for k in range(3))
    w_in, w_short = refs[3 * number : 3 * number + 2]
    rest = refs[3 * number + 2 :]
    output_hbm, grad_hbm = rest[:number], rest[number : 2 * number]
    g1_in, gs_in, out_in, outputs, image_grads = (rest[(k + 2) * number : (k + 3) * number] for k in range(5))
    grad_cell, out_cell, in_sems, out_sems = rest[7 * number :]
    order = range(number)
    loads, stores = {}, []
    for b in order:
        loads[b] = [
            pltpu.make_async_copy(source, target, in_sems.at[b, k])
            for k, (source, target) in enumerate(((g1[b], g1_in[b]), (gs[b], gs_in[b]), (out[b], out_in[b])))
        ]
        for load in loads[b]:
            load.start()
    for b in order:
        side = geo.sides[b]
        size = side * 16
        for load in loads[b]:
            load.wait()

        def line(i, carry, b=b, side=side, size=size):
            rows = aligned(i * size, size)
            out_cell[0:side] = out_in[b][rows, :].astype(F32).reshape(side, 16, WIDTH)
            for q in range(4):
                outputs[b][q // 2, i, q % 2] = out_cell[0:side, 4 * q : 4 * q + 4, :].astype(BF16)
            value = dot_nt(g1_in[b][:, rows, :].reshape(4 * size, WIDTH), w_in[...])
            grad_cell[:, 0:side] = value.reshape(4, side, 16, WIDTH_IN)
            grad_cell[0, 0:side] += dot_nt(gs_in[b][rows, :], w_short[...]).reshape(side, 16, WIDTH_IN)
            for plane in range(4):
                for q in range(4):
                    image_grads[b][q // 2, i, plane // 2, q % 2, :, plane % 2] = grad_cell[
                        plane, 0:side, 4 * q : 4 * q + 4, :
                    ]
            return carry

        cuts = [0, side // 3, 2 * side // 3, side]
        for k in range(3):
            lax.fori_loop(cuts[k], cuts[k + 1], line, 0)
            some = pl.ds(cuts[k], cuts[k + 1] - cuts[k])
            for j, (source, target) in enumerate(((outputs[b], output_hbm[b]), (image_grads[b], grad_hbm[b]))):
                stores.append(pltpu.make_async_copy(source.at[:, some], target.at[:, some], out_sems.at[b, 2 * k + j]))
                stores[-1].start()
    for store in stores:
        store.wait()


def restore(geo, g1, gs, out, w_in, w_short):
    ins = [*g1, *gs, *out, w_in, w_short]
    sides = geo.sides
    out_dims = [(2, side, 2, side, 4, WIDTH) for side in sides]
    grad_dims = [(2, side, 2, 2, side, 2, 4, WIDTH_IN) for side in sides]
    most = max(sides)
    results = pl.pallas_call(
        functools.partial(restore_body, geo),
        out_shape=[shape(dims, BF16) for dims in out_dims] + [shape(dims) for dims in grad_dims],
        in_specs=[anywhere()] * 9 + [whole()] * 2,
        out_specs=[anywhere()] * 6,
        scratch_shapes=[pltpu.VMEM(value.shape, BF16) for value in ins[:9]]
        + [pltpu.VMEM(dims, BF16) for dims in out_dims]
        + [pltpu.VMEM(dims, F32) for dims in grad_dims]
        + [pltpu.VMEM((4, most, 16, WIDTH_IN), F32), pltpu.VMEM((most, 16, WIDTH), F32)]
        + [pltpu.SemaphoreType.DMA((3, 3)), pltpu.SemaphoreType.DMA((3, 6))],
        compiler_params=pltpu.CompilerParams(vmem_limit_bytes=LIMIT),
    )(*ins)
    grids = [
        result.reshape(scale * side, scale * side, 4, -1).transpose(2, 0, 1, 3)
        for result, side, scale in zip(results, sides * 2, [2] * 3 + [4] * 3)
    ]
    return grids


def per_device(*args):
    images, counts = args[0:3], args[3]
    cots = args[6:9]
    geo = Geometry([image.shape[1] // 4 for image in images])
    inner = lax.axis_size("fsdp")
    devices = lax.axis_size("dp") * inner
    infos = [Flat(k == 0, args[4 + k].shape[0] * devices, devices, inner) for k in range(2)]
    split_images = [
        image.transpose(1, 2, 0, 3).reshape(2, side, 2, 2, side, 2, 4, WIDTH_IN)
        for image, side in zip(images, geo.sides)
    ]
    split_cots = [
        value.transpose(1, 2, 0, 3).reshape(2, side, 2, side, 4, WIDTH) for value, side in zip(cots, geo.sides)
    ]
    (acts, cot, mask, live), first, line2 = gather(geo, infos, split_images, split_cots, counts, args[4:6])
    out, g1, gs, first_grads, second_out = blocks(geo, infos, acts, mask, live, first, line2, cot)
    return (
        *restore(geo, g1, gs, out, first[0], first[7]),
        scatter(infos[0], first_grads),
        second_out,
    )


def solution(mesh):
    images = P(("dp", "fsdp"), None, None, None)
    flat = P(("dp", "fsdp"))
    in_specs = (images, images, images, P(("dp", "fsdp"), None), flat, flat, images, images, images)
    out_specs = (images,) * 6 + (flat, flat)
    return jax.shard_map(per_device, mesh=mesh, in_specs=in_specs, out_specs=out_specs, check_vma=False)
```
